32 devices in a mesh: fsdp: 32 (over z, y, x, core).
Axes of the slice: x: 2, y: 2, z: 4, core: 2. Of those that a mesh axis runs over, the one named last changes fastest.
Arguments:
- token_ids: int32 [65536], P('fsdp'), may hold values from 0 to 14591
- masked: int32 [65536], P('fsdp'), may hold values 0 or 1
- swap_kind: int32 [65536], P('fsdp'), may hold values from 0 to 9
- swap_ids: int32 [65536], P('fsdp'), may hold values from 0 to 14591
- out_grad: bfloat16 [65536, 768], P('fsdp'), may hold values from -6 to 6
- embed_table: float32 [15104, 768], P('fsdp'), may hold values from -6 to 6
- table_first: float32 [15104, 768], P('fsdp'), may hold values from -16 to 16
- table_second: float32 [15104, 768], P('fsdp'), may hold values from 10 to 10000
- layer_mats: float32 [768, 9216], P(None, 'fsdp'), may hold values from -4 to 4
- mats_first: float32 [768, 9216], P(None, 'fsdp'), may hold values from -16 to 16
- mats_second: float32 [768, 9216], P(None, 'fsdp'), may hold values from 10 to 10000
- layer_vecs: float32 [9216], P('fsdp'), may hold values from -1.2 to 1.9
- vecs_first: float32 [9216], P('fsdp'), may hold values from -16 to 16
- vecs_second: float32 [9216], P('fsdp'), may hold values from 10 to 10000
Outputs:
- layer_out: bfloat16 [65536, 768], P('fsdp')
- input_grad: bfloat16 [65536, 768], P('fsdp')
- table_grad: float32 [15104, 768], P('fsdp')
- mats_grad: float32 [768, 9216], P(None, 'fsdp')
- vecs_grad: float32 [9216], P('fsdp')
- table_step: float32 [15104, 768], P('fsdp')
- table_first_next: float32 [15104, 768], P('fsdp')
- mats_step: float32 [768, 9216], P(None, 'fsdp')
- mats_first_next: float32 [768, 9216], P(None, 'fsdp')
- vecs_step: float32 [9216], P('fsdp')
- vecs_first_next: float32 [9216], P('fsdp')
The draws below stay inside these ranges and needn't reach their ends.
Inputs may be any that keep to these rules, and one draw needn't show every extreme that they name: `swap_kind`: kinds 0 to 7 mean the mask token 103, kind 8 the id of swap_ids, kind 9 keeps the token's own id.
All inputs are finite; a program needn't handle non-finite values. No bound on the sum of `masked` on one device may be relied on, other than what follows from the above.
Results may differ from the reference program's by a relative error of at most 0.015.
The reference program's roundings to bfloat16 on the way count: a program that leaves them out, or rounds other values in their place, can miss the bound.
Values may be sent and summed in bfloat16 or wider, within the bound.
A program may use at most 320 MiB of HBM per device.

```python
import math
import jax
import jax.numpy as jnp
import numpy as np
from jax import lax

D = 768
HEADS = 12
HEAD_DIM = 64
FF = 3072
VOCAB = 14592
LENGTH = 512
STEP = 10
TOKENS = 65536
TABLE = 15104
W_MATS = 9216
W_VECS = 9216


def base_values(key, shape):
    values = jax.random.normal(key, shape, jnp.float32)
    return jnp.clip(values, -6.0, 6.0)


def draw_layer_mats(key, part):
    key = jax.random.fold_in(key, 11)
    columns = jnp.arange(W_MATS)
    scales = jnp.where(columns < 3 * D, D ** (-0.5), jnp.where(columns < 4 * D, (0.25 * LENGTH / D) ** 0.5, jnp.where(columns < 4 * D + FF, D ** (-0.5), FF ** (-0.5))))
    return base_values(key, (D, W_MATS)) * scales[None, :].astype(jnp.float32)


def draw_layer_vecs(key, part):
    key = jax.random.fold_in(key, 17)
    places = jnp.arange(W_VECS)
    gains = (places >= 3 * D) & (places < 4 * D) | (places >= 6 * D + FF) & (places < 7 * D + FF)
    values = base_values(key, (W_VECS,))
    return jnp.where(gains, 1.0 + 0.15 * values, 0.2 * values)


def plant(result, key, smallest, largest):
    longest = result.shape.index(max(result.shape))
    spots = []
    for shift in (0, 1):
        where = [jax.random.randint(jax.random.fold_in(key, axis), (), 0, length) for axis, length in enumerate(result.shape)]
        where[longest] = (where[longest] + shift) % result.shape[longest]
        spots.append(tuple(where))
    return result.at[spots[0]].set(smallest).at[spots[1]].set(largest)


def steps_of(rng, dims, cuts, low, high):
    level, own = 1.0, jax.random.fold_in(rng, 6)
    for dim, shards_of in cuts:
        draws = jnp.exp(jax.random.uniform(jax.random.fold_in(own, dim), (shards_of,), jnp.float32, low / len(cuts), high / len(cuts)))
        level = level * jnp.repeat(draws, dims[dim] // shards_of).reshape([-1 if axis == dim else 1 for axis in range(len(dims))])
    return level


def rank_bounds(amount, slope):
    weights = [(1 << 20) // math.isqrt(grade ** slope) + 1 for grade in range(1, amount + 1)]
    spread = 1 + sum(weights) // (1 << 30)
    return np.cumsum(np.array([max(1, weight // spread) for weight in weights]))


def skewed_ids(key, dims, count, slope):
    grid = rank_bounds(count, slope)
    ticket = jax.random.randint(jax.random.fold_in(key, 1), dims, 0, int(grid[count - 1]))
    standing = jnp.searchsorted(jnp.asarray(grid, jnp.int32), ticket, side="right")
    return jax.random.permutation(jax.random.fold_in(key, 2), count)[standing].astype(jnp.int32)


def gaussian(key, shape, spread, most, split=(), held_as=jnp.bfloat16):
    entries = spread * jax.random.normal(key, shape, jnp.float32)
    if split:
        entries = entries * steps_of(key, shape, split, -0.22, 0.18)
    return jnp.clip(entries, -most, most).astype(held_as)


def setup_inputs(seed: int = 0) -> dict:
    key_of = jax.random.split(jax.random.key(seed), 15)
    token_ids = plant(skewed_ids(key_of[0], (TOKENS,), VOCAB, 2), jax.random.fold_in(key_of[0], 3), 0, VOCAB - 1).astype(jnp.int32)
    masked = plant((jax.random.randint(key_of[1], (TOKENS,), 0, 100) < 15).astype(jnp.int32), jax.random.fold_in(key_of[1], 1), 0, 1)
    swap_kind = plant(jax.random.randint(key_of[2], (TOKENS,), 0, 10), jax.random.fold_in(key_of[2], 1), 0, 9).astype(jnp.int32)
    swap_ids = plant(jax.random.randint(key_of[3], (TOKENS,), 0, VOCAB), jax.random.fold_in(key_of[3], 1), 0, VOCAB - 1).astype(jnp.int32)
    out_grad = gaussian(key_of[4], (TOKENS, D), 1.0, 6.0, ((0, 32),))
    embed_table = gaussian(key_of[5], (TABLE, D), 0.7, 6.0, ((0, 32),), jnp.float32)
    table_first = gaussian(key_of[6], (TABLE, D), 3.0, 16.0, ((0, 32),), jnp.float32)
    table_second = jnp.clip(jnp.exp(math.log(10000.0) - 6.9077553 * jax.random.uniform(key_of[7], (TABLE, D), jnp.float32) ** steps_of(key_of[7], (TABLE, D), ((0, 32),), -0.2, 0.2)), 10.0, 10000.0)
    layer_mats = draw_layer_mats(jax.random.fold_in(key_of[14], 71), 0)
    mats_first = gaussian(key_of[9], (D, W_MATS), 3.0, 16.0, ((1, 32),), jnp.float32)
    mats_second = jnp.clip(jnp.exp(math.log(10000.0) - 6.9077553 * jax.random.uniform(key_of[10], (D, W_MATS), jnp.float32) ** steps_of(key_of[10], (D, W_MATS), ((1, 32),), -0.2, 0.2)), 10.0, 10000.0)
    layer_vecs = draw_layer_vecs(jax.random.fold_in(key_of[14], 71), 0)
    vecs_first = gaussian(key_of[12], (W_VECS,), 3.0, 16.0, ((0, 32),), jnp.float32)
    vecs_second = jnp.clip(jnp.exp(math.log(10000.0) - 6.9077553 * jax.random.uniform(key_of[13], (W_VECS,), jnp.float32) ** steps_of(key_of[13], (W_VECS,), ((0, 32),), -0.2, 0.2)), 10.0, 10000.0)
    return dict(token_ids=token_ids, masked=masked, swap_kind=swap_kind, swap_ids=swap_ids, out_grad=out_grad, embed_table=embed_table, table_first=table_first, table_second=table_second, layer_mats=layer_mats, mats_first=mats_first, mats_second=mats_second, layer_vecs=layer_vecs, vecs_first=vecs_first, vecs_second=vecs_second)


@jax.custom_vjp
def low(v):
    return lax.optimization_barrier(v.astype(jnp.bfloat16)).astype(jnp.float32)

@jax.custom_vjp
def low_back(v):
    return v

def low_keep(v):
    return (low(v), None)

def low_pass(kept, grad):
    return (grad,)

def back_keep(v):
    return (v, None)

def back_low(kept, grad):
    return (low(grad),)
low.defvjp(low_keep, low_pass)
low_back.defvjp(back_keep, back_low)
norm_eps = 1e-12
mask_token = 103
beta_one = 0.9
beta_two = 0.999
adam_eps = 1e-06
decay_rate = 0.01

def matmul(left, right):
    return jnp.dot(left, right, precision=lax.Precision.HIGHEST)

def layer_norm(total, gain, shift):
    centre = lax.optimization_barrier(jnp.mean(total, -1, keepdims=True))
    centered = total - centre
    variance = lax.optimization_barrier(jnp.mean(centered * centered, -1, keepdims=True))
    return centered * lax.rsqrt(variance + norm_eps) * gain + shift

def layer_forward(inputs, mats, vecs):
    weights = low(mats)
    biases = low(vecs)
    w_qkv = weights[:, :3 * D]
    w_out = weights[:, 3 * D:4 * D]
    w_up = weights[:, 4 * D:4 * D + FF]
    w_down = weights[:, 4 * D + FF:]
    bias_query = biases[0:D]
    bias_value = biases[D:2 * D]
    bias_out = biases[2 * D:3 * D]
    gain_one = biases[3 * D:4 * D]
    shift_one = biases[4 * D:5 * D]
    bias_up = biases[5 * D:5 * D + FF]
    bias_down = biases[5 * D + FF:6 * D + FF]
    gain_two = biases[6 * D + FF:7 * D + FF]
    shift_two = biases[7 * D + FF:8 * D + FF]
    rows = inputs.shape[0]
    seqs = rows // LENGTH
    projected = low_back(matmul(low(inputs), w_qkv))
    projected = projected + jnp.concatenate([bias_query, jnp.zeros((D,), jnp.float32), bias_value])
    projected = low(projected)
    heads = projected.reshape(seqs, LENGTH, 3, HEADS, HEAD_DIM)
    query = heads[:, :, 0]
    keys = heads[:, :, 1]
    values = heads[:, :, 2]
    scores = low_back(jnp.einsum('bqhd,bkhd->bhqk', query, keys, precision=lax.Precision.HIGHEST) * HEAD_DIM ** (-0.5))
    probs = low(jax.nn.softmax(scores, axis=-1))
    attended = low_back(jnp.einsum('bhqk,bkhd->bqhd', probs, values, precision=lax.Precision.HIGHEST))
    attended = attended.reshape(rows, D)
    branch = low_back(matmul(low(attended), w_out)) + bias_out
    normed = layer_norm(inputs + branch, gain_one, shift_one)
    upward = low_back(matmul(low(normed), w_up)) + bias_up
    hidden = low(jax.nn.gelu(upward, approximate=False))
    downward = low_back(matmul(hidden, w_down.T)) + bias_down
    return layer_norm(normed + downward, gain_two, shift_two)

def adam_direction(param, first, second, grad, corr_one, corr_two, decay):
    first_next = beta_one * first + (1.0 - beta_one) * grad
    second_next = beta_two * second + (1.0 - beta_two) * grad * grad
    update = first_next / corr_one / (jnp.sqrt(second_next / corr_two) + adam_eps)
    return (update + decay * param, first_next)

def reference(token_ids, masked, swap_kind, swap_ids, out_grad, embed_table, table_first, table_second, layer_mats, mats_first, mats_second, layer_vecs, vecs_first, vecs_second):
    replaced = jnp.where(swap_kind < 8, mask_token, jnp.where(swap_kind == 8, swap_ids, token_ids))
    chosen = jnp.where(masked == 1, replaced, token_ids).astype(jnp.int32)
    places = (VOCAB + jnp.arange(TOKENS, dtype=jnp.int32) % LENGTH).astype(jnp.int32)

    def embed(table):
        rounded = low(table)
        return rounded[chosen] + rounded[places]
    inputs, embed_back = jax.vjp(embed, embed_table)
    cotangent = out_grad.astype(jnp.float32) * masked.astype(jnp.float32)[:, None]
    group = math.gcd(TOKENS // LENGTH, max(1, 4096 // LENGTH)) * LENGTH
    count = TOKENS // group

    def one_group(carry, pieces):
        rows, grads = pieces
        outputs, back = jax.vjp(layer_forward, rows, layer_mats, layer_vecs)
        grad_rows, grad_mats, grad_vecs = back(grads)
        return ((carry[0] + grad_mats, carry[1] + grad_vecs), (outputs, grad_rows))
    start = (jnp.zeros((D, W_MATS), jnp.float32), jnp.zeros((W_VECS,), jnp.float32))
    (mats_grad, vecs_grad), (outputs, grad_inputs) = lax.scan(one_group, start, (inputs.reshape(count, group, D), cotangent.reshape(count, group, D)))
    grad_inputs = grad_inputs.reshape(TOKENS, D)
    table_grad, = embed_back(grad_inputs)
    counter = jnp.float32(STEP)
    corr_one = 1.0 - jnp.power(jnp.float32(beta_one), counter)
    corr_two = 1.0 - jnp.power(jnp.float32(beta_two), counter)
    table_step, table_first_next = adam_direction(embed_table, table_first, table_second, table_grad, corr_one, corr_two, decay_rate)
    mats_step, mats_first_next = adam_direction(layer_mats, mats_first, mats_second, mats_grad, corr_one, corr_two, decay_rate)
    vecs_step, vecs_first_next = adam_direction(layer_vecs, vecs_first, vecs_second, vecs_grad, corr_one, corr_two, 0.0)
    return (outputs.reshape(TOKENS, D).astype(jnp.bfloat16), grad_inputs.astype(jnp.bfloat16), table_grad, mats_grad, vecs_grad, table_step, table_first_next, mats_step, mats_first_next, vecs_step, vecs_first_next)
```

```python
import functools

import jax
import jax.numpy as jnp
from jax import lax
from jax.experimental import pallas as pl
from jax.experimental.pallas import tpu as pltpu
from jax.sharding import PartitionSpec as P

D = 768
HEADS = 12
HEAD_DIM = 64
FF = 3072
VOCAB = 14592
LENGTH = 512
STEP = 10
QKV = 3 * D

norm_eps = 1e-12
mask_token = 103
beta_one = 0.9
beta_two = 0.999
adam_eps = 1e-06
decay_rate = 0.01

BF = jnp.bfloat16
F32 = jnp.float32
LOG2E = 1.4426950408889634
SCORE = HEAD_DIM ** (-0.5)
MB = 1024 * 1024

ROW_TILE = 256
FF_TILE = 768


def dot_nn(left, right):
    return lax.dot_general(
        left, right, (((1,), (0,)), ((), ())), preferred_element_type=F32
    )


def dot_nt(left, right):
    return lax.dot_general(
        left, right, (((1,), (1,)), ((), ())), preferred_element_type=F32
    )


def dot_tn(left, right):
    return lax.dot_general(
        left, right, (((0,), (0,)), ((), ())), preferred_element_type=F32
    )


def attention_forward_kernel(q_ref, k_ref, v_ref, att_ref, lse_ref):
    query = q_ref[...]
    keys = k_ref[...]
    values_t = v_ref[...].T
    lane = lax.broadcasted_iota(jnp.int32, query.shape, 1)
    outs = []
    for half in range(2):
        mine = (lane < HEAD_DIM) if half == 0 else (lane >= HEAD_DIM)
        picked = jnp.where(mine, query, jnp.zeros_like(query))
        scores = dot_nt(keys, picked)
        highest = jnp.max(scores, 0, keepdims=True)
        expo = jnp.exp2((scores - highest) * (SCORE * LOG2E))
        total = jnp.sum(expo, 0, keepdims=True)
        part = values_t[half * HEAD_DIM : (half + 1) * HEAD_DIM, :]
        outs.append(dot_nn(part, expo.astype(BF)) / total)
        lse_ref[0, half : half + 1, :] = highest * (SCORE * LOG2E) + jnp.log2(total)
    att_ref[...] = jnp.concatenate(outs, 0).T.astype(BF)


def attention_forward(projected):
    rows = projected.shape[0]
    seqs = rows // LENGTH
    pairs = HEADS // 2
    block = (LENGTH, 2 * HEAD_DIM)
    return pl.pallas_call(
        attention_forward_kernel,
        grid=(seqs, pairs),
        in_specs=[
            pl.BlockSpec(block, lambda s, h: (s, h)),
            pl.BlockSpec(block, lambda s, h: (s, pairs + h)),
            pl.BlockSpec(block, lambda s, h: (s, 2 * pairs + h)),
        ],
        out_specs=[
            pl.BlockSpec(block, lambda s, h: (s, h)),
            pl.BlockSpec((1, 2, LENGTH), lambda s, h: (s * pairs + h, 0, 0)),
        ],
        out_shape=[
            jax.ShapeDtypeStruct((rows, D), BF),
            jax.ShapeDtypeStruct((seqs * pairs, 2, LENGTH), F32),
        ],
        compiler_params=pltpu.CompilerParams(vmem_limit_bytes=48 * MB),
        name="attention_forward",
    )(projected, projected, projected)


def attention_backward_kernel(
    q_ref, k_ref, v_ref, att_ref, g_ref, lse_ref, out_ref, bias_ref
):
    query = q_ref[...]
    keys = k_ref[...]
    values = v_ref[...]
    grad = g_ref[...]
    lane = lax.broadcasted_iota(jnp.int32, query.shape, 1)
    first = lane < HEAD_DIM
    product = (att_ref[...].astype(F32) * grad.astype(F32)).T
    zero = jnp.zeros_like(query)
    g_q, g_k, g_v = [], [], []
    for half in range(2):
        mine = first if half == 0 else jnp.logical_not(first)
        scores = dot_nt(keys, jnp.where(mine, query, zero))
        probs = jnp.exp2(scores * (SCORE * LOG2E) - lse_ref[0, half : half + 1, :])
        delta = jnp.sum(
            product[half * HEAD_DIM : (half + 1) * HEAD_DIM, :], 0, keepdims=True
        )
        g_probs = dot_nt(values, jnp.where(mine, grad, zero))
        g_v.append(dot_nn(probs.astype(BF), grad))
        g_scores = (probs * (g_probs - delta)).astype(BF)
        g_k.append(dot_nn(g_scores, query))
        g_q.append(dot_tn(g_scores, keys))
    grad_q = jnp.where(first, g_q[0], g_q[1]) * SCORE
    grad_k = jnp.where(first, g_k[0], g_k[1]) * SCORE
    grad_v = jnp.where(first, g_v[0], g_v[1])
    out_ref[0] = grad_q.astype(BF)
    out_ref[1] = grad_k.astype(BF)
    out_ref[2] = grad_v.astype(BF)

    @pl.when(pl.program_id(1) == 0)
    def _():
        bias_ref[...] = jnp.zeros_like(bias_ref)

    bias_ref[0:1, :] += jnp.sum(grad_q, 0, keepdims=True)
    bias_ref[1:2, :] += jnp.sum(grad_v, 0, keepdims=True)


def attention_backward(projected, attended, grad_att, lse):
    rows = projected.shape[0]
    seqs = rows // LENGTH
    pairs = HEADS // 2
    block = (LENGTH, 2 * HEAD_DIM)
    return pl.pallas_call(
        attention_backward_kernel,
        grid=(pairs, seqs),
        in_specs=[
            pl.BlockSpec(block, lambda h, s: (s, h)),
            pl.BlockSpec(block, lambda h, s: (s, pairs + h)),
            pl.BlockSpec(block, lambda h, s: (s, 2 * pairs + h)),
            pl.BlockSpec(block, lambda h, s: (s, h)),
            pl.BlockSpec(block, lambda h, s: (s, h)),
            pl.BlockSpec((1, 2, LENGTH), lambda h, s: (s * pairs + h, 0, 0)),
        ],
        out_specs=[
            pl.BlockSpec((3,) + block, lambda h, s: (0, s, h)),
            pl.BlockSpec((8, 2 * HEAD_DIM), lambda h, s: (0, h)),
        ],
        out_shape=[
            jax.ShapeDtypeStruct((3, rows, D), BF),
            jax.ShapeDtypeStruct((8, D), F32),
        ],
        compiler_params=pltpu.CompilerParams(vmem_limit_bytes=48 * MB),
        name="attention_backward",
    )(projected, projected, projected, attended, grad_att, lse)


def gelu_parts(values):
    size = jnp.abs(values)
    frac = 1.0 / (1.0 + (0.3275911 * 0.7071067811865476) * size)
    expo = jnp.exp2(values * values * (-0.5 * LOG2E))
    poly = 1.061405429 * 0.5
    for coef in (-1.453152027, 1.421413741, -0.284496736, 0.254829592):
        poly = poly * frac + 0.5 * coef
    tail = poly * frac * expo
    cdf = jnp.where(values >= 0, 1.0 - tail, tail)
    return values * cdf, cdf + values * expo * 0.3989422804014327


def norm_parts(total):
    centre = jnp.mean(total, -1, keepdims=True)
    centered = total - centre
    variance = jnp.mean(centered * centered, -1, keepdims=True)
    scale = lax.rsqrt(variance + norm_eps)
    return centered * scale, scale


def norm_back(scaled, unit, scale):
    return scale * (
        scaled
        - jnp.mean(scaled, -1, keepdims=True)
        - unit * jnp.mean(scaled * unit, -1, keepdims=True)
    )


def middle_kernel(
    att_ref,
    x_ref,
    go_ref,
    mask_ref,
    wout_ref,
    wup_ref,
    wdown_ref,
    vec_ref,
    bup_ref,
    out_ref,
    normed_ref,
    hidden_ref,
    gmid_ref,
    gup_ref,
    gfirst_ref,
    gfirstb_ref,
    gatt_ref,
    sums_ref,
    slope_ref,
):
    @pl.when(pl.program_id(0) == 0)
    def _():
        sums_ref[...] = jnp.zeros_like(sums_ref)

    bias_out = vec_ref[0:1, :]
    gain_one = vec_ref[1:2, :]
    shift_one = vec_ref[2:3, :]
    bias_down = vec_ref[3:4, :]
    gain_two = vec_ref[4:5, :]
    shift_two = vec_ref[5:6, :]

    def note(row, values):
        sums_ref[row : row + 1, 0:D] += jnp.sum(values, 0, keepdims=True)

    branch = dot_nt(att_ref[...], wout_ref[...]) + bias_out
    unit_one, scale_one = norm_parts(x_ref[...] + branch)
    normed = unit_one * gain_one + shift_one
    normed_b = normed.astype(BF)
    normed_ref[...] = normed_b
    downward = jnp.zeros(normed.shape, F32)
    for start in range(0, FF, FF_TILE):
        cols = slice(start, start + FF_TILE)
        upward = dot_nt(normed_b, wup_ref[cols, :]) + bup_ref[0:1, cols]
        hidden, slope = gelu_parts(upward)
        slope_ref[:, cols] = slope
        hidden_b = hidden.astype(BF)
        hidden_ref[:, cols] = hidden_b
        downward += dot_nn(hidden_b, wdown_ref[cols, :])
    unit_two, scale_two = norm_parts(normed + downward + bias_down)
    out_ref[...] = (unit_two * gain_two + shift_two).astype(BF)
    g_out = go_ref[...].astype(F32) * mask_ref[...].astype(F32)
    note(5, g_out * unit_two)
    note(6, g_out)
    g_mid = norm_back(g_out * gain_two, unit_two, scale_two)
    note(4, g_mid)
    g_mid_b = g_mid.astype(BF)
    gmid_ref[...] = g_mid_b
    g_normed = g_mid
    for start in range(0, FF, FF_TILE):
        cols = slice(start, start + FF_TILE)
        g_up = dot_nt(g_mid_b, wdown_ref[cols, :]) * slope_ref[:, cols]
        sums_ref[0:1, cols] += jnp.sum(g_up, 0, keepdims=True)
        g_up_b = g_up.astype(BF)
        gup_ref[:, cols] = g_up_b
        g_normed += dot_nn(g_up_b, wup_ref[cols, :])
    note(2, g_normed * unit_one)
    note(3, g_normed)
    g_first = norm_back(g_normed * gain_one, unit_one, scale_one)
    note(1, g_first)
    gfirst_ref[...] = g_first
    g_first_b = g_first.astype(BF)
    gfirstb_ref[...] = g_first_b
    gatt_ref[...] = dot_nn(g_first_b, wout_ref[...]).astype(BF)


def middle(attended, inputs, out_grad, masked, w_out, w_up, w_down, vecs, bias_up):
    rows = attended.shape[0]
    tile = ROW_TILE

    def row(width):
        return pl.BlockSpec((tile, width), lambda i: (i, 0))

    def whole(shape):
        return pl.BlockSpec(
            shape, lambda i: (0, 0), pipeline_mode=pl.Buffered(buffer_count=1)
        )

    return pl.pallas_call(
        middle_kernel,
        grid=(rows // tile,),
        in_specs=[
            row(D),
            row(D),
            row(D),
            row(1),
            whole((D, D)),
            whole((FF, D)),
            whole((FF, D)),
            whole((8, D)),
            whole((1, FF)),
        ],
        out_specs=[
            row(D),
            row(D),
            row(FF),
            row(D),
            row(FF),
            row(D),
            row(D),
            row(D),
            pl.BlockSpec((8, FF), lambda i: (0, 0)),
        ],
        out_shape=[
            jax.ShapeDtypeStruct((rows, D), BF),
            jax.ShapeDtypeStruct((rows, D), BF),
            jax.ShapeDtypeStruct((rows, FF), BF),
            jax.ShapeDtypeStruct((rows, D), BF),
            jax.ShapeDtypeStruct((rows, FF), BF),
            jax.ShapeDtypeStruct((rows, D), F32),
            jax.ShapeDtypeStruct((rows, D), BF),
            jax.ShapeDtypeStruct((rows, D), BF),
            jax.ShapeDtypeStruct((8, FF), F32),
        ],
        scratch_shapes=[pltpu.VMEM((tile, FF), F32)],
        compiler_params=pltpu.CompilerParams(vmem_limit_bytes=56 * MB),
        name="middle",
    )(attended, inputs, out_grad, masked, w_out, w_up, w_down, vecs, bias_up)


def gather_ids(chosen, places):
    return jnp.concatenate([chosen, places])


def slots_of(ids, owned):
    count = ids.shape[0]
    order = jnp.arange(count, dtype=jnp.int32)
    repeated = jnp.any(
        (ids[:, None] == ids[None, :]) & (order[:, None] < order[None, :]), axis=0
    )
    first = jnp.logical_not(repeated)
    base = (ids // owned) * owned
    below = (
        first[:, None]
        & (ids[:, None] >= base[None, :])
        & (ids[:, None] < ids[None, :])
    )
    return jnp.sum(below.astype(jnp.int32), axis=0)


def requests_of(ids, owner, slot, owned, devices, start, room):
    key = jnp.where((slot >= start) & (slot < start + room), owner * room + slot - start, -1)
    spots = jnp.arange(devices * room, dtype=jnp.int32)
    asked = jnp.max(
        jnp.where(key[:, None] == spots[None, :], (ids - owner * owned)[:, None], -1), axis=0
    )
    return key, asked


def pick(index, amount):
    return (index[:, None] == jnp.arange(amount, dtype=jnp.int32)[None, :]).astype(BF)


def adam_direction(param, first, second, grad, corr_one, corr_two, decay):
    first_next = beta_one * first + (1.0 - beta_one) * grad
    second_next = beta_two * second + (1.0 - beta_two) * grad * grad
    update = first_next / corr_one / (jnp.sqrt(second_next / corr_two) + adam_eps)
    return (update + decay * param, first_next)


def body(
    devices,
    token_ids,
    masked,
    swap_kind,
    swap_ids,
    out_grad,
    embed_table,
    table_first,
    table_second,
    layer_mats,
    mats_first,
    mats_second,
    layer_vecs,
    vecs_first,
    vecs_second,
):
    axis = "fsdp"
    rows = token_ids.shape[0]
    seqs = rows // LENGTH
    owned = embed_table.shape[0]
    share = LENGTH // devices
    me = lax.axis_index(axis)
    replaced = jnp.where(swap_kind < 8, mask_token, jnp.where(swap_kind == 8, swap_ids, token_ids))
    chosen = jnp.where(masked == 1, replaced, token_ids)

    room = 16 * -(-1536 // (16 * devices))
    more = 16
    my_places = VOCAB + me * share + jnp.arange(share, dtype=jnp.int32)
    ids = gather_ids(chosen, my_places)
    owner = ids // owned
    slot = slots_of(ids, owned)
    most = jnp.max(slot) + 1
    key, asked = requests_of(ids, owner, slot, owned, devices, 0, room)
    table_b = embed_table.astype(BF)

    def swap(blocks):
        return lax.all_to_all(blocks, axis, 0, 0, tiled=True)

    notes = jnp.concatenate(
        [asked.reshape(devices, room), jnp.full((devices, 1), most, jnp.int32)], axis=1
    )
    notes = swap(notes)
    wanted = notes[:, :room].reshape(-1)
    longest = jnp.max(notes[:, room])
    found = dot_nn(pick(wanted, owned), table_b).astype(BF)
    found = swap(found.reshape(devices, room, D)).reshape(-1, D)
    got = dot_nn(pick(key, devices * room), found)
    rounds = (longest - room + more - 1) // more

    def fetch_more(state):
        turn, got = state
        key, asked = requests_of(ids, owner, slot, owned, devices, room + turn * more, more)
        wanted = swap(asked.reshape(devices, more)).reshape(-1)
        found = dot_nn(pick(wanted, owned), table_b).astype(BF)
        found = swap(found.reshape(devices, more, D)).reshape(-1, D)
        return turn + 1, got + dot_nn(pick(key, devices * more), found)

    _, got = lax.while_loop(lambda state: state[0] < rounds, fetch_more, (jnp.int32(0), got))
    place_rows = lax.all_gather(got[rows:].astype(BF), axis, axis=0, tiled=True)
    inputs = (
        got[:rows].reshape(seqs, LENGTH, D) + place_rows.astype(F32)[None]
    ).reshape(rows, D)
    inputs_b = inputs.astype(BF)

    mats_t = lax.all_gather(layer_mats.astype(BF).T, axis, axis=0, tiled=True)
    vecs = lax.all_gather(layer_vecs.astype(BF), axis, axis=0, tiled=True).astype(F32)
    w_qkv = mats_t[:QKV]
    w_out = mats_t[QKV : QKV + D]
    w_up = mats_t[QKV + D : QKV + D + FF]
    w_down = mats_t[QKV + D + FF :]
    bias_qkv = jnp.concatenate([vecs[:D], jnp.zeros((D,), F32), vecs[D : 2 * D]])
    bias_up = vecs[5 * D : 5 * D + FF][None]
    small = jnp.concatenate(
        [vecs[2 * D : 5 * D], vecs[5 * D + FF :], jnp.zeros((2 * D,), F32)]
    ).reshape(8, D)

    projected = (dot_nt(inputs_b, w_qkv) + bias_qkv).astype(BF)
    attended, lse = attention_forward(projected)
    (
        outputs,
        normed_b,
        hidden_b,
        g_mid_b,
        g_up_b,
        g_first,
        g_first_b,
        g_att_b,
        sums,
    ) = middle(
        attended, inputs, out_grad, masked[:, None], w_out, w_up, w_down, small, bias_up
    )
    g_w_up = dot_tn(g_up_b, normed_b).astype(BF)
    g_w_down = dot_tn(hidden_b, g_mid_b).astype(BF)
    g_w_out = dot_tn(g_first_b, attended).astype(BF)
    g_proj, bias_sums = attention_backward(projected, attended, g_att_b, lse)
    g_in = g_first
    g_w_qkv = []
    for part in range(3):
        g_in = g_in + dot_nn(g_proj[part], w_qkv[part * D : (part + 1) * D])
        g_w_qkv.append(dot_tn(g_proj[part], inputs_b).astype(BF))
    input_grad = g_in.astype(BF)

    g_mats = jnp.concatenate(g_w_qkv + [g_w_out, g_w_up, g_w_down], axis=0)
    mats_grad = (
        lax.psum_scatter(g_mats, axis, scatter_dimension=0, tiled=True).astype(F32).T
    )
    g_vecs = jnp.concatenate(
        [
            bias_sums[0],
            bias_sums[1],
            sums[1, :D],
            sums[2, :D],
            sums[3, :D],
            sums[0],
            sums[4, :D],
            sums[5, :D],
            sums[6, :D],
        ]
    )
    vecs_grad = lax.psum_scatter(g_vecs, axis, scatter_dimension=0, tiled=True)

    g_place = jnp.sum(g_in.reshape(seqs, LENGTH, D), 0).astype(BF)
    g_place = lax.psum_scatter(g_place, axis, scatter_dimension=0, tiled=True)
    g_ids = jnp.concatenate([input_grad, g_place], axis=0)
    sent = dot_tn(pick(key, devices * room), g_ids).astype(BF)
    sent = swap(sent.reshape(devices, room, D)).reshape(-1, D)
    table_grad = dot_tn(pick(wanted, owned), sent)

    def send_more(state):
        turn, total = state
        key, asked = requests_of(ids, owner, slot, owned, devices, room + turn * more, more)
        wanted = swap(asked.reshape(devices, more)).reshape(-1)
        sent = dot_tn(pick(key, devices * more), g_ids).astype(BF)
        sent = swap(sent.reshape(devices, more, D)).reshape(-1, D)
        return turn + 1, total + dot_tn(pick(wanted, owned), sent)

    _, table_grad = lax.while_loop(
        lambda state: state[0] < rounds, send_more, (jnp.int32(0), table_grad)
    )

    counter = jnp.float32(STEP)
    corr_one = 1.0 - jnp.power(jnp.float32(beta_one), counter)
    corr_two = 1.0 - jnp.power(jnp.float32(beta_two), counter)
    table_step, table_first_next = adam_direction(
        embed_table, table_first, table_second, table_grad, corr_one, corr_two, decay_rate
    )
    mats_step, mats_first_next = adam_direction(
        layer_mats, mats_first, mats_second, mats_grad, corr_one, corr_two, decay_rate
    )
    vecs_step, vecs_first_next = adam_direction(
        layer_vecs, vecs_first, vecs_second, vecs_grad, corr_one, corr_two, 0.0
    )
    return (
        outputs,
        input_grad,
        table_grad,
        mats_grad,
        vecs_grad,
        table_step,
        table_first_next,
        mats_step,
        mats_first_next,
        vecs_step,
        vecs_first_next,
    )


def solution(mesh):
    line = P("fsdp")
    by_rows = P("fsdp", None)
    by_cols = P(None, "fsdp")
    return jax.shard_map(
        functools.partial(body, mesh.shape["fsdp"]),
        mesh=mesh,
        in_specs=(
            line,
            line,
            line,
            line,
            by_rows,
            by_rows,
            by_rows,
            by_rows,
            by_cols,
            by_cols,
            by_cols,
            line,
            line,
            line,
        ),
        out_specs=(
            by_rows,
            by_rows,
            by_rows,
            by_cols,
            line,
            by_rows,
            by_rows,
            by_cols,
            by_cols,
            line,
            line,
        ),
        check_vma=False,
    )
```

```python
import functools

import jax
import jax.numpy as jnp
from jax import lax
from jax.experimental import pallas as pl
from jax.experimental.pallas import tpu as pltpu
from jax.sharding import PartitionSpec as P

D = 768
HEADS = 12
HEAD_DIM = 64
FF = 3072
VOCAB = 14592
LENGTH = 512
STEP = 10
QKV = 3 * D

norm_eps = 1e-12
mask_token = 103
beta_one = 0.9
beta_two = 0.999
adam_eps = 1e-06
decay_rate = 0.01

BF = jnp.bfloat16
F32 = jnp.float32
LOG2E = 1.4426950408889634
SCORE = HEAD_DIM ** (-0.5)
MB = 1024 * 1024

ROW_TILE = 256
FF_TILE = 768


def dot_nn(left, right):
    return lax.dot_general(
        left, right, (((1,), (0,)), ((), ())), preferred_element_type=F32
    )


def dot_nt(left, right):
    return lax.dot_general(
        left, right, (((1,), (1,)), ((), ())), preferred_element_type=F32
    )


def dot_tn(left, right):
    return lax.dot_general(
        left, right, (((0,), (0,)), ((), ())), preferred_element_type=F32
    )


def attention_forward_kernel(q_ref, k_ref, v_ref, att_ref, lse_ref):
    query = q_ref[...]
    keys = k_ref[...]
    values_t = v_ref[...].T
    lane = lax.broadcasted_iota(jnp.int32, query.shape, 1)
    outs = []
    for half in range(2):
        mine = (lane < HEAD_DIM) if half == 0 else (lane >= HEAD_DIM)
        picked = jnp.where(mine, query, jnp.zeros_like(query))
        scores = dot_nt(keys, picked)
        highest = jnp.max(scores, 0, keepdims=True)
        expo = jnp.exp2((scores - highest) * (SCORE * LOG2E))
        total = jnp.sum(expo, 0, keepdims=True)
        part = values_t[half * HEAD_DIM : (half + 1) * HEAD_DIM, :]
        outs.append(dot_nn(part, expo.astype(BF)) / total)
        lse_ref[0, half : half + 1, :] = highest * (SCORE * LOG2E) + jnp.log2(total)
    att_ref[...] = jnp.concatenate(outs, 0).T.astype(BF)


def attention_forward(projected):
    rows = projected.shape[0]
    seqs = rows // LENGTH
    pairs = HEADS // 2
    block = (LENGTH, 2 * HEAD_DIM)
    return pl.pallas_call(
        attention_forward_kernel,
        grid=(seqs, pairs),
        in_specs=[
            pl.BlockSpec(block, lambda s, h: (s, h)),
            pl.BlockSpec(block, lambda s, h: (s, pairs + h)),
            pl.BlockSpec(block, lambda s, h: (s, 2 * pairs + h)),
        ],
        out_specs=[
            pl.BlockSpec(block, lambda s, h: (s, h)),
            pl.BlockSpec((1, 2, LENGTH), lambda s, h: (s * pairs + h, 0, 0)),
        ],
        out_shape=[
            jax.ShapeDtypeStruct((rows, D), BF),
            jax.ShapeDtypeStruct((seqs * pairs, 2, LENGTH), F32),
        ],
        compiler_params=pltpu.CompilerParams(vmem_limit_bytes=48 * MB),
        name="attention_forward",
    )(projected, projected, projected)


def attention_backward_kernel(
    q_ref, k_ref, v_ref, att_ref, g_ref, lse_ref, out_ref, bias_ref
):
    query = q_ref[...]
    keys = k_ref[...]
    values = v_ref[...]
    grad = g_ref[...]
    lane = lax.broadcasted_iota(jnp.int32, query.shape, 1)
    first = lane < HEAD_DIM
    product = (att_ref[...].astype(F32) * grad.astype(F32)).T
    zero = jnp.zeros_like(query)
    g_q, g_k, g_v = [], [], []
    for half in range(2):
        mine = first if half == 0 else jnp.logical_not(first)
        scores = dot_nt(keys, jnp.where(mine, query, zero))
        probs = jnp.exp2(scores * (SCORE * LOG2E) - lse_ref[0, half : half + 1, :])
        delta = jnp.sum(
            product[half * HEAD_DIM : (half + 1) * HEAD_DIM, :], 0, keepdims=True
        )
        g_probs = dot_nt(values, jnp.where(mine, grad, zero))
        g_v.append(dot_nn(probs.astype(BF), grad))
        g_scores = (probs * (g_probs - delta)).astype(BF)
        g_k.append(dot_nn(g_scores, query))
        g_q.append(dot_tn(g_scores, keys))
    grad_q = jnp.where(first, g_q[0], g_q[1]) * SCORE
    grad_k = jnp.where(first, g_k[0], g_k[1]) * SCORE
    grad_v = jnp.where(first, g_v[0], g_v[1])
    out_ref[0] = grad_q.astype(BF)
    out_ref[1] = grad_k.astype(BF)
    out_ref[2] = grad_v.astype(BF)

    @pl.when(pl.program_id(1) == 0)
    def _():
        bias_ref[...] = jnp.zeros_like(bias_ref)

    bias_ref[0:1, :] += jnp.sum(grad_q, 0, keepdims=True)
    bias_ref[1:2, :] += jnp.sum(grad_v, 0, keepdims=True)


def attention_backward(projected, attended, grad_att, lse):
    rows = projected.shape[0]
    seqs = rows // LENGTH
    pairs = HEADS // 2
    block = (LENGTH, 2 * HEAD_DIM)
    return pl.pallas_call(
        attention_backward_kernel,
        grid=(pairs, seqs),
        in_specs=[
            pl.BlockSpec(block, lambda h, s: (s, h)),
            pl.BlockSpec(block, lambda h, s: (s, pairs + h)),
            pl.BlockSpec(block, lambda h, s: (s, 2 * pairs + h)),
            pl.BlockSpec(block, lambda h, s: (s, h)),
            pl.BlockSpec(block, lambda h, s: (s, h)),
            pl.BlockSpec((1, 2, LENGTH), lambda h, s: (s * pairs + h, 0, 0)),
        ],
        out_specs=[
            pl.BlockSpec((3,) + block, lambda h, s: (0, s, h)),
            pl.BlockSpec((8, 2 * HEAD_DIM), lambda h, s: (0, h)),
        ],
        out_shape=[
            jax.ShapeDtypeStruct((3, rows, D), BF),
            jax.ShapeDtypeStruct((8, D), F32),
        ],
        compiler_params=pltpu.CompilerParams(vmem_limit_bytes=48 * MB),
        name="attention_backward",
    )(projected, projected, projected, attended, grad_att, lse)


def gelu_parts(values):
    size = jnp.abs(values)
    frac = 1.0 / (1.0 + (0.3275911 * 0.7071067811865476) * size)
    expo = jnp.exp2(values * values * (-0.5 * LOG2E))
    poly = 1.061405429 * 0.5
    for coef in (-1.453152027, 1.421413741, -0.284496736, 0.254829592):
        poly = poly * frac + 0.5 * coef
    tail = poly * frac * expo
    cdf = jnp.where(values >= 0, 1.0 - tail, tail)
    return values * cdf, cdf + values * expo * 0.3989422804014327


def norm_parts(total):
    centre = jnp.mean(total, -1, keepdims=True)
    centered = total - centre
    variance = jnp.mean(centered * centered, -1, keepdims=True)
    scale = lax.rsqrt(variance + norm_eps)
    return centered * scale, scale


def norm_back(scaled, unit, scale):
    return scale * (
        scaled
        - jnp.mean(scaled, -1, keepdims=True)
        - unit * jnp.mean(scaled * unit, -1, keepdims=True)
    )


def middle_kernel(
    att_ref,
    x_ref,
    go_ref,
    mask_ref,
    wout_ref,
    wup_ref,
    wdown_ref,
    vec_ref,
    bup_ref,
    out_ref,
    normed_ref,
    hidden_ref,
    gmid_ref,
    gup_ref,
    gfirst_ref,
    gfirstb_ref,
    gatt_ref,
    sums_ref,
    slope_ref,
):
    @pl.when(pl.program_id(0) == 0)
    def _():
        sums_ref[...] = jnp.zeros_like(sums_ref)

    bias_out = vec_ref[0:1, :]
    gain_one = vec_ref[1:2, :]
    shift_one = vec_ref[2:3, :]
    bias_down = vec_ref[3:4, :]
    gain_two = vec_ref[4:5, :]
    shift_two = vec_ref[5:6, :]

    def note(row, values):
        sums_ref[row : row + 1, 0:D] += jnp.sum(values, 0, keepdims=True)

    branch = dot_nt(att_ref[...], wout_ref[...]) + bias_out
    unit_one, scale_one = norm_parts(x_ref[...] + branch)
    normed = unit_one * gain_one + shift_one
    normed_b = normed.astype(BF)
    normed_ref[...] = normed_b
    downward = jnp.zeros(normed.shape, F32)
    for start in range(0, FF, FF_TILE):
        cols = slice(start, start + FF_TILE)
        upward = dot_nt(normed_b, wup_ref[cols, :]) + bup_ref[0:1, cols]
        hidden, slope = gelu_parts(upward)
        slope_ref[:, cols] = slope
        hidden_b = hidden.astype(BF)
        hidden_ref[:, cols] = hidden_b
        downward += dot_nn(hidden_b, wdown_ref[cols, :])
    unit_two, scale_two = norm_parts(normed + downward + bias_down)
    out_ref[...] = (unit_two * gain_two + shift_two).astype(BF)
    g_out = go_ref[...].astype(F32) * mask_ref[...].astype(F32)
    note(5, g_out * unit_two)
    note(6, g_out)
    g_mid = norm_back(g_out * gain_two, unit_two, scale_two)
    note(4, g_mid)
    g_mid_b = g_mid.astype(BF)
    gmid_ref[...] = g_mid_b
    g_normed = g_mid
    for start in range(0, FF, FF_TILE):
        cols = slice(start, start + FF_TILE)
        g_up = dot_nt(g_mid_b, wdown_ref[cols, :]) * slope_ref[:, cols]
        sums_ref[0:1, cols] += jnp.sum(g_up, 0, keepdims=True)
        g_up_b = g_up.astype(BF)
        gup_ref[:, cols] = g_up_b
        g_normed += dot_nn(g_up_b, wup_ref[cols, :])
    note(2, g_normed * unit_one)
    note(3, g_normed)
    g_first = norm_back(g_normed * gain_one, unit_one, scale_one)
    note(1, g_first)
    gfirst_ref[...] = g_first
    g_first_b = g_first.astype(BF)
    gfirstb_ref[...] = g_first_b
    gatt_ref[...] = dot_nn(g_first_b, wout_ref[...]).astype(BF)


def middle(attended, inputs, out_grad, masked, mats_t, vecs, bias_up):
    rows = attended.shape[0]
    tile = ROW_TILE

    def row(width):
        return pl.BlockSpec((tile, width), lambda i: (i, 0))

    def whole(shape, place=0):
        return pl.BlockSpec(
            shape, lambda i: (place, 0), pipeline_mode=pl.Buffered(buffer_count=1)
        )

    return pl.pallas_call(
        middle_kernel,
        grid=(rows // tile,),
        in_specs=[
            row(D),
            row(D),
            row(D),
            row(1),
            whole((D, D), 3),
            whole((FF, D), 1),
            whole((FF, D), 2),
            whole((8, D)),
            whole((1, FF)),
        ],
        out_specs=[
            row(D),
            row(D),
            row(FF),
            row(D),
            row(FF),
            row(D),
            row(D),
            row(D),
            pl.BlockSpec((8, FF), lambda i: (0, 0)),
        ],
        out_shape=[
            jax.ShapeDtypeStruct((rows, D), BF),
            jax.ShapeDtypeStruct((rows, D), BF),
            jax.ShapeDtypeStruct((rows, FF), BF),
            jax.ShapeDtypeStruct((rows, D), BF),
            jax.ShapeDtypeStruct((rows, FF), BF),
            jax.ShapeDtypeStruct((rows, D), F32),
            jax.ShapeDtypeStruct((rows, D), BF),
            jax.ShapeDtypeStruct((rows, D), BF),
            jax.ShapeDtypeStruct((8, FF), F32),
        ],
        scratch_shapes=[pltpu.VMEM((tile, FF), F32)],
        compiler_params=pltpu.CompilerParams(vmem_limit_bytes=56 * MB),
        name="middle",
    )(attended, inputs, out_grad, masked, mats_t, mats_t, mats_t, vecs, bias_up)


def entry_kernel(
    key_ref, found_ref, extra_ref, place_ref, w_ref, bias_ref, x_ref, xb_ref, proj_ref
):
    slots = lax.broadcasted_iota(jnp.int32, (LENGTH, found_ref.shape[0]), 1)
    picked = (key_ref[...] == slots).astype(BF)
    inputs = dot_nn(picked, found_ref[...]) + extra_ref[...].astype(F32)
    inputs = inputs + place_ref[...].astype(F32)
    x_ref[...] = inputs
    inputs_b = inputs.astype(BF)
    xb_ref[...] = inputs_b
    for start in range(0, QKV, D):
        cols = slice(start, start + D)
        part = dot_nt(inputs_b, w_ref[cols, :]) + bias_ref[:, cols]
        proj_ref[:, cols] = part.astype(BF)


def fixed(shape, place=0):
    return pl.BlockSpec(
        shape, lambda i: (place, 0), pipeline_mode=pl.Buffered(buffer_count=1)
    )


def entry(key, found, extra, places, mats_t, bias):
    rows = key.shape[0]
    slots = found.shape[0]

    def row(width):
        return pl.BlockSpec((LENGTH, width), lambda i: (i, 0))

    return pl.pallas_call(
        entry_kernel,
        grid=(rows // LENGTH,),
        in_specs=[
            row(1),
            fixed((slots, D)),
            row(D),
            fixed((LENGTH, D)),
            fixed((QKV, D)),
            fixed((1, QKV)),
        ],
        out_specs=[row(D), row(D), row(QKV)],
        out_shape=[
            jax.ShapeDtypeStruct((rows, D), F32),
            jax.ShapeDtypeStruct((rows, D), BF),
            jax.ShapeDtypeStruct((rows, QKV), BF),
        ],
        compiler_params=pltpu.CompilerParams(vmem_limit_bytes=56 * MB),
        cost_estimate=pl.CostEstimate(
            flops=13_000_000_000, bytes_accessed=40_000_000, transcendentals=0
        ),
        name="entry",
    )(key[:, None], found, extra, places, mats_t, bias)


def finish_kernel(
    proj_ref, first_ref, xb_ref, w_ref, grad_ref, place_ref, weights_ref, total, places
):
    step = pl.program_id(0)

    @pl.when(step == 0)
    def _():
        total[...] = jnp.zeros_like(total)
        places[...] = jnp.zeros_like(places)

    g_in = first_ref[...]
    inputs_b = xb_ref[...]
    for part in range(3):
        cols = slice(part * D, (part + 1) * D)
        g_in = g_in + dot_nn(proj_ref[part], w_ref[cols, :])
        total[cols, :] += dot_tn(proj_ref[part], inputs_b)
    grad_ref[...] = g_in.astype(BF)
    places[...] += g_in

    @pl.when(step == pl.num_programs(0) - 1)
    def _():
        weights_ref[...] = total[...].astype(BF)
        place_ref[...] = places[...].astype(BF)


def finish(g_proj, g_first, inputs_b, mats_t):
    rows = g_first.shape[0]

    def row(width):
        return pl.BlockSpec((LENGTH, width), lambda i: (i, 0))

    return pl.pallas_call(
        finish_kernel,
        grid=(rows // LENGTH,),
        in_specs=[
            pl.BlockSpec((3, LENGTH, D), lambda i: (0, i, 0)),
            row(D),
            row(D),
            fixed((QKV, D)),
        ],
        out_specs=[
            row(D),
            pl.BlockSpec((LENGTH, D), lambda i: (0, 0)),
            pl.BlockSpec((QKV, D), lambda i: (0, 0)),
        ],
        out_shape=[
            jax.ShapeDtypeStruct((rows, D), BF),
            jax.ShapeDtypeStruct((LENGTH, D), BF),
            jax.ShapeDtypeStruct((QKV, D), BF),
        ],
        scratch_shapes=[pltpu.VMEM((QKV, D), F32), pltpu.VMEM((LENGTH, D), F32)],
        compiler_params=pltpu.CompilerParams(vmem_limit_bytes=56 * MB),
        cost_estimate=pl.CostEstimate(
            flops=15_000_000_000, bytes_accessed=40_000_000, transcendentals=0
        ),
        name="finish",
    )(g_proj, g_first, inputs_b, mats_t)


MESH = pl.DeviceIdType.MESH
PLANES = 4


def neighbours():
    me = lax.axis_index("fsdp")
    core = lax.rem(me, 2)
    x = lax.rem(me // 2, 2)
    y = lax.rem(me // 4, 2)
    z = me // 8
    step_a = 4 - 2 * core
    step_b = 2 + 2 * core
    a = jnp.where(core == 0, y, x)
    b = jnp.where(core == 0, x, y)
    near_a = me + step_a * (1 - 2 * a)
    near_b = me + step_b * (1 - 2 * b)
    twin = me + 1 - 2 * core
    return me, core, z, a, b, step_a, step_b, near_a, near_b, twin


def greet(me, z, near_a, near_b, twin):
    barrier = pltpu.get_barrier_semaphore()

    def hello(device):
        pl.semaphore_signal(barrier, inc=1, device_id=(device,), device_id_type=MESH)

    for device in (near_a, near_b, twin):
        hello(device)

    @pl.when(z > 0)
    def _():
        hello(me - 8)

    @pl.when(z < PLANES - 1)
    def _():
        hello(me + 8)

    inner = jnp.logical_and(z > 0, z < PLANES - 1)
    pl.semaphore_wait(barrier, jnp.where(inner, 5, 4))


def collect_kernel(
    low_ref,
    rest_ref,
    out_ref,
    own,
    from_twin,
    from_b,
    from_a,
    from_low,
    from_high,
    load_sem,
    twin_sem,
    b_sem,
    a_sem,
    low_sem,
    high_sem,
):
    me, core, z, a, b, step_a, step_b, near_a, near_b, twin = neighbours()
    greet(me, z, near_a, near_b, twin)
    waits = []

    def remote(source, target, sems, slot, device):
        return pltpu.make_async_remote_copy(
            src_ref=source,
            dst_ref=target.at[slot],
            send_sem=sems.at[0, slot],
            recv_sem=sems.at[1, slot],
            device_id=(device,),
            device_id_type=MESH,
        )

    def plane_of(turn):
        return jnp.where(z < 2, PLANES - 1 - turn, turn)

    def parts(slot):
        return slot // 8 == 0, slot % 8 // 2, slot % 2 == 0

    loads, gifts = [], []
    for slot in range(16):
        other_b, turn, other_a = parts(slot)
        plane = plane_of(turn)
        a_at = 1 - a if other_a else a
        b_at = 1 - b if other_b else b
        shard = plane * 8 + a_at * step_a + b_at * step_b + core
        loads.append(
            (
                plane,
                pltpu.make_async_copy(low_ref.at[shard % 8], own.at[slot], load_sem.at[slot]),
                pltpu.make_async_copy(
                    rest_ref.at[jnp.maximum(shard - 8, 0)], own.at[slot], load_sem.at[slot]
                ),
            )
        )
        a_at = 1 - b if other_a else b
        b_at = 1 - a if other_b else a
        shard = plane * 8 + a_at * step_b + b_at * step_a + 1 - core
        gifts.append(
            (
                plane,
                remote(low_ref.at[shard % 8], from_twin, twin_sem, slot, twin),
                remote(rest_ref.at[jnp.maximum(shard - 8, 0)], from_twin, twin_sem, slot, twin),
            )
        )
    order = []
    for turn in range(PLANES):
        order += [2 * turn, 2 * turn + 1]
        if turn:
            order += [8 + 2 * turn - 2, 8 + 2 * turn - 1]
    order += [14, 15]
    for slot in order:
        for plane, from_first, from_rest in (gifts[slot], loads[slot]):
            pl.when(plane == 0)(from_first.start)
            pl.when(plane > 0)(from_rest.start)

    def add(slot, arrived):
        own[slot] = (own[slot].astype(F32) + arrived[...].astype(F32)).astype(BF)

    def stage_twin(slot):
        loads[slot][2].wait()
        gifts[slot][2].wait_recv()
        add(slot, from_twin.at[slot])

    def stage_far(turn):
        for slot in (2 * turn, 2 * turn + 1):
            stage_twin(slot)
            item = remote(own.at[slot], from_b, b_sem, slot, near_b)
            item.start()
            waits.append(item)

    def stage_near(turn):
        for slot in (2 * turn, 2 * turn + 1):
            stage_twin(8 + slot)

    def stage_b(turn):
        for slot in (2 * turn, 2 * turn + 1):
            remote(own.at[slot], from_b, b_sem, slot, near_b).wait_recv()
            add(8 + slot, from_b.at[slot])
            if slot % 2 == 0:
                item = remote(own.at[8 + slot], from_a, a_sem, turn, near_a)
                item.start()
                waits.append(item)

    def along(target, plane, source, up):
        if up:
            return remote(source, from_low, low_sem, plane, me + 8)
        return remote(source, from_high, high_sem, plane, me - 8)

    ends = []

    def stage_a(turn):
        slot = 9 + 2 * turn
        plane = plane_of(turn)
        remote(own.at[slot], from_a, a_sem, turn, near_a).wait_recv()
        add(slot, from_a.at[turn])

        @pl.when(plane > z)
        def _():
            @pl.when(z > 0)
            def _():
                along(None, plane, own.at[slot], True).wait_recv()
                add(slot, from_low.at[plane])

            along(None, plane, own.at[slot], True).start()

        @pl.when(plane < z)
        def _():
            @pl.when(z < PLANES - 1)
            def _():
                along(None, plane, own.at[slot], False).wait_recv()
                add(slot, from_high.at[plane])

            along(None, plane, own.at[slot], False).start()

        ends.append((plane > z, functools.partial(along, None, plane, own.at[slot], True)))
        ends.append((plane < z, functools.partial(along, None, plane, own.at[slot], False)))

        @pl.when(plane == z)
        def _():
            out_ref[...] = own[slot].astype(F32)

            @pl.when(z > 0)
            def _():
                along(None, plane, own.at[slot], True).wait_recv()
                out_ref[...] += from_low[plane].astype(F32)

            @pl.when(z < PLANES - 1)
            def _():
                along(None, plane, own.at[slot], False).wait_recv()
                out_ref[...] += from_high[plane].astype(F32)

    stage_far(0)
    stage_far(1)
    stage_near(0)
    stage_b(0)
    stage_far(2)
    stage_near(1)
    stage_b(1)
    stage_a(0)
    stage_far(3)
    stage_near(2)
    stage_b(2)
    stage_a(1)
    stage_near(3)
    stage_b(3)
    stage_a(2)
    stage_a(3)
    for _, _, item in gifts:
        item.wait_send()
    for item in waits:
        item.wait_send()
    for condition, item in ends:
        pl.when(condition)(lambda item=item: item().wait_send())


def collect(low, rest, ident):
    shape = rest.shape[1:]
    return pl.pallas_call(
        collect_kernel,
        in_specs=[pl.BlockSpec(memory_space=pl.ANY)] * 2,
        out_specs=pl.BlockSpec(memory_space=pltpu.VMEM),
        out_shape=jax.ShapeDtypeStruct(shape, F32),
        scratch_shapes=[
            pltpu.VMEM((16,) + shape, BF),
            pltpu.VMEM((16,) + shape, BF),
            pltpu.VMEM((8,) + shape, BF),
            pltpu.VMEM((4,) + shape, BF),
            pltpu.VMEM((4,) + shape, BF),
            pltpu.VMEM((4,) + shape, BF),
            pltpu.SemaphoreType.DMA((16,)),
            pltpu.SemaphoreType.DMA((2, 16)),
            pltpu.SemaphoreType.DMA((2, 8)),
            pltpu.SemaphoreType.DMA((2, 4)),
            pltpu.SemaphoreType.DMA((2, 4)),
            pltpu.SemaphoreType.DMA((2, 4)),
        ],
        compiler_params=pltpu.CompilerParams(
            collective_id=ident, has_side_effects=True, vmem_limit_bytes=56 * MB
        ),
        cost_estimate=pl.CostEstimate(
            flops=20_000_000, bytes_accessed=300_000_000, transcendentals=0
        ),
        name="collect",
    )(low, rest)


PIECES = 4


def share_places_kernel(split, table_ref, out_ref, stage, load_sem, send_sem, recv_sem):
    first_owner, first_row, count = split
    me, core, z, a, b, step_a, step_b, near_a, near_b, twin = neighbours()
    greet(me, z, near_a, near_b, twin)
    rows = LENGTH // PIECES
    root = first_owner + 1
    gift = pltpu.make_async_remote_copy(
        src_ref=table_ref.at[pl.ds(first_row, count)],
        dst_ref=stage.at[pl.ds(0, count)],
        send_sem=load_sem.at[0],
        recv_sem=load_sem.at[1],
        device_id=(root,),
        device_id_type=MESH,
    )
    mine = pltpu.make_async_copy(
        table_ref.at[pl.ds(0, LENGTH - count)],
        stage.at[pl.ds(count, LENGTH - count)],
        load_sem.at[2],
    )

    @pl.when(me == first_owner)
    def _():
        gift.start()

    @pl.when(me == root)
    def _():
        mine.start()
        mine.wait()
        gift.wait_recv()

    def copy(piece, device, kind):
        part = pl.ds(piece * rows, rows)
        return pltpu.make_async_remote_copy(
            src_ref=out_ref.at[part],
            dst_ref=out_ref.at[part],
            send_sem=send_sem.at[kind, piece],
            recv_sem=recv_sem.at[piece],
            device_id=(device,),
            device_id_type=MESH,
        )

    trunk = jnp.logical_and(core == 1, jnp.logical_and(a == 1, b == 1))
    branch = jnp.logical_and(core == 1, jnp.logical_and(a == 0, b == 1))
    routes = (
        (jnp.logical_and(trunk, z > 0), me - 8),
        (trunk, near_a),
        (jnp.logical_or(trunk, branch), near_b),
        (core == 1, twin),
    )
    for piece in range(PIECES):
        part = slice(piece * rows, (piece + 1) * rows)

        @pl.when(me == root)
        def _(part=part):
            out_ref[part, :] = stage[part, :].astype(BF)

        @pl.when(me != root)
        def _(piece=piece):
            copy(piece, twin, 3).wait_recv()

        for kind, (goes, device) in enumerate(routes):

            @pl.when(goes)
            def _(piece=piece, device=device, kind=kind):
                copy(piece, device, kind).start()

    for piece in range(PIECES):
        for kind, (goes, device) in enumerate(routes):

            @pl.when(goes)
            def _(piece=piece, device=device, kind=kind):
                copy(piece, device, kind).wait_send()

    @pl.when(me == first_owner)
    def _():
        gift.wait_send()


def place_split(devices, owned):
    first_owner = VOCAB // owned
    first_row = VOCAB - first_owner * owned
    return first_owner, first_row, owned - first_row


def share_places(table, split, ident):
    return pl.pallas_call(
        functools.partial(share_places_kernel, split),
        in_specs=[pl.BlockSpec(memory_space=pl.ANY)],
        out_specs=pl.BlockSpec(memory_space=pltpu.VMEM),
        out_shape=jax.ShapeDtypeStruct((LENGTH, D), BF),
        scratch_shapes=[
            pltpu.VMEM((LENGTH, D), F32),
            pltpu.SemaphoreType.DMA((3,)),
            pltpu.SemaphoreType.DMA((4, PIECES)),
            pltpu.SemaphoreType.DMA((PIECES,)),
        ],
        compiler_params=pltpu.CompilerParams(collective_id=ident, has_side_effects=True),
        cost_estimate=pl.CostEstimate(flops=0, bytes_accessed=60_000_000, transcendentals=0),
        name="share_places",
    )(table)


def return_places_kernel(
    split,
    in_ref,
    out_ref,
    sums,
    from_twin,
    from_b,
    from_a,
    from_z,
    ready,
    sems,
    z_sem,
    piece_sem,
    home_sem,
):
    first_owner, first_row, count = split
    root = first_owner + 1
    me, core, z, a, b, step_a, step_b, near_a, near_b, twin = neighbours()
    rows = in_ref.shape[4]
    owned = out_ref.shape[0]
    out_ref[...] = jnp.zeros_like(out_ref)
    barrier = pltpu.get_barrier_semaphore()

    def hello(device):
        pl.semaphore_signal(barrier, inc=1, device_id=(device,), device_id_type=MESH)

    def each(step, carry):
        hello(lax.rem(me + step, 32))
        return carry

    lax.fori_loop(1, 32, each, 0)
    pl.semaphore_wait(barrier, 31)

    def remote(source, target, sem, device):
        return pltpu.make_async_remote_copy(
            src_ref=source,
            dst_ref=target,
            send_sem=sem.at[0],
            recv_sem=sem.at[1],
            device_id=(device,),
            device_id_type=MESH,
        )

    def add(total, extra):
        return (total.astype(F32) + extra.astype(F32)).astype(BF)

    x = jnp.where(core == 0, b, a)
    y = jnp.where(core == 0, a, b)
    gift = remote(in_ref.at[:, :, :, 1 - core], from_twin, sems.at[0], twin)
    gift.start()
    gift.wait_recv()
    sums[...] = add(in_ref[:, :, :, core], from_twin[...])

    @pl.when(core == 0)
    def _():
        item = remote(sums.at[:, :, 1 - x], from_b, sems.at[1], near_b)
        item.start()
        item.wait_recv()
        from_b[...] = add(sums[:, :, x], from_b[...])

    @pl.when(core == 1)
    def _():
        item = remote(sums.at[:, 1 - y], from_b, sems.at[1], near_b)
        item.start()
        item.wait_recv()
        from_b[...] = add(sums[:, y], from_b[...])

    item = remote(from_b.at[:, 1 - a], from_a, sems.at[2], near_a)
    item.start()
    item.wait_recv()
    from_a[...] = add(from_b[:, a], from_a[...])

    def column(plane, action):
        @pl.when(plane != z)
        def _():
            item = pltpu.make_async_remote_copy(
                src_ref=from_a.at[plane],
                dst_ref=from_z.at[z],
                send_sem=z_sem.at[0, plane],
                recv_sem=z_sem.at[1, z],
                device_id=(me + 8 * (plane - z),),
                device_id_type=MESH,
            )
            action(item)

    for plane in range(PLANES):
        column(plane, lambda item: item.start())
    ready[...] = from_a[z].astype(F32)
    for plane in range(PLANES):

        @pl.when(plane != z)
        def _(plane=plane):
            pltpu.make_async_remote_copy(
                src_ref=from_a.at[plane],
                dst_ref=from_z.at[plane],
                send_sem=z_sem.at[0, plane],
                recv_sem=z_sem.at[1, plane],
                device_id=(twin,),
                device_id_type=MESH,
            ).wait_recv()
            ready[...] += from_z[plane].astype(F32)

    def home(device, half):
        place = device * rows + half * 8
        early = place < count
        owner = jnp.where(early, first_owner, root)
        spot = pl.multiple_of(jnp.where(early, first_row + place, place - count), 8)
        return owner, spot

    def piece(device, half):
        owner, spot = home(device, half)
        return pltpu.make_async_remote_copy(
            src_ref=ready.at[pl.ds(half * 8, 8)],
            dst_ref=out_ref.at[pl.ds(spot, 8)],
            send_sem=piece_sem.at[half],
            recv_sem=home_sem.at[device * 2 + half],
            device_id=(owner,),
            device_id_type=MESH,
        )

    for half in range(rows // 8):
        owner, spot = home(me, half)

        @pl.when(owner == me)
        def _(half=half, spot=spot):
            out_ref[pl.ds(spot, 8), :] = ready[half * 8 : half * 8 + 8, :]

        @pl.when(owner != me)
        def _(half=half):
            piece(me, half).start()

    def arrive(index, carry):
        device, half = index // 2, lax.rem(index, 2)
        owner, _ = home(device, half)

        @pl.when(jnp.logical_and(owner == me, device != me))
        def _():
            piece(device, half).wait_recv()

        return carry

    lax.fori_loop(0, 64, arrive, 0)
    for half in range(rows // 8):
        owner, _ = home(me, half)

        @pl.when(owner != me)
        def _(half=half):
            piece(me, half).wait_send()

    gift.wait_send()
    remote(sums.at[:, 0], from_b, sems.at[1], near_b).wait_send()
    item.wait_send()
    for plane in range(PLANES):
        column(plane, lambda item: item.wait_send())


def return_places(sums, owned, split, ident):
    rows = LENGTH // 32
    shape = (rows, D)
    return pl.pallas_call(
        functools.partial(return_places_kernel, split),
        in_specs=[pl.BlockSpec(memory_space=pltpu.VMEM)],
        out_specs=pl.BlockSpec(memory_space=pltpu.VMEM),
        out_shape=jax.ShapeDtypeStruct((owned, D), F32),
        scratch_shapes=[
            pltpu.VMEM((4, 2, 2) + shape, BF),
            pltpu.VMEM((4, 2, 2) + shape, BF),
            pltpu.VMEM((4, 2) + shape, BF),
            pltpu.VMEM((4,) + shape, BF),
            pltpu.VMEM((4,) + shape, BF),
            pltpu.VMEM(shape, F32),
            pltpu.SemaphoreType.DMA((3, 2)),
            pltpu.SemaphoreType.DMA((2, 4)),
            pltpu.SemaphoreType.DMA((2,)),
            pltpu.SemaphoreType.DMA((64,)),
        ],
        compiler_params=pltpu.CompilerParams(collective_id=ident, has_side_effects=True),
        cost_estimate=pl.CostEstimate(flops=0, bytes_accessed=60_000_000, transcendentals=0),
        name="return_places",
    )(sums.reshape((4, 2, 2, 2) + shape))


def slots_of(ids, owned):
    count = ids.shape[0]
    order = jnp.arange(count, dtype=jnp.int32)
    repeated = jnp.any(
        (ids[:, None] == ids[None, :]) & (order[:, None] < order[None, :]), axis=0
    )
    first = jnp.logical_not(repeated)
    base = (ids // owned) * owned
    below = (
        first[:, None]
        & (ids[:, None] >= base[None, :])
        & (ids[:, None] < ids[None, :])
    )
    return jnp.sum(below.astype(jnp.int32), axis=0)


def requests_of(ids, owner, slot, owned, devices, start, room):
    key = jnp.where((slot >= start) & (slot < start + room), owner * room + slot - start, -1)
    spots = jnp.arange(devices * room, dtype=jnp.int32)
    asked = jnp.max(
        jnp.where(key[:, None] == spots[None, :], (ids - owner * owned)[:, None], -1), axis=0
    )
    return key, asked


def pick(index, amount):
    return (index[:, None] == jnp.arange(amount, dtype=jnp.int32)[None, :]).astype(BF)


def adam_direction(param, first, second, grad, corr_one, corr_two, decay):
    first_next = beta_one * first + (1.0 - beta_one) * grad
    second_next = beta_two * second + (1.0 - beta_two) * grad * grad
    update = first_next / corr_one / (jnp.sqrt(second_next / corr_two) + adam_eps)
    return (update + decay * param, first_next)


def body(
    devices,
    token_ids,
    masked,
    swap_kind,
    swap_ids,
    out_grad,
    embed_table,
    table_first,
    table_second,
    layer_mats,
    mats_first,
    mats_second,
    layer_vecs,
    vecs_first,
    vecs_second,
):
    axis = "fsdp"
    rows = token_ids.shape[0]
    owned = embed_table.shape[0]
    entries = layer_vecs.shape[0]
    columns = layer_mats.shape[1]
    me = lax.axis_index(axis)
    by_kernel = devices == 32
    split = place_split(devices, owned)
    replaced = jnp.where(swap_kind < 8, mask_token, jnp.where(swap_kind == 8, swap_ids, token_ids))
    chosen = jnp.where(masked == 1, replaced, token_ids)

    def swap(blocks):
        return lax.all_to_all(blocks, axis, 0, 0, tiled=True)

    mats_t = lax.all_gather(layer_mats.astype(BF).T, axis, axis=0, tiled=True)

    room = 16 * -(-1536 // (16 * devices))
    more = 16
    owner = chosen // owned
    slot = slots_of(chosen, owned)
    most = jnp.max(slot) + 1
    key, asked = requests_of(chosen, owner, slot, owned, devices, 0, room)
    table_b = embed_table.astype(BF)
    own_vecs = layer_vecs.astype(BF).astype(F32)
    notes = jnp.concatenate(
        [
            asked.reshape(devices, room).astype(F32),
            jnp.broadcast_to(own_vecs[None], (devices, entries)),
            jnp.broadcast_to(most.astype(F32), (devices, 1)),
        ],
        axis=1,
    )
    notes = swap(notes)
    wanted = notes[:, :room].astype(jnp.int32).reshape(-1)
    vecs = notes[:, room : room + entries].reshape(-1)
    longest = jnp.max(notes[:, room + entries]).astype(jnp.int32)
    found = dot_nn(pick(wanted, owned), table_b).astype(BF)
    found = swap(found.reshape(devices, room, D)).reshape(-1, D)
    if by_kernel:
        places = share_places(embed_table, split, 1)
    else:
        spots = VOCAB + jnp.arange(LENGTH, dtype=jnp.int32) - me * owned
        places = lax.psum(dot_nn(pick(spots, owned), table_b), axis).astype(BF)
    rounds = (longest - room + more - 1) // more

    def fetch_more(state):
        turn, extra = state
        key, asked = requests_of(chosen, owner, slot, owned, devices, room + turn * more, more)
        wanted = swap(asked.reshape(devices, more)).reshape(-1)
        found = dot_nn(pick(wanted, owned), table_b).astype(BF)
        found = swap(found.reshape(devices, more, D)).reshape(-1, D)
        return turn + 1, extra + dot_nn(pick(key, devices * more), found).astype(BF)

    _, extra = lax.while_loop(
        lambda state: state[0] < rounds, fetch_more, (jnp.int32(0), jnp.zeros((rows, D), BF))
    )

    bias_qkv = jnp.concatenate([vecs[:D], jnp.zeros((D,), F32), vecs[D : 2 * D]])[None]
    bias_up = vecs[5 * D : 5 * D + FF][None]
    small = jnp.concatenate(
        [vecs[2 * D : 5 * D], vecs[5 * D + FF :], jnp.zeros((2 * D,), F32)]
    ).reshape(8, D)

    inputs, inputs_b, projected = entry(key, found, extra, places, mats_t, bias_qkv)
    attended, lse = attention_forward(projected)
    (
        outputs,
        normed_b,
        hidden_b,
        g_mid_b,
        g_up_b,
        g_first,
        g_first_b,
        g_att_b,
        sums,
    ) = middle(attended, inputs, out_grad, masked[:, None], mats_t, small, bias_up)
    g_rest = jnp.concatenate(
        [
            dot_tn(g_first_b, attended).astype(BF),
            dot_tn(g_up_b, normed_b).astype(BF),
            dot_tn(hidden_b, g_mid_b).astype(BF),
        ],
        axis=0,
    )
    g_proj, bias_sums = attention_backward(projected, attended, g_att_b, lse)
    input_grad, g_places, g_qkv = finish(g_proj, g_first, inputs_b, mats_t)

    sent = dot_tn(pick(key, devices * room), input_grad).astype(BF)
    g_vecs = jnp.concatenate(
        [
            bias_sums[0],
            bias_sums[1],
            sums[1, :D],
            sums[2, :D],
            sums[3, :D],
            sums[0],
            sums[4, :D],
            sums[5, :D],
            sums[6, :D],
        ]
    )
    vecs_grad = jnp.sum(swap(g_vecs.reshape(devices, entries)), axis=0)
    sent, g_places, g_qkv, g_rest = lax.optimization_barrier((sent, g_places, g_qkv, g_rest))
    sent = swap(sent.reshape(devices, room, D)).reshape(-1, D)
    if by_kernel:
        g_own_places = return_places(g_places, owned, split, 2)
        mats_grad = collect(
            g_qkv.reshape(-1, columns, D), g_rest.reshape(-1, columns, D), 3
        ).T
    else:
        total = lax.psum(g_places.astype(F32), axis)
        spots = me * owned + jnp.arange(owned, dtype=jnp.int32) - VOCAB
        inside = (spots >= 0) & (spots < LENGTH)
        g_own_places = jnp.where(
            inside[:, None], total[jnp.clip(spots, 0, LENGTH - 1)], 0.0
        )
        mats_grad = lax.psum_scatter(
            jnp.concatenate([g_qkv, g_rest], axis=0), axis, scatter_dimension=0, tiled=True
        )
        mats_grad = mats_grad.astype(F32).T
    table_grad = dot_tn(pick(wanted, owned), sent) + g_own_places

    def send_more(state):
        turn, total = state
        key, asked = requests_of(chosen, owner, slot, owned, devices, room + turn * more, more)
        wanted = swap(asked.reshape(devices, more)).reshape(-1)
        sent = dot_tn(pick(key, devices * more), input_grad).astype(BF)
        sent = swap(sent.reshape(devices, more, D)).reshape(-1, D)
        return turn + 1, total + dot_tn(pick(wanted, owned), sent)

    _, table_grad = lax.while_loop(
        lambda state: state[0] < rounds, send_more, (jnp.int32(0), table_grad)
    )

    counter = jnp.float32(STEP)
    corr_one = 1.0 - jnp.power(jnp.float32(beta_one), counter)
    corr_two = 1.0 - jnp.power(jnp.float32(beta_two), counter)
    table_step, table_first_next = adam_direction(
        embed_table, table_first, table_second, table_grad, corr_one, corr_two, decay_rate
    )
    mats_step, mats_first_next = adam_direction(
        layer_mats, mats_first, mats_second, mats_grad, corr_one, corr_two, decay_rate
    )
    vecs_step, vecs_first_next = adam_direction(
        layer_vecs, vecs_first, vecs_second, vecs_grad, corr_one, corr_two, 0.0
    )
    return (
        outputs,
        input_grad,
        table_grad,
        mats_grad,
        vecs_grad,
        table_step,
        table_first_next,
        mats_step,
        mats_first_next,
        vecs_step,
        vecs_first_next,
    )


def solution(mesh):
    line = P("fsdp")
    by_rows = P("fsdp", None)
    by_cols = P(None, "fsdp")
    return jax.shard_map(
        functools.partial(body, mesh.shape["fsdp"]),
        mesh=mesh,
        in_specs=(
            line,
            line,
            line,
            line,
            by_rows,
            by_rows,
            by_rows,
            by_rows,
            by_cols,
            by_cols,
            by_cols,
            line,
            line,
            line,
        ),
        out_specs=(
            by_rows,
            by_rows,
            by_rows,
            by_cols,
            line,
            by_rows,
            by_rows,
            by_cols,
            by_cols,
            line,
            line,
        ),
        check_vma=False,
    )
```

```python
import functools

import jax
import jax.numpy as jnp
from jax import lax
from jax.experimental import pallas as pl
from jax.experimental.pallas import tpu as pltpu
from jax.sharding import PartitionSpec as P

D = 768
HEADS = 12
HEAD_DIM = 64
FF = 3072
VOCAB = 14592
LENGTH = 512
STEP = 10
QKV = 3 * D

norm_eps = 1e-12
mask_token = 103
beta_one = 0.9
beta_two = 0.999
adam_eps = 1e-06
decay_rate = 0.01

BF = jnp.bfloat16
F32 = jnp.float32
LOG2E = 1.4426950408889634
SCORE = HEAD_DIM ** (-0.5)
MB = 1024 * 1024

ROW_TILE = 256
FF_TILE = 768


def dot_nn(left, right):
    return lax.dot_general(
        left, right, (((1,), (0,)), ((), ())), preferred_element_type=F32
    )


def dot_nt(left, right):
    return lax.dot_general(
        left, right, (((1,), (1,)), ((), ())), preferred_element_type=F32
    )


def dot_tn(left, right):
    return lax.dot_general(
        left, right, (((0,), (0,)), ((), ())), preferred_element_type=F32
    )


def attention_forward_kernel(q_ref, k_ref, v_ref, att_ref, lse_ref):
    query = q_ref[...]
    keys = k_ref[...]
    values_t = v_ref[...].T
    lane = lax.broadcasted_iota(jnp.int32, query.shape, 1)
    outs = []
    for half in range(2):
        mine = (lane < HEAD_DIM) if half == 0 else (lane >= HEAD_DIM)
        picked = jnp.where(mine, query, jnp.zeros_like(query))
        scores = dot_nt(keys, picked)
        highest = jnp.max(scores, 0, keepdims=True)
        expo = jnp.exp2((scores - highest) * (SCORE * LOG2E))
        total = jnp.sum(expo, 0, keepdims=True)
        part = values_t[half * HEAD_DIM : (half + 1) * HEAD_DIM, :]
        outs.append(dot_nn(part, expo.astype(BF)) / total)
        lse_ref[0, half : half + 1, :] = highest * (SCORE * LOG2E) + jnp.log2(total)
    att_ref[...] = jnp.concatenate(outs, 0).T.astype(BF)


def attention_forward(projected):
    rows = projected.shape[0]
    seqs = rows // LENGTH
    pairs = HEADS // 2
    block = (LENGTH, 2 * HEAD_DIM)
    return pl.pallas_call(
        attention_forward_kernel,
        grid=(seqs, pairs),
        in_specs=[
            pl.BlockSpec(block, lambda s, h: (s, h)),
            pl.BlockSpec(block, lambda s, h: (s, pairs + h)),
            pl.BlockSpec(block, lambda s, h: (s, 2 * pairs + h)),
        ],
        out_specs=[
            pl.BlockSpec(block, lambda s, h: (s, h)),
            pl.BlockSpec((1, 2, LENGTH), lambda s, h: (s * pairs + h, 0, 0)),
        ],
        out_shape=[
            jax.ShapeDtypeStruct((rows, D), BF),
            jax.ShapeDtypeStruct((seqs * pairs, 2, LENGTH), F32),
        ],
        compiler_params=pltpu.CompilerParams(vmem_limit_bytes=48 * MB),
        name="attention_forward",
    )(projected, projected, projected)


def gelu_parts(values):
    size = jnp.abs(values)
    frac = 1.0 / (1.0 + (0.3275911 * 0.7071067811865476) * size)
    expo = jnp.exp2(values * values * (-0.5 * LOG2E))
    poly = 1.061405429 * 0.5
    for coef in (-1.453152027, 1.421413741, -0.284496736, 0.254829592):
        poly = poly * frac + 0.5 * coef
    tail = poly * frac * expo
    cdf = jnp.where(values >= 0, 1.0 - tail, tail)
    return values * cdf, cdf + values * expo * 0.3989422804014327


def norm_parts(total):
    centre = jnp.mean(total, -1, keepdims=True)
    centered = total - centre
    variance = jnp.mean(centered * centered, -1, keepdims=True)
    scale = lax.rsqrt(variance + norm_eps)
    return centered * scale, scale


def norm_back(scaled, unit, scale):
    return scale * (
        scaled
        - jnp.mean(scaled, -1, keepdims=True)
        - unit * jnp.mean(scaled * unit, -1, keepdims=True)
    )


def middle_kernel(
    att_ref,
    x_ref,
    go_ref,
    mask_ref,
    wout_ref,
    wup_ref,
    wdown_ref,
    vec_ref,
    bup_ref,
    out_ref,
    normed_ref,
    hidden_ref,
    gmid_ref,
    gup_ref,
    gfirst_ref,
    gfirstb_ref,
    gatt_ref,
    sums_ref,
    slope_ref,
):
    @pl.when(pl.program_id(0) == 0)
    def _():
        sums_ref[...] = jnp.zeros_like(sums_ref)

    bias_out = vec_ref[0:1, :]
    gain_one = vec_ref[1:2, :]
    shift_one = vec_ref[2:3, :]
    bias_down = vec_ref[3:4, :]
    gain_two = vec_ref[4:5, :]
    shift_two = vec_ref[5:6, :]

    def note(row, values):
        sums_ref[row : row + 1, 0:D] += jnp.sum(values, 0, keepdims=True)

    branch = dot_nt(att_ref[...], wout_ref[...]) + bias_out
    unit_one, scale_one = norm_parts(x_ref[...] + branch)
    normed = unit_one * gain_one + shift_one
    normed_b = normed.astype(BF)
    normed_ref[...] = normed_b
    downward = jnp.zeros(normed.shape, F32)
    for start in range(0, FF, FF_TILE):
        cols = slice(start, start + FF_TILE)
        upward = dot_nt(normed_b, wup_ref[cols, :]) + bup_ref[0:1, cols]
        hidden, slope = gelu_parts(upward)
        slope_ref[:, cols] = slope
        hidden_b = hidden.astype(BF)
        hidden_ref[:, cols] = hidden_b
        downward += dot_nn(hidden_b, wdown_ref[cols, :])
    unit_two, scale_two = norm_parts(normed + downward + bias_down)
    out_ref[...] = (unit_two * gain_two + shift_two).astype(BF)
    g_out = go_ref[...].astype(F32) * mask_ref[...].astype(F32)
    note(5, g_out * unit_two)
    note(6, g_out)
    g_mid = norm_back(g_out * gain_two, unit_two, scale_two)
    note(4, g_mid)
    g_mid_b = g_mid.astype(BF)
    gmid_ref[...] = g_mid_b
    g_normed = g_mid
    for start in range(0, FF, FF_TILE):
        cols = slice(start, start + FF_TILE)
        g_up = dot_nt(g_mid_b, wdown_ref[cols, :]) * slope_ref[:, cols]
        sums_ref[0:1, cols] += jnp.sum(g_up, 0, keepdims=True)
        g_up_b = g_up.astype(BF)
        gup_ref[:, cols] = g_up_b
        g_normed += dot_nn(g_up_b, wup_ref[cols, :])
    note(2, g_normed * unit_one)
    note(3, g_normed)
    g_first = norm_back(g_normed * gain_one, unit_one, scale_one)
    note(1, g_first)
    gfirst_ref[...] = g_first
    g_first_b = g_first.astype(BF)
    gfirstb_ref[...] = g_first_b
    gatt_ref[...] = dot_nn(g_first_b, wout_ref[...]).astype(BF)


def middle(attended, inputs, out_grad, masked, mats_t, vecs, bias_up):
    rows = attended.shape[0]
    tile = ROW_TILE

    def row(width):
        return pl.BlockSpec((tile, width), lambda i: (i, 0))

    def whole(shape, place=0):
        return pl.BlockSpec(
            shape, lambda i: (place, 0), pipeline_mode=pl.Buffered(buffer_count=1)
        )

    return pl.pallas_call(
        middle_kernel,
        grid=(rows // tile,),
        in_specs=[
            row(D),
            row(D),
            row(D),
            row(1),
            whole((D, D), 3),
            whole((FF, D), 1),
            whole((FF, D), 2),
            whole((8, D)),
            whole((1, FF)),
        ],
        out_specs=[
            row(D),
            row(D),
            row(FF),
            row(D),
            row(FF),
            row(D),
            row(D),
            row(D),
            pl.BlockSpec((8, FF), lambda i: (0, 0)),
        ],
        out_shape=[
            jax.ShapeDtypeStruct((rows, D), BF),
            jax.ShapeDtypeStruct((rows, D), BF),
            jax.ShapeDtypeStruct((rows, FF), BF),
            jax.ShapeDtypeStruct((rows, D), BF),
            jax.ShapeDtypeStruct((rows, FF), BF),
            jax.ShapeDtypeStruct((rows, D), F32),
            jax.ShapeDtypeStruct((rows, D), BF),
            jax.ShapeDtypeStruct((rows, D), BF),
            jax.ShapeDtypeStruct((8, FF), F32),
        ],
        scratch_shapes=[pltpu.VMEM((tile, FF), F32)],
        compiler_params=pltpu.CompilerParams(vmem_limit_bytes=56 * MB),
        name="middle",
    )(attended, inputs, out_grad, masked, mats_t, mats_t, mats_t, vecs, bias_up)


def entry_kernel(
    key_ref, found_ref, extra_ref, place_ref, w_ref, bias_ref, x_ref, xb_ref, proj_ref
):
    slots = lax.broadcasted_iota(jnp.int32, (LENGTH, found_ref.shape[0]), 1)
    picked = (key_ref[...] == slots).astype(BF)
    inputs = dot_nn(picked, found_ref[...]) + extra_ref[...].astype(F32)
    inputs = inputs + place_ref[...].astype(F32)
    x_ref[...] = inputs
    inputs_b = inputs.astype(BF)
    xb_ref[...] = inputs_b
    for start in range(0, QKV, D):
        cols = slice(start, start + D)
        part = dot_nt(inputs_b, w_ref[cols, :]) + bias_ref[:, cols]
        proj_ref[:, cols] = part.astype(BF)


def fixed(shape, place=0):
    return pl.BlockSpec(
        shape, lambda i: (place, 0), pipeline_mode=pl.Buffered(buffer_count=1)
    )


def entry(key, found, extra, places, mats_t, bias):
    rows = key.shape[0]
    slots = found.shape[0]

    def row(width):
        return pl.BlockSpec((LENGTH, width), lambda i: (i, 0))

    return pl.pallas_call(
        entry_kernel,
        grid=(rows // LENGTH,),
        in_specs=[
            row(1),
            fixed((slots, D)),
            row(D),
            fixed((LENGTH, D)),
            fixed((QKV, D)),
            fixed((1, QKV)),
        ],
        out_specs=[row(D), row(D), row(QKV)],
        out_shape=[
            jax.ShapeDtypeStruct((rows, D), F32),
            jax.ShapeDtypeStruct((rows, D), BF),
            jax.ShapeDtypeStruct((rows, QKV), BF),
        ],
        compiler_params=pltpu.CompilerParams(vmem_limit_bytes=56 * MB),
        cost_estimate=pl.CostEstimate(
            flops=13_000_000_000, bytes_accessed=40_000_000, transcendentals=0
        ),
        name="entry",
    )(key[:, None], found, extra, places, mats_t, bias)


def rest_kernel(first_ref, att_ref, up_ref, normed_ref, hidden_ref, mid_ref, out_ref):
    step = pl.program_id(0)
    chunks = FF // D

    @pl.when(step == 0)
    def _():
        out_ref[...] = dot_tn(first_ref[...], att_ref[...]).astype(BF)

    @pl.when(jnp.logical_and(step > 0, step <= chunks))
    def _():
        out_ref[...] = dot_tn(up_ref[...], normed_ref[...]).astype(BF)

    @pl.when(step > chunks)
    def _():
        out_ref[...] = dot_tn(hidden_ref[...], mid_ref[...]).astype(BF)


def rest_gradients(g_first_b, attended, g_up_b, normed_b, hidden_b, g_mid_b):
    rows = attended.shape[0]
    chunks = FF // D
    full = fixed((rows, D))
    return pl.pallas_call(
        rest_kernel,
        grid=(1 + 2 * chunks,),
        in_specs=[
            full,
            full,
            pl.BlockSpec((rows, D), lambda i: (0, jnp.clip(i - 1, 0, chunks - 1))),
            full,
            pl.BlockSpec((rows, D), lambda i: (0, jnp.clip(i - 1 - chunks, 0, chunks - 1))),
            full,
        ],
        out_specs=pl.BlockSpec((D, D), lambda i: (i, 0)),
        out_shape=jax.ShapeDtypeStruct((D + 2 * FF, D), BF),
        compiler_params=pltpu.CompilerParams(vmem_limit_bytes=56 * MB),
        cost_estimate=pl.CostEstimate(
            flops=22_000_000_000, bytes_accessed=50_000_000, transcendentals=0
        ),
        name="rest_gradients",
    )(g_first_b, attended, g_up_b, normed_b, hidden_b, g_mid_b)


MESH = pl.DeviceIdType.MESH
PLANES = 4


def neighbours():
    me = lax.axis_index("fsdp")
    core = lax.rem(me, 2)
    x = lax.rem(me // 2, 2)
    y = lax.rem(me // 4, 2)
    z = me // 8
    step_a = 4 - 2 * core
    step_b = 2 + 2 * core
    a = jnp.where(core == 0, y, x)
    b = jnp.where(core == 0, x, y)
    near_a = me + step_a * (1 - 2 * a)
    near_b = me + step_b * (1 - 2 * b)
    twin = me + 1 - 2 * core
    return me, core, z, a, b, step_a, step_b, near_a, near_b, twin


def greet(me, z, near_a, near_b, twin):
    barrier = pltpu.get_barrier_semaphore()

    def hello(device):
        pl.semaphore_signal(barrier, inc=1, device_id=(device,), device_id_type=MESH)

    for device in (near_a, near_b, twin):
        hello(device)

    @pl.when(z > 0)
    def _():
        hello(me - 8)

    @pl.when(z < PLANES - 1)
    def _():
        hello(me + 8)

    inner = jnp.logical_and(z > 0, z < PLANES - 1)
    pl.semaphore_wait(barrier, jnp.where(inner, 5, 4))


class RestSums:
    TURNS = PLANES - 1

    def __init__(self, in_ref, out_ref, scratch):
        self.in_ref, self.out_ref = in_ref, out_ref
        (
            self.own,
            self.from_twin,
            self.from_b,
            self.from_a,
            self.from_low,
            self.from_high,
            self.load_sem,
            self.twin_sem,
            self.b_sem,
            self.a_sem,
            self.low_sem,
            self.high_sem,
        ) = scratch
        self.place = neighbours()

    @staticmethod
    def scratch(shape):
        return [
            pltpu.VMEM((12,) + shape, BF),
            pltpu.VMEM((12,) + shape, BF),
            pltpu.VMEM((6,) + shape, BF),
            pltpu.VMEM((3,) + shape, BF),
            pltpu.VMEM((4,) + shape, BF),
            pltpu.VMEM((4,) + shape, BF),
            pltpu.SemaphoreType.DMA((12,)),
            pltpu.SemaphoreType.DMA((2, 12)),
            pltpu.SemaphoreType.DMA((2, 6)),
            pltpu.SemaphoreType.DMA((2, 3)),
            pltpu.SemaphoreType.DMA((2, 4)),
            pltpu.SemaphoreType.DMA((2, 4)),
        ]

    def remote(self, source, target, sems, slot, device):
        return pltpu.make_async_remote_copy(
            src_ref=source,
            dst_ref=target.at[slot],
            send_sem=sems.at[0, slot],
            recv_sem=sems.at[1, slot],
            device_id=(device,),
            device_id_type=MESH,
        )

    def plane_of(self, turn):
        z = self.place[2]
        last = PLANES - 1 - turn
        inner = (1, 3, 2)[turn]
        return jnp.where(z < 2, last, jnp.where(z == 2, inner, 1 + turn))

    def shards(self, slot):
        me, core, z, a, b, step_a, step_b, near_a, near_b, twin = self.place
        other_b, turn, other_a = slot < 6, slot % 6 // 2, slot % 2 == 0
        base = (self.plane_of(turn) - 1) * 8
        a_at = 1 - a if other_a else a
        b_at = 1 - b if other_b else b
        mine = base + a_at * step_a + b_at * step_b + core
        a_at = 1 - b if other_a else b
        b_at = 1 - a if other_b else a
        twins = base + a_at * step_b + b_at * step_a + 1 - core
        return mine, twins

    def load(self, slot):
        return pltpu.make_async_copy(
            self.in_ref.at[self.shards(slot)[0]], self.own.at[slot], self.load_sem.at[slot]
        )

    def gift(self, slot):
        return self.remote(
            self.in_ref.at[self.shards(slot)[1]],
            self.from_twin,
            self.twin_sem,
            slot,
            self.place[9],
        )

    def over_b(self, slot):
        return self.remote(self.own.at[slot], self.from_b, self.b_sem, slot, self.place[8])

    def over_a(self, turn):
        return self.remote(
            self.own.at[6 + 2 * turn], self.from_a, self.a_sem, turn, self.place[7]
        )

    def along(self, turn, up):
        plane = self.plane_of(turn)
        source = self.own.at[7 + 2 * turn]
        if up:
            return self.remote(source, self.from_low, self.low_sem, plane, self.place[0] + 8)
        return self.remote(source, self.from_high, self.high_sem, plane, self.place[0] - 8)

    def add(self, slot, arrived):
        self.own[slot] = (self.own[slot].astype(F32) + arrived[...].astype(F32)).astype(BF)

    def start(self):
        me, core, z, a, b, step_a, step_b, near_a, near_b, twin = self.place
        greet(me, z, near_a, near_b, twin)
        for slot in (0, 1, 2, 3, 6, 7, 4, 5, 8, 9, 10, 11):
            self.gift(slot).start()
            self.load(slot).start()

    def far(self, turn):
        for slot in (2 * turn, 2 * turn + 1):
            self.load(slot).wait()
            self.gift(slot).wait_recv()
            self.add(slot, self.from_twin.at[slot])
            self.over_b(slot).start()

    def near(self, turn):
        for slot in (6 + 2 * turn, 7 + 2 * turn):
            self.load(slot).wait()
            self.gift(slot).wait_recv()
            self.add(slot, self.from_twin.at[slot])

    def stage_b(self, turn):
        for slot in (2 * turn, 2 * turn + 1):
            self.over_b(slot).wait_recv()
            self.add(6 + slot, self.from_b.at[slot])
        self.over_a(turn).start()

    def stage_a(self, turn):
        z = self.place[2]
        slot = 7 + 2 * turn
        plane = self.plane_of(turn)
        self.over_a(turn).wait_recv()
        self.add(slot, self.from_a.at[turn])

        @pl.when(jnp.logical_and(plane > z, z > 0))
        def _():
            self.along(turn, True).wait_recv()
            self.add(slot, self.from_low.at[plane])

        @pl.when(plane > z)
        def _():
            self.along(turn, True).start()

        @pl.when(jnp.logical_and(plane < z, z < PLANES - 1))
        def _():
            self.along(turn, False).wait_recv()
            self.add(slot, self.from_high.at[plane])

        @pl.when(plane < z)
        def _():
            self.along(turn, False).start()

        @pl.when(plane == z)
        def _():
            self.along(turn, True).wait_recv()
            self.out_ref[...] = self.own[slot].astype(F32) + self.from_low[plane].astype(F32)

        @pl.when(jnp.logical_and(plane == z, z < PLANES - 1))
        def _():
            self.along(turn, False).wait_recv()
            self.out_ref[...] += self.from_high[plane].astype(F32)

    def end(self):
        z = self.place[2]
        for slot in range(12):
            self.gift(slot).wait_send()
        for slot in range(6):
            self.over_b(slot).wait_send()
        for turn in range(self.TURNS):
            self.over_a(turn).wait_send()
            plane = self.plane_of(turn)

            @pl.when(plane > z)
            def _(turn=turn):
                self.along(turn, True).wait_send()

            @pl.when(plane < z)
            def _(turn=turn):
                self.along(turn, False).wait_send()

    def schedule(self):
        return {
            0: [self.start],
            1: [lambda: self.far(0)],
            2: [lambda: self.far(1)],
            3: [lambda: self.near(0)],
            4: [lambda: self.far(2)],
            5: [lambda: self.near(1)],
            6: [lambda: self.near(2)],
            7: [lambda: self.stage_b(0)],
            11: [lambda: self.stage_b(1)],
            13: [lambda: self.stage_a(0)],
            16: [lambda: self.stage_b(2)],
            19: [lambda: self.stage_a(1)],
            24: [lambda: self.stage_a(2)],
            27: [self.end],
        }


PIECES = 4


def share_places_kernel(split, table_ref, out_ref, stage, load_sem, send_sem, recv_sem):
    first_owner, first_row, count = split
    me, core, z, a, b, step_a, step_b, near_a, near_b, twin = neighbours()
    greet(me, z, near_a, near_b, twin)
    rows = LENGTH // PIECES
    root = first_owner + 1
    gift = pltpu.make_async_remote_copy(
        src_ref=table_ref.at[pl.ds(first_row, count)],
        dst_ref=stage.at[pl.ds(0, count)],
        send_sem=load_sem.at[0],
        recv_sem=load_sem.at[1],
        device_id=(root,),
        device_id_type=MESH,
    )
    mine = pltpu.make_async_copy(
        table_ref.at[pl.ds(0, LENGTH - count)],
        stage.at[pl.ds(count, LENGTH - count)],
        load_sem.at[2],
    )

    @pl.when(me == first_owner)
    def _():
        gift.start()

    @pl.when(me == root)
    def _():
        mine.start()
        mine.wait()
        gift.wait_recv()

    def copy(piece, device, kind):
        part = pl.ds(piece * rows, rows)
        return pltpu.make_async_remote_copy(
            src_ref=out_ref.at[part],
            dst_ref=out_ref.at[part],
            send_sem=send_sem.at[kind, piece],
            recv_sem=recv_sem.at[piece],
            device_id=(device,),
            device_id_type=MESH,
        )

    trunk = jnp.logical_and(core == 1, jnp.logical_and(a == 1, b == 1))
    branch = jnp.logical_and(core == 1, jnp.logical_and(a == 0, b == 1))
    routes = (
        (jnp.logical_and(trunk, z > 0), me - 8),
        (trunk, near_a),
        (jnp.logical_or(trunk, branch), near_b),
        (core == 1, twin),
    )
    for piece in range(PIECES):
        part = slice(piece * rows, (piece + 1) * rows)

        @pl.when(me == root)
        def _(part=part):
            out_ref[part, :] = stage[part, :].astype(BF)

        @pl.when(me != root)
        def _(piece=piece):
            copy(piece, twin, 3).wait_recv()

        for kind, (goes, device) in enumerate(routes):

            @pl.when(goes)
            def _(piece=piece, device=device, kind=kind):
                copy(piece, device, kind).start()

    for piece in range(PIECES):
        for kind, (goes, device) in enumerate(routes):

            @pl.when(goes)
            def _(piece=piece, device=device, kind=kind):
                copy(piece, device, kind).wait_send()

    @pl.when(me == first_owner)
    def _():
        gift.wait_send()


def place_split(devices, owned):
    first_owner = VOCAB // owned
    first_row = VOCAB - first_owner * owned
    return first_owner, first_row, owned - first_row


def share_places(table, split, ident):
    return pl.pallas_call(
        functools.partial(share_places_kernel, split),
        in_specs=[pl.BlockSpec(memory_space=pl.ANY)],
        out_specs=pl.BlockSpec(memory_space=pltpu.VMEM),
        out_shape=jax.ShapeDtypeStruct((LENGTH, D), BF),
        scratch_shapes=[
            pltpu.VMEM((LENGTH, D), F32),
            pltpu.SemaphoreType.DMA((3,)),
            pltpu.SemaphoreType.DMA((4, PIECES)),
            pltpu.SemaphoreType.DMA((PIECES,)),
        ],
        compiler_params=pltpu.CompilerParams(collective_id=ident, has_side_effects=True),
        cost_estimate=pl.CostEstimate(flops=0, bytes_accessed=60_000_000, transcendentals=0),
        name="share_places",
    )(table)


CHUNKS = 3


def homecoming_kernel(
    split,
    place_ref,
    first_ref,
    out_ref,
    mats_ref,
    sums,
    from_twin,
    from_b,
    from_a,
    from_z,
    ready,
    own,
    own_twin,
    own_b,
    own_a,
    own_high,
    sems,
    z_sem,
    piece_sem,
    home_sem,
    load_sem,
    twin_sem,
    b_sem,
    a_sem,
    high_sem,
):
    first_owner, first_row, count = split
    root = first_owner + 1
    me, core, z, a, b, step_a, step_b, near_a, near_b, twin = neighbours()
    rows = place_ref.shape[4]
    height = first_ref.shape[1] // CHUNKS
    out_ref[...] = jnp.zeros_like(out_ref)
    barrier = pltpu.get_barrier_semaphore()

    def each(step, carry):
        pl.semaphore_signal(
            barrier, inc=1, device_id=(lax.rem(me + step, 32),), device_id_type=MESH
        )
        return carry

    lax.fori_loop(1, 32, each, 0)
    pl.semaphore_wait(barrier, 31)

    def remote(source, target, send, receive, device):
        return pltpu.make_async_remote_copy(
            src_ref=source,
            dst_ref=target,
            send_sem=send,
            recv_sem=receive,
            device_id=(device,),
            device_id_type=MESH,
        )

    def add(total, extra):
        return (total.astype(F32) + extra.astype(F32)).astype(BF)

    x = jnp.where(core == 0, b, a)
    y = jnp.where(core == 0, a, b)
    gift = remote(place_ref.at[:, :, :, 1 - core], from_twin, sems.at[0, 0], sems.at[0, 1], twin)
    gift.start()
    loads, gifts = [], []
    for slot in range(4):
        other_b, other_a = slot < 2, slot % 2 == 0
        a_at, b_at = (1 - a if other_a else a), (1 - b if other_b else b)
        shard = a_at * step_a + b_at * step_b + core
        loads.append(pltpu.make_async_copy(first_ref.at[shard], own.at[slot], load_sem.at[slot]))
        a_at, b_at = (1 - b if other_a else b), (1 - a if other_b else a)
        shard = a_at * step_b + b_at * step_a + 1 - core
        gifts.append(
            remote(
                first_ref.at[shard],
                own_twin.at[slot],
                twin_sem.at[0, slot],
                twin_sem.at[1, slot],
                twin,
            )
        )
    for slot in range(4):
        gifts[slot].start()
        loads[slot].start()
    gift.wait_recv()
    sums[...] = add(place_ref[:, :, :, core], from_twin[...])

    @pl.when(core == 0)
    def _():
        remote(sums.at[:, :, 1 - x], from_b, sems.at[1, 0], sems.at[1, 1], near_b).start()

    @pl.when(core == 1)
    def _():
        remote(sums.at[:, 1 - y], from_b, sems.at[1, 0], sems.at[1, 1], near_b).start()

    over_b = [
        remote(own.at[slot], own_b.at[slot], b_sem.at[0, slot], b_sem.at[1, slot], near_b)
        for slot in range(2)
    ]
    for slot in range(4):
        loads[slot].wait()
        gifts[slot].wait_recv()
        own[slot] = add(own[slot], own_twin[slot])
        if slot < 2:
            over_b[slot].start()

    small_b = remote(sums.at[:, 0], from_b, sems.at[1, 0], sems.at[1, 1], near_b)
    small_b.wait_recv()

    @pl.when(core == 0)
    def _():
        from_b[...] = add(sums[:, :, x], from_b[...])

    @pl.when(core == 1)
    def _():
        from_b[...] = add(sums[:, y], from_b[...])

    small_a = remote(from_b.at[:, 1 - a], from_a, sems.at[2, 0], sems.at[2, 1], near_a)
    small_a.start()
    over_a = remote(own.at[2], own_a, a_sem.at[0], a_sem.at[1], near_a)
    for slot in range(2):
        over_b[slot].wait_recv()
        own[2 + slot] = add(own[2 + slot], own_b[slot])
        if slot == 0:
            over_a.start()
    small_a.wait_recv()
    from_a[...] = add(from_b[:, a], from_a[...])

    def column(plane, action):
        @pl.when(plane != z)
        def _():
            action(
                remote(
                    from_a.at[plane],
                    from_z.at[z],
                    z_sem.at[0, plane],
                    z_sem.at[1, z],
                    me + 8 * (plane - z),
                )
            )

    for plane in range(PLANES):
        column(plane, lambda item: item.start())
    over_a.wait_recv()

    def down(chunk):
        part = pl.ds(chunk * height, height)
        return remote(
            own.at[3, part],
            own_high.at[part],
            high_sem.at[0, chunk],
            high_sem.at[1, chunk],
            me - 8,
        )

    for chunk in range(CHUNKS):
        part = pl.ds(chunk * height, height)
        own[3, part] = add(own[3, part], own_a[part])

        @pl.when(z < PLANES - 1)
        def _(chunk=chunk, part=part):
            down(chunk).wait_recv()
            own[3, part] = add(own[3, part], own_high[part])

        @pl.when(z > 0)
        def _(chunk=chunk):
            down(chunk).start()

    mats_ref[...] = own[3].astype(F32)
    ready[...] = from_a[z].astype(F32)
    for plane in range(PLANES):

        @pl.when(plane != z)
        def _(plane=plane):
            remote(
                from_a.at[plane], from_z.at[plane], z_sem.at[0, plane], z_sem.at[1, plane], twin
            ).wait_recv()
            ready[...] += from_z[plane].astype(F32)

    def home(device, half):
        place = device * rows + half * 8
        early = place < count
        owner = jnp.where(early, first_owner, root)
        spot = pl.multiple_of(jnp.where(early, first_row + place, place - count), 8)
        return owner, spot

    def piece(device, half):
        owner, spot = home(device, half)
        return remote(
            ready.at[pl.ds(half * 8, 8)],
            out_ref.at[pl.ds(spot, 8)],
            piece_sem.at[half],
            home_sem.at[device * 2 + half],
            owner,
        )

    for half in range(2):
        owner, spot = home(me, half)

        @pl.when(owner == me)
        def _(half=half, spot=spot):
            out_ref[pl.ds(spot, 8), :] = ready[half * 8 : half * 8 + 8, :]

        @pl.when(owner != me)
        def _(half=half):
            piece(me, half).start()

    def arrive(index, carry):
        device, half = index // 2, lax.rem(index, 2)
        owner, _ = home(device, half)

        @pl.when(jnp.logical_and(owner == me, device != me))
        def _():
            piece(device, half).wait_recv()

        return carry

    @pl.when(me >= first_owner)
    def _():
        lax.fori_loop(0, 64, arrive, 0)

    for half in range(2):
        owner, _ = home(me, half)

        @pl.when(owner != me)
        def _(half=half):
            piece(me, half).wait_send()

    for item in [gift, small_b, small_a, over_a] + gifts + over_b:
        item.wait_send()
    for plane in range(PLANES):
        column(plane, lambda item: item.wait_send())
    for chunk in range(CHUNKS):

        @pl.when(z > 0)
        def _(chunk=chunk):
            down(chunk).wait_send()


def homecoming(place_sums, first, owned, split, ident):
    rows = LENGTH // 32
    small = (rows, D)
    shape = first.shape[1:]
    return pl.pallas_call(
        functools.partial(homecoming_kernel, split),
        in_specs=[
            pl.BlockSpec(memory_space=pltpu.VMEM),
            pl.BlockSpec(memory_space=pl.ANY),
        ],
        out_specs=[pl.BlockSpec(memory_space=pltpu.VMEM)] * 2,
        out_shape=[
            jax.ShapeDtypeStruct((owned, D), F32),
            jax.ShapeDtypeStruct(shape, F32),
        ],
        scratch_shapes=[
            pltpu.VMEM((4, 2, 2) + small, BF),
            pltpu.VMEM((4, 2, 2) + small, BF),
            pltpu.VMEM((4, 2) + small, BF),
            pltpu.VMEM((4,) + small, BF),
            pltpu.VMEM((4,) + small, BF),
            pltpu.VMEM(small, F32),
            pltpu.VMEM((4,) + shape, BF),
            pltpu.VMEM((4,) + shape, BF),
            pltpu.VMEM((2,) + shape, BF),
            pltpu.VMEM(shape, BF),
            pltpu.VMEM(shape, BF),
            pltpu.SemaphoreType.DMA((3, 2)),
            pltpu.SemaphoreType.DMA((2, 4)),
            pltpu.SemaphoreType.DMA((2,)),
            pltpu.SemaphoreType.DMA((64,)),
            pltpu.SemaphoreType.DMA((4,)),
            pltpu.SemaphoreType.DMA((2, 4)),
            pltpu.SemaphoreType.DMA((2, 2)),
            pltpu.SemaphoreType.DMA((2,)),
            pltpu.SemaphoreType.DMA((2, CHUNKS)),
        ],
        compiler_params=pltpu.CompilerParams(
            collective_id=ident, has_side_effects=True, vmem_limit_bytes=40 * MB
        ),
        cost_estimate=pl.CostEstimate(
            flops=0, bytes_accessed=200_000_000, transcendentals=0
        ),
        name="homecoming",
    )(place_sums.reshape((4, 2, 2, 2) + small), first)


def backward_kernel(
    by_kernel,
    q_ref,
    k_ref,
    v_ref,
    att_ref,
    g_ref,
    lse_ref,
    first_ref,
    xb_ref,
    w_ref,
    rest_ref,
    grad_ref,
    place_ref,
    weights_ref,
    bias_ref,
    mats_ref,
    proj,
    total,
    places,
    *scratch,
):
    seq, head = pl.program_id(0), pl.program_id(1)
    pairs = HEADS // 2
    step = seq * (pairs + 1) + head

    @pl.when(step == 0)
    def _():
        total[...] = jnp.zeros_like(total)
        places[...] = jnp.zeros_like(places)
        bias_ref[...] = jnp.zeros_like(bias_ref)
        mats_ref[...] = jnp.zeros_like(mats_ref)

    if by_kernel:
        sums = RestSums(rest_ref, mats_ref, scratch)
        for when, actions in sums.schedule().items():

            @pl.when(step == when)
            def _(actions=actions):
                for action in actions:
                    action()

    @pl.when(head < pairs)
    def _():
        cols = pl.ds(pl.multiple_of(head * 2 * HEAD_DIM, 2 * HEAD_DIM), 2 * HEAD_DIM)
        query = q_ref[...]
        keys = k_ref[...]
        values = v_ref[...]
        grad = g_ref[...]
        lane = lax.broadcasted_iota(jnp.int32, query.shape, 1)
        first = lane < HEAD_DIM
        product = (att_ref[...].astype(F32) * grad.astype(F32)).T
        zero = jnp.zeros_like(query)
        g_q, g_k, g_v = [], [], []
        for half in range(2):
            mine = first if half == 0 else jnp.logical_not(first)
            scores = dot_nt(keys, jnp.where(mine, query, zero))
            probs = jnp.exp2(scores * (SCORE * LOG2E) - lse_ref[0, half : half + 1, :])
            delta = jnp.sum(
                product[half * HEAD_DIM : (half + 1) * HEAD_DIM, :], 0, keepdims=True
            )
            g_probs = dot_nt(values, jnp.where(mine, grad, zero))
            g_v.append(dot_nn(probs.astype(BF), grad))
            g_scores = (probs * (g_probs - delta)).astype(BF)
            g_k.append(dot_nn(g_scores, query))
            g_q.append(dot_tn(g_scores, keys))
        grad_q = jnp.where(first, g_q[0], g_q[1]) * SCORE
        grad_k = jnp.where(first, g_k[0], g_k[1]) * SCORE
        grad_v = jnp.where(first, g_v[0], g_v[1])
        proj[0, :, cols] = grad_q.astype(BF)
        proj[1, :, cols] = grad_k.astype(BF)
        proj[2, :, cols] = grad_v.astype(BF)
        bias_ref[0:1, cols] += jnp.sum(grad_q, 0, keepdims=True)
        bias_ref[1:2, cols] += jnp.sum(grad_v, 0, keepdims=True)

    @pl.when(head == pairs)
    def _():
        g_in = first_ref[...]
        inputs_b = xb_ref[...]
        for part in range(3):
            cols = slice(part * D, (part + 1) * D)
            g_in = g_in + dot_nn(proj[part], w_ref[cols, :])
            total[cols, :] += dot_tn(proj[part], inputs_b)
        grad_ref[...] = g_in.astype(BF)
        places[...] += g_in

    @pl.when(step == pl.num_programs(0) * (pairs + 1) - 1)
    def _():
        weights_ref[...] = total[...].astype(BF)
        place_ref[...] = places[...].astype(BF)


def backward(by_kernel, projected, attended, grad_att, lse, g_first, inputs_b, mats_t, rest, ident):
    rows = projected.shape[0]
    seqs = rows // LENGTH
    pairs = HEADS // 2
    block = (LENGTH, 2 * HEAD_DIM)
    shape = rest.shape[1:]

    def pair(offset):
        return pl.BlockSpec(block, lambda s, h: (s, offset + jnp.minimum(h, pairs - 1)))

    def row(width):
        return pl.BlockSpec((LENGTH, width), lambda s, h: (s, 0))

    def steady(shape):
        return pl.BlockSpec(
            shape, lambda s, h: (0, 0), pipeline_mode=pl.Buffered(buffer_count=1)
        )

    def kept(shape):
        return pl.BlockSpec(shape, lambda s, h: (0, 0))

    return pl.pallas_call(
        functools.partial(backward_kernel, by_kernel),
        grid=(seqs, pairs + 1),
        in_specs=[
            pair(0),
            pair(pairs),
            pair(2 * pairs),
            pair(0),
            pair(0),
            pl.BlockSpec(
                (1, 2, LENGTH), lambda s, h: (s * pairs + jnp.minimum(h, pairs - 1), 0, 0)
            ),
            row(D),
            row(D),
            steady((QKV, D)),
            pl.BlockSpec(memory_space=pl.ANY),
        ],
        out_specs=[
            row(D),
            kept((LENGTH, D)),
            kept((QKV, D)),
            kept((8, D)),
            kept(shape),
        ],
        out_shape=[
            jax.ShapeDtypeStruct((rows, D), BF),
            jax.ShapeDtypeStruct((LENGTH, D), BF),
            jax.ShapeDtypeStruct((QKV, D), BF),
            jax.ShapeDtypeStruct((8, D), F32),
            jax.ShapeDtypeStruct(shape, F32),
        ],
        scratch_shapes=[
            pltpu.VMEM((3, LENGTH, D), BF),
            pltpu.VMEM((QKV, D), F32),
            pltpu.VMEM((LENGTH, D), F32),
        ]
        + (RestSums.scratch(shape) if by_kernel else []),
        compiler_params=pltpu.CompilerParams(
            vmem_limit_bytes=60 * MB,
            **(dict(collective_id=ident, has_side_effects=True) if by_kernel else {}),
        ),
        cost_estimate=pl.CostEstimate(
            flops=60_000_000_000, bytes_accessed=60_000_000, transcendentals=0
        ),
        name="backward",
    )(
        projected,
        projected,
        projected,
        attended,
        grad_att,
        lse,
        g_first,
        inputs_b,
        mats_t,
        rest,
    )


def slots_of(ids, owned):
    count = ids.shape[0]
    order = jnp.arange(count, dtype=jnp.int32)
    repeated = jnp.any(
        (ids[:, None] == ids[None, :]) & (order[:, None] < order[None, :]), axis=0
    )
    first = jnp.logical_not(repeated)
    base = (ids // owned) * owned
    below = (
        first[:, None]
        & (ids[:, None] >= base[None, :])
        & (ids[:, None] < ids[None, :])
    )
    return jnp.sum(below.astype(jnp.int32), axis=0)


def requests_of(ids, owner, slot, owned, devices, start, room):
    key = jnp.where((slot >= start) & (slot < start + room), owner * room + slot - start, -1)
    spots = jnp.arange(devices * room, dtype=jnp.int32)
    asked = jnp.max(
        jnp.where(key[:, None] == spots[None, :], (ids - owner * owned)[:, None], -1), axis=0
    )
    return key, asked


def pick(index, amount):
    return (index[:, None] == jnp.arange(amount, dtype=jnp.int32)[None, :]).astype(BF)


def adam_direction(param, first, second, grad, corr_one, corr_two, decay):
    first_next = beta_one * first + (1.0 - beta_one) * grad
    second_next = beta_two * second + (1.0 - beta_two) * grad * grad
    update = first_next / corr_one / (jnp.sqrt(second_next / corr_two) + adam_eps)
    return (update + decay * param, first_next)


def body(
    devices,
    token_ids,
    masked,
    swap_kind,
    swap_ids,
    out_grad,
    embed_table,
    table_first,
    table_second,
    layer_mats,
    mats_first,
    mats_second,
    layer_vecs,
    vecs_first,
    vecs_second,
):
    axis = "fsdp"
    rows = token_ids.shape[0]
    owned = embed_table.shape[0]
    entries = layer_vecs.shape[0]
    columns = layer_mats.shape[1]
    me = lax.axis_index(axis)
    by_kernel = devices == 32
    split = place_split(devices, owned)
    replaced = jnp.where(swap_kind < 8, mask_token, jnp.where(swap_kind == 8, swap_ids, token_ids))
    chosen = jnp.where(masked == 1, replaced, token_ids)

    def swap(blocks):
        return lax.all_to_all(blocks, axis, 0, 0, tiled=True)

    mats_t = lax.all_gather(layer_mats.astype(BF).T, axis, axis=0, tiled=True)

    room = 16 * -(-1536 // (16 * devices))
    more = 16
    owner = chosen // owned
    slot = slots_of(chosen, owned)
    most = jnp.max(slot) + 1
    key, asked = requests_of(chosen, owner, slot, owned, devices, 0, room)
    table_b = embed_table.astype(BF)
    own_vecs = layer_vecs.astype(BF).astype(F32)
    notes = jnp.concatenate(
        [
            asked.reshape(devices, room).astype(F32),
            jnp.broadcast_to(own_vecs[None], (devices, entries)),
            jnp.broadcast_to(most.astype(F32), (devices, 1)),
        ],
        axis=1,
    )
    notes = swap(notes)
    wanted = notes[:, :room].astype(jnp.int32).reshape(-1)
    vecs = notes[:, room : room + entries].reshape(-1)
    longest = jnp.max(notes[:, room + entries]).astype(jnp.int32)
    found = dot_nn(pick(wanted, owned), table_b).astype(BF)
    found = swap(found.reshape(devices, room, D)).reshape(-1, D)
    if by_kernel:
        places = share_places(embed_table, split, 1)
    else:
        spots = VOCAB + jnp.arange(LENGTH, dtype=jnp.int32) - me * owned
        places = lax.psum(dot_nn(pick(spots, owned), table_b), axis).astype(BF)
    rounds = (longest - room + more - 1) // more

    def fetch_more(state):
        turn, extra = state
        key, asked = requests_of(chosen, owner, slot, owned, devices, room + turn * more, more)
        wanted = swap(asked.reshape(devices, more)).reshape(-1)
        found = dot_nn(pick(wanted, owned), table_b).astype(BF)
        found = swap(found.reshape(devices, more, D)).reshape(-1, D)
        return turn + 1, extra + dot_nn(pick(key, devices * more), found).astype(BF)

    _, extra = lax.while_loop(
        lambda state: state[0] < rounds, fetch_more, (jnp.int32(0), jnp.zeros((rows, D), BF))
    )

    bias_qkv = jnp.concatenate([vecs[:D], jnp.zeros((D,), F32), vecs[D : 2 * D]])[None]
    bias_up = vecs[5 * D : 5 * D + FF][None]
    small = jnp.concatenate(
        [vecs[2 * D : 5 * D], vecs[5 * D + FF :], jnp.zeros((2 * D,), F32)]
    ).reshape(8, D)

    inputs, inputs_b, projected = entry(key, found, extra, places, mats_t, bias_qkv)
    attended, lse = attention_forward(projected)
    (
        outputs,
        normed_b,
        hidden_b,
        g_mid_b,
        g_up_b,
        g_first,
        g_first_b,
        g_att_b,
        sums,
    ) = middle(attended, inputs, out_grad, masked[:, None], mats_t, small, bias_up)
    g_rest = rest_gradients(g_first_b, attended, g_up_b, normed_b, hidden_b, g_mid_b)
    input_grad, g_places, g_qkv, bias_sums, rest_grad = backward(
        by_kernel,
        projected,
        attended,
        g_att_b,
        lse,
        g_first,
        inputs_b,
        mats_t,
        g_rest.reshape(-1, columns, D),
        2,
    )

    sent = dot_tn(pick(key, devices * room), input_grad).astype(BF)
    g_vecs = jnp.concatenate(
        [
            bias_sums[0],
            bias_sums[1],
            sums[1, :D],
            sums[2, :D],
            sums[3, :D],
            sums[0],
            sums[4, :D],
            sums[5, :D],
            sums[6, :D],
        ]
    )
    vecs_grad = jnp.sum(swap(g_vecs.reshape(devices, entries)), axis=0)
    sent, g_places, g_qkv = lax.optimization_barrier((sent, g_places, g_qkv))
    sent = swap(sent.reshape(devices, room, D)).reshape(-1, D)
    if by_kernel:
        g_own_places, first_grad = homecoming(
            g_places, g_qkv.reshape(-1, columns, D), owned, split, 3
        )
        mats_grad = jnp.where(me < QKV // columns, first_grad, rest_grad).T
    else:
        total = lax.psum(g_places.astype(F32), axis)
        spots = me * owned + jnp.arange(owned, dtype=jnp.int32) - VOCAB
        inside = (spots >= 0) & (spots < LENGTH)
        g_own_places = jnp.where(
            inside[:, None], total[jnp.clip(spots, 0, LENGTH - 1)], 0.0
        )
        mats_grad = lax.psum_scatter(
            jnp.concatenate([g_qkv, g_rest], axis=0), axis, scatter_dimension=0, tiled=True
        )
        mats_grad = mats_grad.astype(F32).T
    table_grad = dot_tn(pick(wanted, owned), sent) + g_own_places

    def send_more(state):
        turn, total = state
        key, asked = requests_of(chosen, owner, slot, owned, devices, room + turn * more, more)
        wanted = swap(asked.reshape(devices, more)).reshape(-1)
        sent = dot_tn(pick(key, devices * more), input_grad).astype(BF)
        sent = swap(sent.reshape(devices, more, D)).reshape(-1, D)
        return turn + 1, total + dot_tn(pick(wanted, owned), sent)

    _, table_grad = lax.while_loop(
        lambda state: state[0] < rounds, send_more, (jnp.int32(0), table_grad)
    )

    counter = jnp.float32(STEP)
    corr_one = 1.0 - jnp.power(jnp.float32(beta_one), counter)
    corr_two = 1.0 - jnp.power(jnp.float32(beta_two), counter)
    table_step, table_first_next = adam_direction(
        embed_table, table_first, table_second, table_grad, corr_one, corr_two, decay_rate
    )
    mats_step, mats_first_next = adam_direction(
        layer_mats, mats_first, mats_second, mats_grad, corr_one, corr_two, decay_rate
    )
    vecs_step, vecs_first_next = adam_direction(
        layer_vecs, vecs_first, vecs_second, vecs_grad, corr_one, corr_two, 0.0
    )
    return (
        outputs,
        input_grad,
        table_grad,
        mats_grad,
        vecs_grad,
        table_step,
        table_first_next,
        mats_step,
        mats_first_next,
        vecs_step,
        vecs_first_next,
    )


def solution(mesh):
    line = P("fsdp")
    by_rows = P("fsdp", None)
    by_cols = P(None, "fsdp")
    return jax.shard_map(
        functools.partial(body, mesh.shape["fsdp"]),
        mesh=mesh,
        in_specs=(
            line,
            line,
            line,
            line,
            by_rows,
            by_rows,
            by_rows,
            by_rows,
            by_cols,
            by_cols,
            by_cols,
            line,
            line,
            line,
        ),
        out_specs=(
            by_rows,
            by_rows,
            by_rows,
            by_cols,
            line,
            by_rows,
            by_rows,
            by_cols,
            by_cols,
            line,
            line,
        ),
        check_vma=False,
    )
```

```python
import functools

import jax
import jax.numpy as jnp
from jax import lax
from jax.experimental import pallas as pl
from jax.experimental.pallas import tpu as pltpu
from jax.sharding import PartitionSpec as P

D = 768
HEADS = 12
HEAD_DIM = 64
FF = 3072
VOCAB = 14592
LENGTH = 512
STEP = 10
QKV = 3 * D

norm_eps = 1e-12
mask_token = 103
beta_one = 0.9
beta_two = 0.999
adam_eps = 1e-06
decay_rate = 0.01

BF = jnp.bfloat16
F32 = jnp.float32
LOG2E = 1.4426950408889634
SCORE = HEAD_DIM ** (-0.5)
MB = 1024 * 1024

ROW_TILE = 256


def dot_nn(left, right):
    return lax.dot_general(
        left, right, (((1,), (0,)), ((), ())), preferred_element_type=F32
    )


def dot_nt(left, right):
    return lax.dot_general(
        left, right, (((1,), (1,)), ((), ())), preferred_element_type=F32
    )


def dot_tn(left, right):
    return lax.dot_general(
        left, right, (((0,), (0,)), ((), ())), preferred_element_type=F32
    )


def gelu_parts(values):
    size = jnp.abs(values)
    frac = 1.0 / (1.0 + (0.3275911 * 0.7071067811865476) * size)
    expo = jnp.exp2(values * values * (-0.5 * LOG2E))
    poly = 1.061405429 * 0.5
    for coef in (-1.453152027, 1.421413741, -0.284496736, 0.254829592):
        poly = poly * frac + 0.5 * coef
    tail = poly * frac * expo
    cdf = jnp.where(values >= 0, 1.0 - tail, tail)
    return values * cdf, cdf + values * expo * 0.3989422804014327


def norm_parts(total):
    centre = jnp.mean(total, -1, keepdims=True)
    centered = total - centre
    variance = jnp.mean(centered * centered, -1, keepdims=True)
    scale = lax.rsqrt(variance + norm_eps)
    return centered * scale, scale


def norm_back(scaled, unit, scale):
    return scale * (
        scaled
        - jnp.mean(scaled, -1, keepdims=True)
        - unit * jnp.mean(scaled * unit, -1, keepdims=True)
    )


def middle_kernel(
    att_ref,
    x_ref,
    go_ref,
    mask_ref,
    wout_ref,
    up_0,
    up_1,
    up_2,
    up_3,
    down_0,
    down_1,
    down_2,
    down_3,
    vec_ref,
    bup_ref,
    out_ref,
    normed_ref,
    hidden_ref,
    gmid_ref,
    gup_ref,
    gfirst_ref,
    gfirstb_ref,
    gatt_ref,
    sums_ref,
    slope_ref,
):
    @pl.when(pl.program_id(0) == 0)
    def _():
        sums_ref[...] = jnp.zeros_like(sums_ref)

    ups = (up_0, up_1, up_2, up_3)
    downs = (down_0, down_1, down_2, down_3)
    bias_out = vec_ref[0:1, :]
    gain_one = vec_ref[1:2, :]
    shift_one = vec_ref[2:3, :]
    bias_down = vec_ref[3:4, :]
    gain_two = vec_ref[4:5, :]
    shift_two = vec_ref[5:6, :]

    def note(row, values):
        sums_ref[row : row + 1, 0:D] += jnp.sum(values, 0, keepdims=True)

    branch = dot_nt(att_ref[...], wout_ref[...]) + bias_out
    unit_one, scale_one = norm_parts(x_ref[...] + branch)
    normed = unit_one * gain_one + shift_one
    normed_b = normed.astype(BF)
    normed_ref[...] = normed_b
    downward = jnp.zeros(normed.shape, F32)
    for start in range(0, FF, D):
        cols = slice(start, start + D)
        upward = dot_nt(normed_b, ups[start // D][...]) + bup_ref[0:1, cols]
        hidden, slope = gelu_parts(upward)
        slope_ref[:, cols] = slope
        hidden_b = hidden.astype(BF)
        hidden_ref[:, cols] = hidden_b
        downward += dot_nn(hidden_b, downs[start // D][...])
    unit_two, scale_two = norm_parts(normed + downward + bias_down)
    out_ref[...] = (unit_two * gain_two + shift_two).astype(BF)
    g_out = go_ref[...].astype(F32) * mask_ref[...].astype(F32)
    note(5, g_out * unit_two)
    note(6, g_out)
    g_mid = norm_back(g_out * gain_two, unit_two, scale_two)
    note(4, g_mid)
    g_mid_b = g_mid.astype(BF)
    gmid_ref[...] = g_mid_b
    g_normed = g_mid
    for start in range(0, FF, D):
        cols = slice(start, start + D)
        g_up = dot_nt(g_mid_b, downs[start // D][...]) * slope_ref[:, cols]
        sums_ref[0:1, cols] += jnp.sum(g_up, 0, keepdims=True)
        g_up_b = g_up.astype(BF)
        gup_ref[:, cols] = g_up_b
        g_normed += dot_nn(g_up_b, ups[start // D][...])
    note(2, g_normed * unit_one)
    note(3, g_normed)
    g_first = norm_back(g_normed * gain_one, unit_one, scale_one)
    note(1, g_first)
    gfirst_ref[...] = g_first
    g_first_b = g_first.astype(BF)
    gfirstb_ref[...] = g_first_b
    gatt_ref[...] = dot_nn(g_first_b, wout_ref[...]).astype(BF)


def middle(attended, inputs, out_grad, masked, rest, vecs, bias_up):
    rows = attended.shape[0]
    tile = ROW_TILE

    def row(width):
        return pl.BlockSpec((tile, width), lambda i: (i, 0))

    def whole(shape, place=0):
        return pl.BlockSpec(
            shape, lambda i: (place, 0), pipeline_mode=pl.Buffered(buffer_count=1)
        )

    return pl.pallas_call(
        middle_kernel,
        grid=(rows // tile,),
        in_specs=[
            row(D),
            row(D),
            row(D),
            row(1),
            *[whole((D, D), place) for place in range(9)],
            whole((8, D)),
            whole((1, FF)),
        ],
        out_specs=[
            row(D),
            row(D),
            row(FF),
            row(D),
            row(FF),
            row(D),
            row(D),
            row(D),
            pl.BlockSpec((8, FF), lambda i: (0, 0)),
        ],
        out_shape=[
            jax.ShapeDtypeStruct((rows, D), BF),
            jax.ShapeDtypeStruct((rows, D), BF),
            jax.ShapeDtypeStruct((rows, FF), BF),
            jax.ShapeDtypeStruct((rows, D), BF),
            jax.ShapeDtypeStruct((rows, FF), BF),
            jax.ShapeDtypeStruct((rows, D), F32),
            jax.ShapeDtypeStruct((rows, D), BF),
            jax.ShapeDtypeStruct((rows, D), BF),
            jax.ShapeDtypeStruct((8, FF), F32),
        ],
        scratch_shapes=[pltpu.VMEM((tile, FF), F32)],
        compiler_params=pltpu.CompilerParams(vmem_limit_bytes=56 * MB),
        name="middle",
    )(attended, inputs, out_grad, masked, *[rest] * 9, vecs, bias_up)


def fixed(shape, place=0):
    return pl.BlockSpec(
        shape, lambda i: (place, 0), pipeline_mode=pl.Buffered(buffer_count=1)
    )


def rest_kernel(first_ref, att_ref, up_ref, normed_ref, hidden_ref, mid_ref, out_ref):
    step = pl.program_id(0)
    chunks = FF // D

    @pl.when(step == 0)
    def _():
        out_ref[...] = dot_tn(first_ref[...], att_ref[...]).astype(BF)

    @pl.when(jnp.logical_and(step > 0, step <= chunks))
    def _():
        out_ref[...] = dot_tn(up_ref[...], normed_ref[...]).astype(BF)

    @pl.when(step > chunks)
    def _():
        out_ref[...] = dot_tn(hidden_ref[...], mid_ref[...]).astype(BF)


def rest_gradients(g_first_b, attended, g_up_b, normed_b, hidden_b, g_mid_b):
    rows = attended.shape[0]
    chunks = FF // D
    full = fixed((rows, D))
    return pl.pallas_call(
        rest_kernel,
        grid=(1 + 2 * chunks,),
        in_specs=[
            full,
            full,
            pl.BlockSpec((rows, D), lambda i: (0, jnp.clip(i - 1, 0, chunks - 1))),
            full,
            pl.BlockSpec((rows, D), lambda i: (0, jnp.clip(i - 1 - chunks, 0, chunks - 1))),
            full,
        ],
        out_specs=pl.BlockSpec((D, D), lambda i: (i, 0)),
        out_shape=jax.ShapeDtypeStruct((D + 2 * FF, D), BF),
        compiler_params=pltpu.CompilerParams(vmem_limit_bytes=56 * MB),
        cost_estimate=pl.CostEstimate(
            flops=22_000_000_000, bytes_accessed=50_000_000, transcendentals=0
        ),
        name="rest_gradients",
    )(g_first_b, attended, g_up_b, normed_b, hidden_b, g_mid_b)


MESH = pl.DeviceIdType.MESH
PLANES = 4


def neighbours():
    me = lax.axis_index("fsdp")
    core = lax.rem(me, 2)
    x = lax.rem(me // 2, 2)
    y = lax.rem(me // 4, 2)
    z = me // 8
    step_a = 4 - 2 * core
    step_b = 2 + 2 * core
    a = jnp.where(core == 0, y, x)
    b = jnp.where(core == 0, x, y)
    near_a = me + step_a * (1 - 2 * a)
    near_b = me + step_b * (1 - 2 * b)
    twin = me + 1 - 2 * core
    return me, core, z, a, b, step_a, step_b, near_a, near_b, twin


def greet(me, z, near_a, near_b, twin):
    barrier = pltpu.get_barrier_semaphore()

    def hello(device):
        pl.semaphore_signal(barrier, inc=1, device_id=(device,), device_id_type=MESH)

    for device in (near_a, near_b, twin):
        hello(device)

    @pl.when(z > 0)
    def _():
        hello(me - 8)

    @pl.when(z < PLANES - 1)
    def _():
        hello(me + 8)

    inner = jnp.logical_and(z > 0, z < PLANES - 1)
    pl.semaphore_wait(barrier, jnp.where(inner, 5, 4))


class RestSpread:
    def __init__(self, in_ref, out_ref, scratch):
        self.in_ref, self.out_ref = in_ref, out_ref
        self.own_sem, self.send_sem, self.recv_sem = scratch
        self.place = neighbours()

    @staticmethod
    def scratch():
        return [
            pltpu.SemaphoreType.DMA,
            pltpu.SemaphoreType.DMA((5, 24)),
            pltpu.SemaphoreType.DMA((24,)),
        ]

    def copy(self, shard, device, kind, source=None):
        return pltpu.make_async_remote_copy(
            src_ref=self.out_ref.at[shard] if source is None else source,
            dst_ref=self.out_ref.at[shard],
            send_sem=self.send_sem.at[kind, shard],
            recv_sem=self.recv_sem.at[shard],
            device_id=(device,),
            device_id_type=MESH,
        )

    def shard(self, plane, other_a, other_b):
        me, core, z, a, b, step_a, step_b, near_a, near_b, twin = self.place
        a_at = 1 - a if other_a else a
        b_at = 1 - b if other_b else b
        return jnp.maximum(plane - 1, 0) * 8 + a_at * step_a + b_at * step_b + core

    def planes(self, far):
        z = self.place[2]
        for way in (1, -1) if far else (1,):
            plane = z - way * far
            yield way, plane, jnp.logical_and(plane >= 1, plane < PLANES)

    def routes(self, far):
        me, core, z, a, b, step_a, step_b, near_a, near_b, twin = self.place
        for way, plane, there in self.planes(far):
            shard = self.shard(plane, False, False)
            for onward in (way,) if far else (1, -1):
                goes = jnp.logical_and(z + onward >= 0, z + onward < PLANES)
                yield (
                    jnp.logical_and(there, goes),
                    shard,
                    me + 8 * onward,
                    0 if onward == 1 else 1,
                )
            yield there, shard, near_b, 3
            yield there, shard, near_a, 2
            yield there, shard, twin, 4

    def routes_a(self, far):
        near_b, twin = self.place[8:]
        for way, plane, there in self.planes(far):
            shard = self.shard(plane, True, False)
            yield there, shard, near_b, 3
            yield there, shard, twin, 4

    def routes_b(self, far):
        twin = self.place[9]
        for way, plane, there in self.planes(far):
            for other_a in (False, True):
                yield there, self.shard(plane, other_a, True), twin, 4

    def own(self):
        return pltpu.make_async_copy(
            self.in_ref, self.out_ref.at[self.shard(self.place[2], False, False)], self.own_sem
        )

    def start(self):
        me, core, z, a, b, step_a, step_b, near_a, near_b, twin = self.place
        greet(me, z, near_a, near_b, twin)

        @pl.when(z > 0)
        def _():
            self.own().start()

        for goes, shard, device, kind in self.routes(0):
            pl.when(goes)(
                lambda shard=shard, device=device, kind=kind: self.copy(
                    shard, device, kind, self.in_ref
                ).start()
            )

    def pass_on(self, routes):
        seen = []
        for goes, shard, device, kind in routes:
            if kind == 4:
                seen.append((goes, shard))
        for goes, shard in seen:
            pl.when(goes)(
                lambda shard=shard: self.copy(shard, self.place[9], 4).wait_recv()
            )
            for other, place, device, kind in routes:
                if place is shard:
                    pl.when(other)(
                        lambda shard=shard, device=device, kind=kind: self.copy(
                            shard, device, kind
                        ).start()
                    )

    def column(self, far):
        self.pass_on(list(self.routes(far)))

    def along_a(self, far):
        self.pass_on(list(self.routes_a(far)))

    def along_b(self, far):
        self.pass_on(list(self.routes_b(far)))

    def end(self):
        me, core, z, a, b, step_a, step_b, near_a, near_b, twin = self.place

        def from_twin(place, carry):
            self.copy(place * 2 + 1 - core, twin, 4).wait_recv()
            return carry

        lax.fori_loop(0, 12, from_twin, 0)
        for far in range(PLANES):
            for routes in (self.routes(far), self.routes_a(far), self.routes_b(far)):
                for goes, shard, device, kind in routes:
                    pl.when(goes)(
                        lambda shard=shard, device=device, kind=kind: self.copy(
                            shard, device, kind
                        ).wait_send()
                    )

        @pl.when(z > 0)
        def _():
            self.own().wait()

    def schedule(self):
        return {
            0: [self.start],
            4: [lambda: self.along_a(0)],
            5: [lambda: self.column(1)],
            8: [lambda: self.along_a(1), lambda: self.along_b(0)],
            11: [lambda: self.column(2)],
            13: [lambda: self.along_a(2), lambda: self.along_b(1)],
            16: [lambda: self.column(3)],
            18: [lambda: self.along_a(3), lambda: self.along_b(2)],
            24: [lambda: self.along_b(3)],
            27: [self.end],
        }


class RestSums:
    TURNS = PLANES - 1

    def __init__(self, in_ref, out_ref, scratch):
        self.in_ref, self.out_ref = in_ref, out_ref
        (
            self.own,
            self.from_twin,
            self.from_b,
            self.from_a,
            self.from_low,
            self.from_high,
            self.load_sem,
            self.twin_sem,
            self.b_sem,
            self.a_sem,
            self.low_sem,
            self.high_sem,
        ) = scratch
        self.place = neighbours()

    @staticmethod
    def scratch(shape):
        return [
            pltpu.VMEM((12,) + shape, BF),
            pltpu.VMEM((12,) + shape, BF),
            pltpu.VMEM((6,) + shape, BF),
            pltpu.VMEM((3,) + shape, BF),
            pltpu.VMEM((4,) + shape, BF),
            pltpu.VMEM((4,) + shape, BF),
            pltpu.SemaphoreType.DMA((12,)),
            pltpu.SemaphoreType.DMA((2, 12)),
            pltpu.SemaphoreType.DMA((2, 6)),
            pltpu.SemaphoreType.DMA((2, 3)),
            pltpu.SemaphoreType.DMA((2, 4)),
            pltpu.SemaphoreType.DMA((2, 4)),
        ]

    def remote(self, source, target, sems, slot, device):
        return pltpu.make_async_remote_copy(
            src_ref=source,
            dst_ref=target.at[slot],
            send_sem=sems.at[0, slot],
            recv_sem=sems.at[1, slot],
            device_id=(device,),
            device_id_type=MESH,
        )

    def plane_of(self, turn):
        z = self.place[2]
        last = PLANES - 1 - turn
        inner = (1, 3, 2)[turn]
        return jnp.where(z < 2, last, jnp.where(z == 2, inner, 1 + turn))

    def shards(self, slot):
        me, core, z, a, b, step_a, step_b, near_a, near_b, twin = self.place
        other_b, turn, other_a = slot < 6, slot % 6 // 2, slot % 2 == 0
        base = (self.plane_of(turn) - 1) * 8
        a_at = 1 - a if other_a else a
        b_at = 1 - b if other_b else b
        mine = base + a_at * step_a + b_at * step_b + core
        a_at = 1 - b if other_a else b
        b_at = 1 - a if other_b else a
        twins = base + a_at * step_b + b_at * step_a + 1 - core
        return mine, twins

    def load(self, slot):
        return pltpu.make_async_copy(
            self.in_ref.at[self.shards(slot)[0]], self.own.at[slot], self.load_sem.at[slot]
        )

    def gift(self, slot):
        return self.remote(
            self.in_ref.at[self.shards(slot)[1]],
            self.from_twin,
            self.twin_sem,
            slot,
            self.place[9],
        )

    def over_b(self, slot):
        return self.remote(self.own.at[slot], self.from_b, self.b_sem, slot, self.place[8])

    def over_a(self, turn):
        return self.remote(
            self.own.at[6 + 2 * turn], self.from_a, self.a_sem, turn, self.place[7]
        )

    def along(self, turn, up):
        plane = self.plane_of(turn)
        source = self.own.at[7 + 2 * turn]
        if up:
            return self.remote(source, self.from_low, self.low_sem, plane, self.place[0] + 8)
        return self.remote(source, self.from_high, self.high_sem, plane, self.place[0] - 8)

    def add(self, slot, arrived):
        self.own[slot] = (self.own[slot].astype(F32) + arrived[...].astype(F32)).astype(BF)

    def start(self):
        me, core, z, a, b, step_a, step_b, near_a, near_b, twin = self.place
        greet(me, z, near_a, near_b, twin)
        for slot in (0, 1, 2, 3, 6, 7, 4, 5, 8, 9, 10, 11):
            self.gift(slot).start()
            self.load(slot).start()

    def far(self, turn):
        for slot in (2 * turn, 2 * turn + 1):
            self.load(slot).wait()
            self.gift(slot).wait_recv()
            self.add(slot, self.from_twin.at[slot])
            self.over_b(slot).start()

    def near(self, turn):
        for slot in (6 + 2 * turn, 7 + 2 * turn):
            self.load(slot).wait()
            self.gift(slot).wait_recv()
            self.add(slot, self.from_twin.at[slot])

    def stage_b(self, turn):
        for slot in (2 * turn, 2 * turn + 1):
            self.over_b(slot).wait_recv()
            self.add(6 + slot, self.from_b.at[slot])
        self.over_a(turn).start()

    def stage_a(self, turn):
        z = self.place[2]
        slot = 7 + 2 * turn
        plane = self.plane_of(turn)
        self.over_a(turn).wait_recv()
        self.add(slot, self.from_a.at[turn])

        @pl.when(jnp.logical_and(plane > z, z > 0))
        def _():
            self.along(turn, True).wait_recv()
            self.add(slot, self.from_low.at[plane])

        @pl.when(plane > z)
        def _():
            self.along(turn, True).start()

        @pl.when(jnp.logical_and(plane < z, z < PLANES - 1))
        def _():
            self.along(turn, False).wait_recv()
            self.add(slot, self.from_high.at[plane])

        @pl.when(plane < z)
        def _():
            self.along(turn, False).start()

        @pl.when(plane == z)
        def _():
            self.along(turn, True).wait_recv()
            self.out_ref[...] = self.own[slot].astype(F32) + self.from_low[plane].astype(F32)

        @pl.when(jnp.logical_and(plane == z, z < PLANES - 1))
        def _():
            self.along(turn, False).wait_recv()
            self.out_ref[...] += self.from_high[plane].astype(F32)

    def end(self):
        z = self.place[2]
        for slot in range(12):
            self.gift(slot).wait_send()
        for slot in range(6):
            self.over_b(slot).wait_send()
        for turn in range(self.TURNS):
            self.over_a(turn).wait_send()
            plane = self.plane_of(turn)

            @pl.when(plane > z)
            def _(turn=turn):
                self.along(turn, True).wait_send()

            @pl.when(plane < z)
            def _(turn=turn):
                self.along(turn, False).wait_send()

    def schedule(self):
        return {
            0: [self.start],
            1: [lambda: self.far(0)],
            2: [lambda: self.far(1)],
            3: [lambda: self.near(0)],
            4: [lambda: self.far(2)],
            5: [lambda: self.near(1)],
            6: [lambda: self.near(2)],
            7: [lambda: self.stage_b(0)],
            11: [lambda: self.stage_b(1)],
            13: [lambda: self.stage_a(0)],
            16: [lambda: self.stage_b(2)],
            19: [lambda: self.stage_a(1)],
            24: [lambda: self.stage_a(2)],
            27: [self.end],
        }


PIECES = 4
CHUNKS = 3


def broadcast_kernel(
    split,
    table_ref,
    block_ref,
    out_ref,
    w_ref,
    stage,
    own_sem,
    load_sem,
    send_sem,
    recv_sem,
    w_send,
    w_recv,
):
    first_owner, first_row, count = split
    me, core, z, a, b, step_a, step_b, near_a, near_b, twin = neighbours()
    greet(me, z, near_a, near_b, twin)
    rows = LENGTH // PIECES
    height = block_ref.shape[0] // CHUNKS
    root = first_owner + 1
    gift = pltpu.make_async_remote_copy(
        src_ref=table_ref.at[pl.ds(first_row, count)],
        dst_ref=stage.at[pl.ds(0, count)],
        send_sem=load_sem.at[0],
        recv_sem=load_sem.at[1],
        device_id=(root,),
        device_id_type=MESH,
    )
    mine = pltpu.make_async_copy(
        table_ref.at[pl.ds(0, LENGTH - count)],
        stage.at[pl.ds(count, LENGTH - count)],
        load_sem.at[2],
    )
    shard = lax.rem(me, 8)
    own = pltpu.make_async_copy(block_ref, w_ref.at[shard], own_sem)

    @pl.when(me == first_owner)
    def _():
        gift.start()

    @pl.when(me == root)
    def _():
        mine.start()

    @pl.when(z == 0)
    def _():
        own.start()

    def copy(piece, device, kind):
        part = pl.ds(piece * rows, rows)
        return pltpu.make_async_remote_copy(
            src_ref=out_ref.at[part],
            dst_ref=out_ref.at[part],
            send_sem=send_sem.at[kind, piece],
            recv_sem=recv_sem.at[piece],
            device_id=(device,),
            device_id_type=MESH,
        )

    def block(place, chunk, device, kind, source=None):
        part = pl.ds(chunk * height, height)
        return pltpu.make_async_remote_copy(
            src_ref=w_ref.at[place, part] if source is None else source.at[part],
            dst_ref=w_ref.at[place, part],
            send_sem=w_send.at[kind, place, chunk],
            recv_sem=w_recv.at[place, chunk],
            device_id=(device,),
            device_id_type=MESH,
        )

    trunk = jnp.logical_and(core == 1, jnp.logical_and(a == 1, b == 1))
    branch = jnp.logical_and(core == 1, jnp.logical_and(a == 0, b == 1))
    routes = (
        (jnp.logical_and(trunk, z > 0), me - 8),
        (trunk, near_a),
        (jnp.logical_or(trunk, branch), near_b),
        (core == 1, twin),
    )
    shard_a = (1 - a) * step_a + b * step_b + core
    shards_b = [
        a * step_a + (1 - b) * step_b + core,
        (1 - a) * step_a + (1 - b) * step_b + core,
    ]

    def from_own(chunk):
        def sends(source):
            pl.when(z < PLANES - 1)(lambda: block(shard, chunk, me + 8, 0, source).start())
            block(shard, chunk, near_b, 1, source).start()
            block(shard, chunk, near_a, 2, source).start()
            block(shard, chunk, twin, 3, source).start()

        @pl.when(z == 0)
        def _():
            sends(block_ref)

        @pl.when(z > 0)
        def _():
            block(shard, chunk, twin, 3).wait_recv()
            sends(None)

    def from_a(chunk):
        block(shard_a, chunk, twin, 3).wait_recv()
        block(shard_a, chunk, near_b, 1).start()
        block(shard_a, chunk, twin, 3).start()

    def from_b(chunk):
        for place in shards_b:
            block(place, chunk, twin, 3).wait_recv()
            block(place, chunk, twin, 3).start()

    def positions(piece):
        part = slice(piece * rows, (piece + 1) * rows)

        @pl.when(me == root)
        def _():
            if piece == 0:
                mine.wait()
                gift.wait_recv()
            out_ref[part, :] = stage[part, :].astype(BF)

        @pl.when(me != root)
        def _():
            copy(piece, twin, 3).wait_recv()

        for kind, (goes, device) in enumerate(routes):
            pl.when(goes)(lambda kind=kind, device=device: copy(piece, device, kind).start())

    from_own(0)
    positions(0)
    from_own(1)
    from_a(0)
    positions(1)
    from_own(2)
    from_a(1)
    from_b(0)
    positions(2)
    from_a(2)
    from_b(1)
    positions(3)
    from_b(2)

    def from_twin(place, carry):
        for chunk in range(CHUNKS):
            block(place * 2 + 1 - core, chunk, twin, 3).wait_recv()
        return carry

    lax.fori_loop(0, 4, from_twin, 0)
    for piece in range(PIECES):
        for kind, (goes, device) in enumerate(routes):
            pl.when(goes)(
                lambda piece=piece, kind=kind, device=device: copy(
                    piece, device, kind
                ).wait_send()
            )
    for chunk in range(CHUNKS):

        @pl.when(z < PLANES - 1)
        def _(chunk=chunk):
            block(shard, chunk, me + 8, 0).wait_send()

        block(shard, chunk, near_b, 1).wait_send()
        block(shard, chunk, near_a, 2).wait_send()
        block(shard, chunk, twin, 3).wait_send()
        block(shard_a, chunk, near_b, 1).wait_send()
        block(shard_a, chunk, twin, 3).wait_send()
        for place in shards_b:
            block(place, chunk, twin, 3).wait_send()

    @pl.when(me == first_owner)
    def _():
        gift.wait_send()

    @pl.when(z == 0)
    def _():
        own.wait()


def place_split(devices, owned):
    first_owner = VOCAB // owned
    first_row = VOCAB - first_owner * owned
    return first_owner, first_row, owned - first_row


def broadcast(table, block, split, ident):
    return pl.pallas_call(
        functools.partial(broadcast_kernel, split),
        in_specs=[pl.BlockSpec(memory_space=pl.ANY)] * 2,
        out_specs=[
            pl.BlockSpec(memory_space=pltpu.VMEM),
            pl.BlockSpec(memory_space=pl.ANY),
        ],
        out_shape=[
            jax.ShapeDtypeStruct((LENGTH, D), BF),
            jax.ShapeDtypeStruct((8,) + block.shape, BF),
        ],
        scratch_shapes=[
            pltpu.VMEM((LENGTH, D), F32),
            pltpu.SemaphoreType.DMA,
            pltpu.SemaphoreType.DMA((3,)),
            pltpu.SemaphoreType.DMA((4, PIECES)),
            pltpu.SemaphoreType.DMA((PIECES,)),
            pltpu.SemaphoreType.DMA((4, 8, CHUNKS)),
            pltpu.SemaphoreType.DMA((8, CHUNKS)),
        ],
        compiler_params=pltpu.CompilerParams(collective_id=ident, has_side_effects=True),
        cost_estimate=pl.CostEstimate(flops=0, bytes_accessed=100_000_000, transcendentals=0),
        name="broadcast",
    )(table, block)


def homecoming_kernel(
    split,
    place_ref,
    first_ref,
    out_ref,
    mats_ref,
    sums,
    from_twin,
    from_b,
    from_a,
    from_z,
    ready,
    own,
    own_twin,
    own_b,
    own_a,
    own_high,
    sems,
    z_sem,
    piece_sem,
    home_sem,
    load_sem,
    twin_sem,
    b_sem,
    a_sem,
    high_sem,
):
    first_owner, first_row, count = split
    root = first_owner + 1
    me, core, z, a, b, step_a, step_b, near_a, near_b, twin = neighbours()
    rows = place_ref.shape[4]
    height = first_ref.shape[1] // CHUNKS
    out_ref[...] = jnp.zeros_like(out_ref)
    barrier = pltpu.get_barrier_semaphore()

    def each(step, carry):
        pl.semaphore_signal(
            barrier, inc=1, device_id=(lax.rem(me + step, 32),), device_id_type=MESH
        )
        return carry

    lax.fori_loop(1, 32, each, 0)
    pl.semaphore_wait(barrier, 31)

    def remote(source, target, send, receive, device):
        return pltpu.make_async_remote_copy(
            src_ref=source,
            dst_ref=target,
            send_sem=send,
            recv_sem=receive,
            device_id=(device,),
            device_id_type=MESH,
        )

    def add(total, extra):
        return (total.astype(F32) + extra.astype(F32)).astype(BF)

    x = jnp.where(core == 0, b, a)
    y = jnp.where(core == 0, a, b)
    gift = remote(place_ref.at[:, :, :, 1 - core], from_twin, sems.at[0, 0], sems.at[0, 1], twin)
    gift.start()
    loads, gifts = [], []
    for slot in range(4):
        other_b, other_a = slot < 2, slot % 2 == 0
        a_at, b_at = (1 - a if other_a else a), (1 - b if other_b else b)
        shard = a_at * step_a + b_at * step_b + core
        loads.append(pltpu.make_async_copy(first_ref.at[shard], own.at[slot], load_sem.at[slot]))
        a_at, b_at = (1 - b if other_a else b), (1 - a if other_b else a)
        shard = a_at * step_b + b_at * step_a + 1 - core
        gifts.append(
            remote(
                first_ref.at[shard],
                own_twin.at[slot],
                twin_sem.at[0, slot],
                twin_sem.at[1, slot],
                twin,
            )
        )
    for slot in range(4):
        gifts[slot].start()
        loads[slot].start()
    gift.wait_recv()
    sums[...] = add(place_ref[:, :, :, core], from_twin[...])

    @pl.when(core == 0)
    def _():
        remote(sums.at[:, :, 1 - x], from_b, sems.at[1, 0], sems.at[1, 1], near_b).start()

    @pl.when(core == 1)
    def _():
        remote(sums.at[:, 1 - y], from_b, sems.at[1, 0], sems.at[1, 1], near_b).start()

    over_b = [
        remote(own.at[slot], own_b.at[slot], b_sem.at[0, slot], b_sem.at[1, slot], near_b)
        for slot in range(2)
    ]
    for slot in range(4):
        loads[slot].wait()
        gifts[slot].wait_recv()
        own[slot] = add(own[slot], own_twin[slot])
        if slot < 2:
            over_b[slot].start()

    small_b = remote(sums.at[:, 0], from_b, sems.at[1, 0], sems.at[1, 1], near_b)
    small_b.wait_recv()

    @pl.when(core == 0)
    def _():
        from_b[...] = add(sums[:, :, x], from_b[...])

    @pl.when(core == 1)
    def _():
        from_b[...] = add(sums[:, y], from_b[...])

    small_a = remote(from_b.at[:, 1 - a], from_a, sems.at[2, 0], sems.at[2, 1], near_a)
    small_a.start()
    over_a = remote(own.at[2], own_a, a_sem.at[0], a_sem.at[1], near_a)
    for slot in range(2):
        over_b[slot].wait_recv()
        own[2 + slot] = add(own[2 + slot], own_b[slot])
        if slot == 0:
            over_a.start()
    small_a.wait_recv()
    from_a[...] = add(from_b[:, a], from_a[...])

    def column(plane, action):
        @pl.when(plane != z)
        def _():
            action(
                remote(
                    from_a.at[plane],
                    from_z.at[z],
                    z_sem.at[0, plane],
                    z_sem.at[1, z],
                    me + 8 * (plane - z),
                )
            )

    for plane in range(PLANES):
        column(plane, lambda item: item.start())
    over_a.wait_recv()

    def down(chunk):
        part = pl.ds(chunk * height, height)
        return remote(
            own.at[3, part],
            own_high.at[part],
            high_sem.at[0, chunk],
            high_sem.at[1, chunk],
            me - 8,
        )

    for chunk in range(CHUNKS):
        part = pl.ds(chunk * height, height)
        own[3, part] = add(own[3, part], own_a[part])

        @pl.when(z < PLANES - 1)
        def _(chunk=chunk, part=part):
            down(chunk).wait_recv()
            own[3, part] = add(own[3, part], own_high[part])

        @pl.when(z > 0)
        def _(chunk=chunk):
            down(chunk).start()

    mats_ref[...] = own[3].astype(F32)
    ready[...] = from_a[z].astype(F32)
    for plane in range(PLANES):

        @pl.when(plane != z)
        def _(plane=plane):
            remote(
                from_a.at[plane], from_z.at[plane], z_sem.at[0, plane], z_sem.at[1, plane], twin
            ).wait_recv()
            ready[...] += from_z[plane].astype(F32)

    def home(device, half):
        place = device * rows + half * 8
        early = place < count
        owner = jnp.where(early, first_owner, root)
        spot = pl.multiple_of(jnp.where(early, first_row + place, place - count), 8)
        return owner, spot

    def piece(device, half):
        owner, spot = home(device, half)
        return remote(
            ready.at[pl.ds(half * 8, 8)],
            out_ref.at[pl.ds(spot, 8)],
            piece_sem.at[half],
            home_sem.at[device * 2 + half],
            owner,
        )

    for half in range(2):
        owner, spot = home(me, half)

        @pl.when(owner == me)
        def _(half=half, spot=spot):
            out_ref[pl.ds(spot, 8), :] = ready[half * 8 : half * 8 + 8, :]

        @pl.when(owner != me)
        def _(half=half):
            piece(me, half).start()

    def arrive(index, carry):
        device, half = index // 2, lax.rem(index, 2)
        owner, _ = home(device, half)

        @pl.when(jnp.logical_and(owner == me, device != me))
        def _():
            piece(device, half).wait_recv()

        return carry

    @pl.when(me >= first_owner)
    def _():
        lax.fori_loop(0, 64, arrive, 0)

    for half in range(2):
        owner, _ = home(me, half)

        @pl.when(owner != me)
        def _(half=half):
            piece(me, half).wait_send()

    for item in [gift, small_b, small_a, over_a] + gifts + over_b:
        item.wait_send()
    for plane in range(PLANES):
        column(plane, lambda item: item.wait_send())
    for chunk in range(CHUNKS):

        @pl.when(z > 0)
        def _(chunk=chunk):
            down(chunk).wait_send()


def homecoming(place_sums, first, owned, split, ident):
    rows = LENGTH // 32
    small = (rows, D)
    shape = first.shape[1:]
    return pl.pallas_call(
        functools.partial(homecoming_kernel, split),
        in_specs=[
            pl.BlockSpec(memory_space=pltpu.VMEM),
            pl.BlockSpec(memory_space=pl.ANY),
        ],
        out_specs=[pl.BlockSpec(memory_space=pltpu.VMEM)] * 2,
        out_shape=[
            jax.ShapeDtypeStruct((owned, D), F32),
            jax.ShapeDtypeStruct(shape, F32),
        ],
        scratch_shapes=[
            pltpu.VMEM((4, 2, 2) + small, BF),
            pltpu.VMEM((4, 2, 2) + small, BF),
            pltpu.VMEM((4, 2) + small, BF),
            pltpu.VMEM((4,) + small, BF),
            pltpu.VMEM((4,) + small, BF),
            pltpu.VMEM(small, F32),
            pltpu.VMEM((4,) + shape, BF),
            pltpu.VMEM((4,) + shape, BF),
            pltpu.VMEM((2,) + shape, BF),
            pltpu.VMEM(shape, BF),
            pltpu.VMEM(shape, BF),
            pltpu.SemaphoreType.DMA((3, 2)),
            pltpu.SemaphoreType.DMA((2, 4)),
            pltpu.SemaphoreType.DMA((2,)),
            pltpu.SemaphoreType.DMA((64,)),
            pltpu.SemaphoreType.DMA((4,)),
            pltpu.SemaphoreType.DMA((2, 4)),
            pltpu.SemaphoreType.DMA((2, 2)),
            pltpu.SemaphoreType.DMA((2,)),
            pltpu.SemaphoreType.DMA((2, CHUNKS)),
        ],
        compiler_params=pltpu.CompilerParams(
            collective_id=ident, has_side_effects=True, vmem_limit_bytes=40 * MB
        ),
        cost_estimate=pl.CostEstimate(
            flops=0, bytes_accessed=200_000_000, transcendentals=0
        ),
        name="homecoming",
    )(place_sums.reshape((4, 2, 2, 2) + small), first)


def forward_kernel(
    by_kernel,
    key_ref,
    found_ref,
    extra_ref,
    place_ref,
    w_ref,
    bias_ref,
    block_ref,
    x_ref,
    xb_ref,
    proj_ref,
    att_ref,
    lse_ref,
    *scratch,
):
    seq, head = pl.program_id(0), pl.program_id(1)
    pairs = HEADS // 2
    step = seq * (pairs + 1) + head
    if by_kernel:
        gather = RestSpread(block_ref, scratch[0], scratch[1:])
        for when, actions in gather.schedule().items():

            @pl.when(step == when)
            def _(actions=actions):
                for action in actions:
                    action()

    @pl.when(head == 0)
    def _():
        slots = lax.broadcasted_iota(jnp.int32, (LENGTH, found_ref.shape[0]), 1)
        picked = (key_ref[...] == slots).astype(BF)
        inputs = dot_nn(picked, found_ref[...]) + extra_ref[...].astype(F32)
        inputs = inputs + place_ref[...].astype(F32)
        x_ref[...] = inputs
        inputs_b = inputs.astype(BF)
        xb_ref[...] = inputs_b
        for start in range(0, QKV, D):
            cols = slice(start, start + D)
            part = dot_nt(inputs_b, w_ref[cols, :]) + bias_ref[:, cols]
            proj_ref[:, cols] = part.astype(BF)

    @pl.when(head > 0)
    def _():
        width = 2 * HEAD_DIM
        start = (head - 1) * width
        query = proj_ref[:, pl.ds(pl.multiple_of(start, width), width)]
        keys = proj_ref[:, pl.ds(pl.multiple_of(D + start, width), width)]
        values_t = proj_ref[:, pl.ds(pl.multiple_of(2 * D + start, width), width)].T
        lane = lax.broadcasted_iota(jnp.int32, query.shape, 1)
        outs = []
        for half in range(2):
            mine = (lane < HEAD_DIM) if half == 0 else (lane >= HEAD_DIM)
            picked = jnp.where(mine, query, jnp.zeros_like(query))
            scores = dot_nt(keys, picked)
            highest = jnp.max(scores, 0, keepdims=True)
            expo = jnp.exp2((scores - highest) * (SCORE * LOG2E))
            total = jnp.sum(expo, 0, keepdims=True)
            part = values_t[half * HEAD_DIM : (half + 1) * HEAD_DIM, :]
            outs.append(dot_nn(part, expo.astype(BF)) / total)
            lse_ref[0, half : half + 1, :] = highest * (SCORE * LOG2E) + jnp.log2(total)
        att_ref[...] = jnp.concatenate(outs, 0).T.astype(BF)


def forward(by_kernel, key, found, extra, places, w_qkv, bias, block, ident):
    rows = key.shape[0]
    seqs = rows // LENGTH
    pairs = HEADS // 2
    slots = found.shape[0]

    def row(width):
        return pl.BlockSpec((LENGTH, width), lambda s, h: (s, 0))

    def steady(shape):
        return pl.BlockSpec(
            shape, lambda s, h: (0, 0), pipeline_mode=pl.Buffered(buffer_count=1)
        )

    out_specs = [
        row(D),
        row(D),
        row(QKV),
        pl.BlockSpec((LENGTH, 2 * HEAD_DIM), lambda s, h: (s, jnp.maximum(h - 1, 0))),
        pl.BlockSpec(
            (1, 2, LENGTH), lambda s, h: (s * pairs + jnp.maximum(h - 1, 0), 0, 0)
        ),
    ]
    out_shape = [
        jax.ShapeDtypeStruct((rows, D), F32),
        jax.ShapeDtypeStruct((rows, D), BF),
        jax.ShapeDtypeStruct((rows, QKV), BF),
        jax.ShapeDtypeStruct((rows, D), BF),
        jax.ShapeDtypeStruct((seqs * pairs, 2, LENGTH), F32),
    ]
    params = {}
    scratch = []
    if by_kernel:
        out_specs.append(pl.BlockSpec(memory_space=pl.ANY))
        out_shape.append(jax.ShapeDtypeStruct((24,) + block.shape, BF))
        params = dict(collective_id=ident, has_side_effects=True)
        scratch = RestSpread.scratch()
    return pl.pallas_call(
        functools.partial(forward_kernel, by_kernel),
        grid=(seqs, pairs + 1),
        in_specs=[
            row(1),
            steady((slots, D)),
            row(D),
            steady((LENGTH, D)),
            steady((QKV, D)),
            steady((1, QKV)),
            pl.BlockSpec(memory_space=pl.ANY),
        ],
        out_specs=out_specs,
        out_shape=out_shape,
        scratch_shapes=scratch,
        compiler_params=pltpu.CompilerParams(vmem_limit_bytes=56 * MB, **params),
        cost_estimate=pl.CostEstimate(
            flops=40_000_000_000, bytes_accessed=60_000_000, transcendentals=0
        ),
        name="forward",
    )(key[:, None], found, extra, places, w_qkv, bias, block)


def backward_kernel(
    by_kernel,
    q_ref,
    k_ref,
    v_ref,
    att_ref,
    g_ref,
    lse_ref,
    first_ref,
    xb_ref,
    w_ref,
    rest_ref,
    grad_ref,
    place_ref,
    weights_ref,
    bias_ref,
    mats_ref,
    proj,
    total,
    places,
    *scratch,
):
    seq, head = pl.program_id(0), pl.program_id(1)
    pairs = HEADS // 2
    step = seq * (pairs + 1) + head

    @pl.when(step == 0)
    def _():
        total[...] = jnp.zeros_like(total)
        places[...] = jnp.zeros_like(places)
        bias_ref[...] = jnp.zeros_like(bias_ref)
        mats_ref[...] = jnp.zeros_like(mats_ref)

    if by_kernel:
        sums = RestSums(rest_ref, mats_ref, scratch)
        for when, actions in sums.schedule().items():

            @pl.when(step == when)
            def _(actions=actions):
                for action in actions:
                    action()

    @pl.when(head < pairs)
    def _():
        cols = pl.ds(pl.multiple_of(head * 2 * HEAD_DIM, 2 * HEAD_DIM), 2 * HEAD_DIM)
        query = q_ref[...]
        keys = k_ref[...]
        values = v_ref[...]
        grad = g_ref[...]
        lane = lax.broadcasted_iota(jnp.int32, query.shape, 1)
        first = lane < HEAD_DIM
        product = (att_ref[...].astype(F32) * grad.astype(F32)).T
        zero = jnp.zeros_like(query)
        g_q, g_k, g_v = [], [], []
        for half in range(2):
            mine = first if half == 0 else jnp.logical_not(first)
            scores = dot_nt(keys, jnp.where(mine, query, zero))
            probs = jnp.exp2(scores * (SCORE * LOG2E) - lse_ref[0, half : half + 1, :])
            delta = jnp.sum(
                product[half * HEAD_DIM : (half + 1) * HEAD_DIM, :], 0, keepdims=True
            )
            g_probs = dot_nt(values, jnp.where(mine, grad, zero))
            g_v.append(dot_nn(probs.astype(BF), grad))
            g_scores = (probs * (g_probs - delta)).astype(BF)
            g_k.append(dot_nn(g_scores, query))
            g_q.append(dot_tn(g_scores, keys))
        grad_q = jnp.where(first, g_q[0], g_q[1]) * SCORE
        grad_k = jnp.where(first, g_k[0], g_k[1]) * SCORE
        grad_v = jnp.where(first, g_v[0], g_v[1])
        proj[0, :, cols] = grad_q.astype(BF)
        proj[1, :, cols] = grad_k.astype(BF)
        proj[2, :, cols] = grad_v.astype(BF)
        bias_ref[0:1, cols] += jnp.sum(grad_q, 0, keepdims=True)
        bias_ref[1:2, cols] += jnp.sum(grad_v, 0, keepdims=True)

    @pl.when(head == pairs)
    def _():
        g_in = first_ref[...]
        inputs_b = xb_ref[...]
        for part in range(3):
            cols = slice(part * D, (part + 1) * D)
            g_in = g_in + dot_nn(proj[part], w_ref[cols, :])
            total[cols, :] += dot_tn(proj[part], inputs_b)
        grad_ref[...] = g_in.astype(BF)
        places[...] += g_in

    @pl.when(step == pl.num_programs(0) * (pairs + 1) - 1)
    def _():
        weights_ref[...] = total[...].astype(BF)
        place_ref[...] = places[...].astype(BF)


def backward(by_kernel, projected, attended, grad_att, lse, g_first, inputs_b, w_qkv, rest, ident):
    rows = projected.shape[0]
    seqs = rows // LENGTH
    pairs = HEADS // 2
    block = (LENGTH, 2 * HEAD_DIM)
    shape = rest.shape[1:]

    def pair(offset):
        return pl.BlockSpec(block, lambda s, h: (s, offset + jnp.minimum(h, pairs - 1)))

    def row(width):
        return pl.BlockSpec((LENGTH, width), lambda s, h: (s, 0))

    def steady(shape):
        return pl.BlockSpec(
            shape, lambda s, h: (0, 0), pipeline_mode=pl.Buffered(buffer_count=1)
        )

    def kept(shape):
        return pl.BlockSpec(shape, lambda s, h: (0, 0))

    return pl.pallas_call(
        functools.partial(backward_kernel, by_kernel),
        grid=(seqs, pairs + 1),
        in_specs=[
            pair(0),
            pair(pairs),
            pair(2 * pairs),
            pair(0),
            pair(0),
            pl.BlockSpec(
                (1, 2, LENGTH), lambda s, h: (s * pairs + jnp.minimum(h, pairs - 1), 0, 0)
            ),
            row(D),
            row(D),
            steady((QKV, D)),
            pl.BlockSpec(memory_space=pl.ANY),
        ],
        out_specs=[
            row(D),
            kept((LENGTH, D)),
            kept((QKV, D)),
            kept((8, D)),
            kept(shape),
        ],
        out_shape=[
            jax.ShapeDtypeStruct((rows, D), BF),
            jax.ShapeDtypeStruct((LENGTH, D), BF),
            jax.ShapeDtypeStruct((QKV, D), BF),
            jax.ShapeDtypeStruct((8, D), F32),
            jax.ShapeDtypeStruct(shape, F32),
        ],
        scratch_shapes=[
            pltpu.VMEM((3, LENGTH, D), BF),
            pltpu.VMEM((QKV, D), F32),
            pltpu.VMEM((LENGTH, D), F32),
        ]
        + (RestSums.scratch(shape) if by_kernel else []),
        compiler_params=pltpu.CompilerParams(
            vmem_limit_bytes=60 * MB,
            **(dict(collective_id=ident, has_side_effects=True) if by_kernel else {}),
        ),
        cost_estimate=pl.CostEstimate(
            flops=60_000_000_000, bytes_accessed=60_000_000, transcendentals=0
        ),
        name="backward",
    )(
        projected,
        projected,
        projected,
        attended,
        grad_att,
        lse,
        g_first,
        inputs_b,
        w_qkv,
        rest,
    )


def slots_of(ids, owned):
    count = ids.shape[0]
    order = jnp.arange(count, dtype=jnp.int32)
    repeated = jnp.any(
        (ids[:, None] == ids[None, :]) & (order[:, None] < order[None, :]), axis=0
    )
    first = jnp.logical_not(repeated)
    base = (ids // owned) * owned
    below = (
        first[:, None]
        & (ids[:, None] >= base[None, :])
        & (ids[:, None] < ids[None, :])
    )
    return jnp.sum(below.astype(jnp.int32), axis=0)


def requests_of(ids, owner, slot, owned, devices, start, room):
    key = jnp.where((slot >= start) & (slot < start + room), owner * room + slot - start, -1)
    spots = jnp.arange(devices * room, dtype=jnp.int32)
    asked = jnp.max(
        jnp.where(key[:, None] == spots[None, :], (ids - owner * owned)[:, None], -1), axis=0
    )
    return key, asked


def pick(index, amount):
    return (index[:, None] == jnp.arange(amount, dtype=jnp.int32)[None, :]).astype(BF)


def adam_direction(param, first, second, grad, corr_one, corr_two, decay):
    first_next = beta_one * first + (1.0 - beta_one) * grad
    second_next = beta_two * second + (1.0 - beta_two) * grad * grad
    update = first_next / corr_one / (jnp.sqrt(second_next / corr_two) + adam_eps)
    return (update + decay * param, first_next)


def body(
    devices,
    token_ids,
    masked,
    swap_kind,
    swap_ids,
    out_grad,
    embed_table,
    table_first,
    table_second,
    layer_mats,
    mats_first,
    mats_second,
    layer_vecs,
    vecs_first,
    vecs_second,
):
    axis = "fsdp"
    rows = token_ids.shape[0]
    owned = embed_table.shape[0]
    entries = layer_vecs.shape[0]
    columns = layer_mats.shape[1]
    me = lax.axis_index(axis)
    by_kernel = devices == 32
    split = place_split(devices, owned)
    replaced = jnp.where(swap_kind < 8, mask_token, jnp.where(swap_kind == 8, swap_ids, token_ids))
    chosen = jnp.where(masked == 1, replaced, token_ids)

    def swap(blocks):
        return lax.all_to_all(blocks, axis, 0, 0, tiled=True)

    block = layer_mats.astype(BF).T

    room = 16 * -(-1536 // (16 * devices))
    more = 16
    owner = chosen // owned
    slot = slots_of(chosen, owned)
    most = jnp.max(slot) + 1
    key, asked = requests_of(chosen, owner, slot, owned, devices, 0, room)
    _, asked_more = requests_of(chosen, owner, slot, owned, devices, room, more)
    table_b = embed_table.astype(BF)
    own_vecs = layer_vecs.astype(BF).astype(F32)
    notes = jnp.concatenate(
        [
            asked.reshape(devices, room).astype(F32),
            asked_more.reshape(devices, more).astype(F32),
            jnp.broadcast_to(own_vecs[None], (devices, entries)),
            jnp.broadcast_to(most.astype(F32), (devices, 1)),
        ],
        axis=1,
    )
    notes = swap(notes)
    wanted = notes[:, :room].astype(jnp.int32).reshape(-1)
    wanted_more = notes[:, room : room + more].astype(jnp.int32).reshape(-1)
    vecs = notes[:, room + more : room + more + entries].reshape(-1)
    longest = jnp.max(notes[:, room + more + entries]).astype(jnp.int32)
    found = dot_nn(pick(wanted, owned), table_b).astype(BF)
    found = swap(found.reshape(devices, room, D)).reshape(-1, D)
    if by_kernel:
        places, w_qkv = broadcast(embed_table, block, split, 1)
        w_qkv = w_qkv.reshape(QKV, D)
    else:
        spots = VOCAB + jnp.arange(LENGTH, dtype=jnp.int32) - me * owned
        places = lax.psum(dot_nn(pick(spots, owned), table_b), axis).astype(BF)
        mats_t = lax.all_gather(block, axis, axis=0, tiled=True)
        w_qkv, rest = mats_t[:QKV], mats_t[QKV:]
    rounds = (longest - room + more - 1) // more

    def further(turn):
        key, asked = requests_of(chosen, owner, slot, owned, devices, room + turn * more, more)
        wanted = lax.cond(
            turn == 0,
            lambda: wanted_more,
            lambda: swap(asked.reshape(devices, more)).reshape(-1),
        )
        return key, wanted

    def fetch_more(state):
        turn, extra = state
        key, wanted = further(turn)
        found = dot_nn(pick(wanted, owned), table_b).astype(BF)
        found = swap(found.reshape(devices, more, D)).reshape(-1, D)
        return turn + 1, extra + dot_nn(pick(key, devices * more), found).astype(BF)

    nothing, places = lax.optimization_barrier((jnp.zeros((), BF), places))
    _, extra = lax.while_loop(
        lambda state: state[0] < rounds,
        fetch_more,
        (jnp.int32(0), jnp.broadcast_to(nothing, (rows, D))),
    )

    bias_qkv = jnp.concatenate([vecs[:D], jnp.zeros((D,), F32), vecs[D : 2 * D]])[None]
    bias_up = vecs[5 * D : 5 * D + FF][None]
    small = jnp.concatenate(
        [vecs[2 * D : 5 * D], vecs[5 * D + FF :], jnp.zeros((2 * D,), F32)]
    ).reshape(8, D)

    results = forward(by_kernel, key, found, extra, places, w_qkv, bias_qkv, block, 4)
    inputs, inputs_b, projected, attended, lse = results[:5]
    if by_kernel:
        rest = results[5].reshape(-1, D)
    (
        outputs,
        normed_b,
        hidden_b,
        g_mid_b,
        g_up_b,
        g_first,
        g_first_b,
        g_att_b,
        sums,
    ) = middle(attended, inputs, out_grad, masked[:, None], rest, small, bias_up)
    g_rest = rest_gradients(g_first_b, attended, g_up_b, normed_b, hidden_b, g_mid_b)
    input_grad, g_places, g_qkv, bias_sums, rest_grad = backward(
        by_kernel,
        projected,
        attended,
        g_att_b,
        lse,
        g_first,
        inputs_b,
        w_qkv,
        g_rest.reshape(-1, columns, D),
        2,
    )

    sent = dot_tn(pick(key, devices * room), input_grad).astype(BF)
    g_vecs = jnp.concatenate(
        [
            bias_sums[0],
            bias_sums[1],
            sums[1, :D],
            sums[2, :D],
            sums[3, :D],
            sums[0],
            sums[4, :D],
            sums[5, :D],
            sums[6, :D],
        ]
    )
    vecs_grad = jnp.sum(swap(g_vecs.reshape(devices, entries)), axis=0)
    sent, g_places, g_qkv = lax.optimization_barrier((sent, g_places, g_qkv))
    sent = swap(sent.reshape(devices, room, D)).reshape(-1, D)
    if by_kernel:
        g_own_places, first_grad = homecoming(
            g_places, g_qkv.reshape(-1, columns, D), owned, split, 3
        )
        mats_grad = jnp.where(me < QKV // columns, first_grad, rest_grad).T
    else:
        total = lax.psum(g_places.astype(F32), axis)
        spots = me * owned + jnp.arange(owned, dtype=jnp.int32) - VOCAB
        inside = (spots >= 0) & (spots < LENGTH)
        g_own_places = jnp.where(
            inside[:, None], total[jnp.clip(spots, 0, LENGTH - 1)], 0.0
        )
        mats_grad = lax.psum_scatter(
            jnp.concatenate([g_qkv, g_rest], axis=0), axis, scatter_dimension=0, tiled=True
        )
        mats_grad = mats_grad.astype(F32).T
    table_grad = dot_tn(pick(wanted, owned), sent) + g_own_places

    def send_more(state):
        turn, total = state
        key, wanted = further(turn)
        sent = dot_tn(pick(key, devices * more), input_grad).astype(BF)
        sent = swap(sent.reshape(devices, more, D)).reshape(-1, D)
        return turn + 1, total + dot_tn(pick(wanted, owned), sent)

    _, table_grad = lax.while_loop(
        lambda state: state[0] < rounds, send_more, (jnp.int32(0), table_grad)
    )

    counter = jnp.float32(STEP)
    corr_one = 1.0 - jnp.power(jnp.float32(beta_one), counter)
    corr_two = 1.0 - jnp.power(jnp.float32(beta_two), counter)
    table_step, table_first_next = adam_direction(
        embed_table, table_first, table_second, table_grad, corr_one, corr_two, decay_rate
    )
    mats_step, mats_first_next = adam_direction(
        layer_mats, mats_first, mats_second, mats_grad, corr_one, corr_two, decay_rate
    )
    vecs_step, vecs_first_next = adam_direction(
        layer_vecs, vecs_first, vecs_second, vecs_grad, corr_one, corr_two, 0.0
    )
    return (
        outputs,
        input_grad,
        table_grad,
        mats_grad,
        vecs_grad,
        table_step,
        table_first_next,
        mats_step,
        mats_first_next,
        vecs_step,
        vecs_first_next,
    )


def solution(mesh):
    line = P("fsdp")
    by_rows = P("fsdp", None)
    by_cols = P(None, "fsdp")
    return jax.shard_map(
        functools.partial(body, mesh.shape["fsdp"]),
        mesh=mesh,
        in_specs=(
            line,
            line,
            line,
            line,
            by_rows,
            by_rows,
            by_rows,
            by_rows,
            by_cols,
            by_cols,
            by_cols,
            line,
            line,
            line,
        ),
        out_specs=(
            by_rows,
            by_rows,
            by_rows,
            by_cols,
            line,
            by_rows,
            by_rows,
            by_cols,
            by_cols,
            line,
            line,
        ),
        check_vma=False,
    )
```

```python
import functools

import jax
import jax.numpy as jnp
from jax import lax
from jax.experimental import pallas as pl
from jax.experimental.pallas import tpu as pltpu
from jax.sharding import PartitionSpec as P

D = 768
HEADS = 12
HEAD_DIM = 64
FF = 3072
VOCAB = 14592
LENGTH = 512
STEP = 10
QKV = 3 * D

norm_eps = 1e-12
mask_token = 103
beta_one = 0.9
beta_two = 0.999
adam_eps = 1e-06
decay_rate = 0.01

BF = jnp.bfloat16
F32 = jnp.float32
LOG2E = 1.4426950408889634
SCORE = HEAD_DIM ** (-0.5)
MB = 1024 * 1024

ROW_TILE = 256


def dot_nn(left, right):
    return lax.dot_general(
        left, right, (((1,), (0,)), ((), ())), preferred_element_type=F32
    )


def dot_nt(left, right):
    return lax.dot_general(
        left, right, (((1,), (1,)), ((), ())), preferred_element_type=F32
    )


def dot_tn(left, right):
    return lax.dot_general(
        left, right, (((0,), (0,)), ((), ())), preferred_element_type=F32
    )


def gelu_parts(values):
    size = jnp.abs(values)
    frac = 1.0 / (1.0 + (0.3275911 * 0.7071067811865476) * size)
    expo = jnp.exp2(values * values * (-0.5 * LOG2E))
    poly = 1.061405429 * 0.5
    for coef in (-1.453152027, 1.421413741, -0.284496736, 0.254829592):
        poly = poly * frac + 0.5 * coef
    tail = poly * frac * expo
    cdf = jnp.where(values >= 0, 1.0 - tail, tail)
    return values * cdf, cdf + values * expo * 0.3989422804014327


def norm_parts(total):
    centre = jnp.mean(total, -1, keepdims=True)
    centered = total - centre
    variance = jnp.mean(centered * centered, -1, keepdims=True)
    scale = lax.rsqrt(variance + norm_eps)
    return centered * scale, scale


def norm_back(scaled, unit, scale):
    return scale * (
        scaled
        - jnp.mean(scaled, -1, keepdims=True)
        - unit * jnp.mean(scaled * unit, -1, keepdims=True)
    )


def middle_kernel(
    att_ref,
    x_ref,
    go_ref,
    mask_ref,
    wout_ref,
    up_0,
    up_1,
    up_2,
    up_3,
    down_0,
    down_1,
    down_2,
    down_3,
    vec_ref,
    bup_ref,
    out_ref,
    normed_ref,
    hidden_ref,
    gmid_ref,
    gup_ref,
    gfirst_ref,
    gfirstb_ref,
    gatt_ref,
    sums_ref,
    slope_ref,
):
    @pl.when(pl.program_id(0) == 0)
    def _():
        sums_ref[...] = jnp.zeros_like(sums_ref)

    ups = (up_0, up_1, up_2, up_3)
    downs = (down_0, down_1, down_2, down_3)
    bias_out = vec_ref[0:1, :]
    gain_one = vec_ref[1:2, :]
    shift_one = vec_ref[2:3, :]
    bias_down = vec_ref[3:4, :]
    gain_two = vec_ref[4:5, :]
    shift_two = vec_ref[5:6, :]

    def note(row, values):
        sums_ref[row : row + 1, 0:D] += jnp.sum(values, 0, keepdims=True)

    branch = dot_nt(att_ref[...], wout_ref[...]) + bias_out
    unit_one, scale_one = norm_parts(x_ref[...] + branch)
    normed = unit_one * gain_one + shift_one
    normed_b = normed.astype(BF)
    normed_ref[...] = normed_b
    downward = jnp.zeros(normed.shape, F32)
    for start in range(0, FF, D):
        cols = slice(start, start + D)
        upward = dot_nt(normed_b, ups[start // D][...]) + bup_ref[0:1, cols]
        hidden, slope = gelu_parts(upward)
        slope_ref[:, cols] = slope
        hidden_b = hidden.astype(BF)
        hidden_ref[:, cols] = hidden_b
        downward += dot_nn(hidden_b, downs[start // D][...])
    unit_two, scale_two = norm_parts(normed + downward + bias_down)
    out_ref[...] = (unit_two * gain_two + shift_two).astype(BF)
    g_out = go_ref[...].astype(F32) * mask_ref[...].astype(F32)
    note(5, g_out * unit_two)
    note(6, g_out)
    g_mid = norm_back(g_out * gain_two, unit_two, scale_two)
    note(4, g_mid)
    g_mid_b = g_mid.astype(BF)
    gmid_ref[...] = g_mid_b
    g_normed = g_mid
    for start in range(0, FF, D):
        cols = slice(start, start + D)
        g_up = dot_nt(g_mid_b, downs[start // D][...]) * slope_ref[:, cols]
        sums_ref[0:1, cols] += jnp.sum(g_up, 0, keepdims=True)
        g_up_b = g_up.astype(BF)
        gup_ref[:, cols] = g_up_b
        g_normed += dot_nn(g_up_b, ups[start // D][...])
    note(2, g_normed * unit_one)
    note(3, g_normed)
    g_first = norm_back(g_normed * gain_one, unit_one, scale_one)
    note(1, g_first)
    gfirst_ref[...] = g_first
    g_first_b = g_first.astype(BF)
    gfirstb_ref[...] = g_first_b
    gatt_ref[...] = dot_nn(g_first_b, wout_ref[...]).astype(BF)


def middle(attended, inputs, out_grad, masked, rest, vecs, bias_up):
    rows = attended.shape[0]
    tile = ROW_TILE

    def row(width):
        return pl.BlockSpec((tile, width), lambda i: (i, 0))

    def whole(shape, place=0):
        return pl.BlockSpec(
            shape, lambda i: (place, 0), pipeline_mode=pl.Buffered(buffer_count=1)
        )

    return pl.pallas_call(
        middle_kernel,
        grid=(rows // tile,),
        in_specs=[
            row(D),
            row(D),
            row(D),
            row(1),
            *[whole((D, D), place) for place in range(9)],
            whole((8, D)),
            whole((1, FF)),
        ],
        out_specs=[
            row(D),
            row(D),
            row(FF),
            row(D),
            row(FF),
            row(D),
            row(D),
            row(D),
            pl.BlockSpec((8, FF), lambda i: (0, 0)),
        ],
        out_shape=[
            jax.ShapeDtypeStruct((rows, D), BF),
            jax.ShapeDtypeStruct((rows, D), BF),
            jax.ShapeDtypeStruct((rows, FF), BF),
            jax.ShapeDtypeStruct((rows, D), BF),
            jax.ShapeDtypeStruct((rows, FF), BF),
            jax.ShapeDtypeStruct((rows, D), F32),
            jax.ShapeDtypeStruct((rows, D), BF),
            jax.ShapeDtypeStruct((rows, D), BF),
            jax.ShapeDtypeStruct((8, FF), F32),
        ],
        scratch_shapes=[pltpu.VMEM((tile, FF), F32)],
        compiler_params=pltpu.CompilerParams(vmem_limit_bytes=56 * MB),
        name="middle",
    )(attended, inputs, out_grad, masked, *[rest] * 9, vecs, bias_up)


def fixed(shape, place=0):
    return pl.BlockSpec(
        shape, lambda i: (place, 0), pipeline_mode=pl.Buffered(buffer_count=1)
    )


def rest_kernel(first_ref, att_ref, up_ref, normed_ref, hidden_ref, mid_ref, out_ref):
    step = pl.program_id(0)
    chunks = FF // D

    @pl.when(step == 0)
    def _():
        out_ref[...] = dot_tn(first_ref[...], att_ref[...]).astype(BF)

    @pl.when(jnp.logical_and(step > 0, step <= chunks))
    def _():
        out_ref[...] = dot_tn(up_ref[...], normed_ref[...]).astype(BF)

    @pl.when(step > chunks)
    def _():
        out_ref[...] = dot_tn(hidden_ref[...], mid_ref[...]).astype(BF)


def rest_gradients(g_first_b, attended, g_up_b, normed_b, hidden_b, g_mid_b):
    rows = attended.shape[0]
    chunks = FF // D
    full = fixed((rows, D))
    return pl.pallas_call(
        rest_kernel,
        grid=(1 + 2 * chunks,),
        in_specs=[
            full,
            full,
            pl.BlockSpec((rows, D), lambda i: (0, jnp.clip(i - 1, 0, chunks - 1))),
            full,
            pl.BlockSpec((rows, D), lambda i: (0, jnp.clip(i - 1 - chunks, 0, chunks - 1))),
            full,
        ],
        out_specs=pl.BlockSpec((D, D), lambda i: (i, 0)),
        out_shape=jax.ShapeDtypeStruct((D + 2 * FF, D), BF),
        compiler_params=pltpu.CompilerParams(vmem_limit_bytes=56 * MB),
        cost_estimate=pl.CostEstimate(
            flops=22_000_000_000, bytes_accessed=50_000_000, transcendentals=0
        ),
        name="rest_gradients",
    )(g_first_b, attended, g_up_b, normed_b, hidden_b, g_mid_b)


MESH = pl.DeviceIdType.MESH
PLANES = 4


def neighbours():
    me = lax.axis_index("fsdp")
    core = lax.rem(me, 2)
    x = lax.rem(me // 2, 2)
    y = lax.rem(me // 4, 2)
    z = me // 8
    step_a = 4 - 2 * core
    step_b = 2 + 2 * core
    a = jnp.where(core == 0, y, x)
    b = jnp.where(core == 0, x, y)
    near_a = me + step_a * (1 - 2 * a)
    near_b = me + step_b * (1 - 2 * b)
    twin = me + 1 - 2 * core
    return me, core, z, a, b, step_a, step_b, near_a, near_b, twin


def greet(me, z, near_a, near_b, twin):
    barrier = pltpu.get_barrier_semaphore()

    def hello(device):
        pl.semaphore_signal(barrier, inc=1, device_id=(device,), device_id_type=MESH)

    for device in (near_a, near_b, twin):
        hello(device)

    @pl.when(z > 0)
    def _():
        hello(me - 8)

    @pl.when(z < PLANES - 1)
    def _():
        hello(me + 8)

    inner = jnp.logical_and(z > 0, z < PLANES - 1)
    pl.semaphore_wait(barrier, jnp.where(inner, 5, 4))


class RestSpread:
    def __init__(self, in_ref, out_ref, scratch):
        self.in_ref, self.out_ref = in_ref, out_ref
        self.own_sem, self.send_sem, self.recv_sem = scratch
        self.place = neighbours()

    @staticmethod
    def scratch():
        return [
            pltpu.SemaphoreType.DMA,
            pltpu.SemaphoreType.DMA((5, 24)),
            pltpu.SemaphoreType.DMA((24,)),
        ]

    def copy(self, shard, device, kind, source=None):
        return pltpu.make_async_remote_copy(
            src_ref=self.out_ref.at[shard] if source is None else source,
            dst_ref=self.out_ref.at[shard],
            send_sem=self.send_sem.at[kind, shard],
            recv_sem=self.recv_sem.at[shard],
            device_id=(device,),
            device_id_type=MESH,
        )

    def shard(self, plane, other_a, other_b):
        me, core, z, a, b, step_a, step_b, near_a, near_b, twin = self.place
        a_at = 1 - a if other_a else a
        b_at = 1 - b if other_b else b
        return jnp.maximum(plane - 1, 0) * 8 + a_at * step_a + b_at * step_b + core

    def planes(self, far):
        z = self.place[2]
        for way in (1, -1) if far else (1,):
            plane = z - way * far
            yield way, plane, jnp.logical_and(plane >= 1, plane < PLANES)

    def routes(self, far):
        me, core, z, a, b, step_a, step_b, near_a, near_b, twin = self.place
        for way, plane, there in self.planes(far):
            shard = self.shard(plane, False, False)
            for onward in (way,) if far else (1, -1):
                goes = jnp.logical_and(z + onward >= 0, z + onward < PLANES)
                yield (
                    jnp.logical_and(there, goes),
                    shard,
                    me + 8 * onward,
                    0 if onward == 1 else 1,
                )
            yield there, shard, near_b, 3
            yield there, shard, near_a, 2
            yield there, shard, twin, 4

    def routes_a(self, far):
        near_b, twin = self.place[8:]
        for way, plane, there in self.planes(far):
            shard = self.shard(plane, True, False)
            yield there, shard, near_b, 3
            yield there, shard, twin, 4

    def routes_b(self, far):
        twin = self.place[9]
        for way, plane, there in self.planes(far):
            for other_a in (False, True):
                yield there, self.shard(plane, other_a, True), twin, 4

    def own(self):
        return pltpu.make_async_copy(
            self.in_ref, self.out_ref.at[self.shard(self.place[2], False, False)], self.own_sem
        )

    def start(self):
        me, core, z, a, b, step_a, step_b, near_a, near_b, twin = self.place
        greet(me, z, near_a, near_b, twin)

        @pl.when(z > 0)
        def _():
            self.own().start()

        for goes, shard, device, kind in self.routes(0):
            pl.when(goes)(
                lambda shard=shard, device=device, kind=kind: self.copy(
                    shard, device, kind, self.in_ref
                ).start()
            )

    def pass_on(self, routes):
        seen = []
        for goes, shard, device, kind in routes:
            if kind == 4:
                seen.append((goes, shard))
        for goes, shard in seen:
            pl.when(goes)(
                lambda shard=shard: self.copy(shard, self.place[9], 4).wait_recv()
            )
            for other, place, device, kind in routes:
                if place is shard:
                    pl.when(other)(
                        lambda shard=shard, device=device, kind=kind: self.copy(
                            shard, device, kind
                        ).start()
                    )

    def column(self, far):
        self.pass_on(list(self.routes(far)))

    def along_a(self, far):
        self.pass_on(list(self.routes_a(far)))

    def along_b(self, far):
        self.pass_on(list(self.routes_b(far)))

    def end(self):
        me, core, z, a, b, step_a, step_b, near_a, near_b, twin = self.place

        def from_twin(place, carry):
            self.copy(place * 2 + 1 - core, twin, 4).wait_recv()
            return carry

        lax.fori_loop(0, 12, from_twin, 0)
        for far in range(PLANES):
            for routes in (self.routes(far), self.routes_a(far), self.routes_b(far)):
                for goes, shard, device, kind in routes:
                    pl.when(goes)(
                        lambda shard=shard, device=device, kind=kind: self.copy(
                            shard, device, kind
                        ).wait_send()
                    )

        @pl.when(z > 0)
        def _():
            self.own().wait()

    def schedule(self):
        return {
            0: [self.start],
            6: [lambda: self.column(1)],
            8: [lambda: self.along_a(0)],
            10: [lambda: self.column(2)],
            14: [lambda: self.along_a(1)],
            15: [lambda: self.column(3)],
            18: [lambda: self.along_a(2)],
            22: [lambda: self.along_a(3)],
            24: [lambda: self.along_b(0)],
            25: [lambda: self.along_b(1)],
            26: [lambda: self.along_b(2)],
            27: [lambda: self.along_b(3), self.end],
        }


class RestSums:
    TURNS = PLANES - 1

    def __init__(self, in_ref, out_ref, scratch):
        self.in_ref, self.out_ref = in_ref, out_ref
        (
            self.own,
            self.from_twin,
            self.from_b,
            self.from_a,
            self.from_low,
            self.from_high,
            self.load_sem,
            self.twin_sem,
            self.b_sem,
            self.a_sem,
            self.low_sem,
            self.high_sem,
        ) = scratch
        self.place = neighbours()

    @staticmethod
    def scratch(shape):
        return [
            pltpu.VMEM((12,) + shape, BF),
            pltpu.VMEM((12,) + shape, BF),
            pltpu.VMEM((6,) + shape, BF),
            pltpu.VMEM((3,) + shape, BF),
            pltpu.VMEM((4,) + shape, BF),
            pltpu.VMEM((4,) + shape, BF),
            pltpu.SemaphoreType.DMA((12,)),
            pltpu.SemaphoreType.DMA((2, 12)),
            pltpu.SemaphoreType.DMA((2, 6)),
            pltpu.SemaphoreType.DMA((2, 3)),
            pltpu.SemaphoreType.DMA((2, 4)),
            pltpu.SemaphoreType.DMA((2, 4)),
        ]

    def remote(self, source, target, sems, slot, device):
        return pltpu.make_async_remote_copy(
            src_ref=source,
            dst_ref=target.at[slot],
            send_sem=sems.at[0, slot],
            recv_sem=sems.at[1, slot],
            device_id=(device,),
            device_id_type=MESH,
        )

    def plane_of(self, turn):
        z = self.place[2]
        last = PLANES - 1 - turn
        inner = (1, 3, 2)[turn]
        return jnp.where(z < 2, last, jnp.where(z == 2, inner, 1 + turn))

    def shards(self, slot):
        me, core, z, a, b, step_a, step_b, near_a, near_b, twin = self.place
        other_b, turn, other_a = slot < 6, slot % 6 // 2, slot % 2 == 0
        base = (self.plane_of(turn) - 1) * 8
        a_at = 1 - a if other_a else a
        b_at = 1 - b if other_b else b
        mine = base + a_at * step_a + b_at * step_b + core
        a_at = 1 - b if other_a else b
        b_at = 1 - a if other_b else a
        twins = base + a_at * step_b + b_at * step_a + 1 - core
        return mine, twins

    def load(self, slot):
        return pltpu.make_async_copy(
            self.in_ref.at[self.shards(slot)[0]], self.own.at[slot], self.load_sem.at[slot]
        )

    def gift(self, slot):
        return self.remote(
            self.in_ref.at[self.shards(slot)[1]],
            self.from_twin,
            self.twin_sem,
            slot,
            self.place[9],
        )

    def over_b(self, slot):
        return self.remote(self.own.at[slot], self.from_b, self.b_sem, slot, self.place[8])

    def over_a(self, turn):
        return self.remote(
            self.own.at[6 + 2 * turn], self.from_a, self.a_sem, turn, self.place[7]
        )

    def along(self, turn, up):
        plane = self.plane_of(turn)
        source = self.own.at[7 + 2 * turn]
        if up:
            return self.remote(source, self.from_low, self.low_sem, plane, self.place[0] + 8)
        return self.remote(source, self.from_high, self.high_sem, plane, self.place[0] - 8)

    def add(self, slot, arrived):
        self.own[slot] = self.own[slot] + arrived[...]

    def start(self):
        me, core, z, a, b, step_a, step_b, near_a, near_b, twin = self.place
        greet(me, z, near_a, near_b, twin)
        for slot in (0, 1, 2, 3, 6, 7, 4, 5, 8, 9, 10, 11):
            self.gift(slot).start()
            self.load(slot).start()

    def far(self, turn):
        for slot in (2 * turn, 2 * turn + 1):
            self.load(slot).wait()
            self.gift(slot).wait_recv()
            self.add(slot, self.from_twin.at[slot])
            self.over_b(slot).start()

    def near(self, turn):
        for slot in (6 + 2 * turn, 7 + 2 * turn):
            self.load(slot).wait()
            self.gift(slot).wait_recv()
            self.add(slot, self.from_twin.at[slot])

    def stage_b(self, turn):
        for slot in (2 * turn, 2 * turn + 1):
            self.over_b(slot).wait_recv()
            self.add(6 + slot, self.from_b.at[slot])
        self.over_a(turn).start()

    def stage_a(self, turn):
        z = self.place[2]
        slot = 7 + 2 * turn
        self.over_a(turn).wait_recv()
        self.add(slot, self.from_a.at[turn])

        @pl.when(z == 0)
        def _():
            self.along(turn, True).start()

        if turn < 2:

            @pl.when(z == PLANES - 1)
            def _():
                self.along(turn, False).start()

    def stage_z(self, turn):
        z = self.place[2]
        slot = 7 + 2 * turn
        plane = self.plane_of(turn)
        if turn < 2:
            inner = jnp.logical_and(z > 0, z < PLANES - 1)

            @pl.when(jnp.logical_and(inner, plane > z))
            def _():
                self.along(turn, True).wait_recv()
                self.add(slot, self.from_low.at[plane])
                self.along(turn, True).start()

            @pl.when(jnp.logical_and(inner, plane < z))
            def _():
                self.along(turn, False).wait_recv()
                self.add(slot, self.from_high.at[plane])
                self.along(turn, False).start()

            return

        @pl.when(z > 0)
        def _():
            self.along(turn, True).wait_recv()
            self.out_ref[...] = self.own[slot].astype(F32) + self.from_low[plane].astype(F32)

        @pl.when(jnp.logical_and(z > 0, z < PLANES - 1))
        def _():
            self.along(turn, False).wait_recv()
            self.out_ref[...] += self.from_high[plane].astype(F32)

    def end(self):
        z = self.place[2]
        for slot in range(12):
            self.gift(slot).wait_send()
        for slot in range(6):
            self.over_b(slot).wait_send()
        for turn in range(self.TURNS):
            self.over_a(turn).wait_send()
            plane = self.plane_of(turn)

            @pl.when(plane > z)
            def _(turn=turn):
                self.along(turn, True).wait_send()

            @pl.when(plane < z)
            def _(turn=turn):
                self.along(turn, False).wait_send()

    def schedule(self):
        return {
            0: [self.start],
            2: [lambda: self.far(0)],
            3: [lambda: self.near(0)],
            6: [lambda: self.far(1)],
            7: [lambda: self.near(1)],
            8: [lambda: self.stage_b(0)],
            9: [lambda: self.far(2)],
            10: [lambda: self.near(2)],
            14: [lambda: self.stage_b(1), lambda: self.stage_a(0)],
            18: [lambda: self.stage_b(2)],
            19: [lambda: self.stage_a(1)],
            20: [lambda: self.stage_z(0)],
            22: [lambda: self.stage_a(2)],
            24: [lambda: self.stage_z(1)],
            27: [lambda: self.stage_z(2), self.end],
        }


PIECES = 4
CHUNKS = 3


def broadcast_kernel(
    split,
    table_ref,
    block_ref,
    out_ref,
    w_ref,
    stage,
    own_sem,
    load_sem,
    send_sem,
    recv_sem,
    w_send,
    w_recv,
):
    first_owner, first_row, count = split
    me, core, z, a, b, step_a, step_b, near_a, near_b, twin = neighbours()
    greet(me, z, near_a, near_b, twin)
    rows = LENGTH // PIECES
    height = block_ref.shape[0] // CHUNKS
    root = first_owner + 1
    gift = pltpu.make_async_remote_copy(
        src_ref=table_ref.at[pl.ds(first_row, count)],
        dst_ref=stage.at[pl.ds(0, count)],
        send_sem=load_sem.at[0],
        recv_sem=load_sem.at[1],
        device_id=(root,),
        device_id_type=MESH,
    )
    mine = pltpu.make_async_copy(
        table_ref.at[pl.ds(0, LENGTH - count)],
        stage.at[pl.ds(count, LENGTH - count)],
        load_sem.at[2],
    )
    shard = lax.rem(me, 8)
    own = pltpu.make_async_copy(block_ref, w_ref.at[shard], own_sem)

    @pl.when(me == first_owner)
    def _():
        gift.start()

    @pl.when(me == root)
    def _():
        mine.start()

    @pl.when(z == 0)
    def _():
        own.start()

    def copy(piece, device, kind):
        part = pl.ds(piece * rows, rows)
        return pltpu.make_async_remote_copy(
            src_ref=out_ref.at[part],
            dst_ref=out_ref.at[part],
            send_sem=send_sem.at[kind, piece],
            recv_sem=recv_sem.at[piece],
            device_id=(device,),
            device_id_type=MESH,
        )

    def block(place, chunk, device, kind, source=None):
        part = pl.ds(chunk * height, height)
        return pltpu.make_async_remote_copy(
            src_ref=w_ref.at[place, part] if source is None else source.at[part],
            dst_ref=w_ref.at[place, part],
            send_sem=w_send.at[kind, place, chunk],
            recv_sem=w_recv.at[place, chunk],
            device_id=(device,),
            device_id_type=MESH,
        )

    trunk = jnp.logical_and(core == 1, jnp.logical_and(a == 1, b == 1))
    branch = jnp.logical_and(core == 1, jnp.logical_and(a == 0, b == 1))
    routes = (
        (jnp.logical_and(trunk, z > 0), me - 8),
        (trunk, near_a),
        (jnp.logical_or(trunk, branch), near_b),
        (core == 1, twin),
    )
    shard_a = (1 - a) * step_a + b * step_b + core
    shards_b = [
        a * step_a + (1 - b) * step_b + core,
        (1 - a) * step_a + (1 - b) * step_b + core,
    ]

    def sends(chunk, source):
        pl.when(z < PLANES - 1)(lambda: block(shard, chunk, me + 8, 0, source).start())
        block(shard, chunk, near_b, 1, source).start()
        block(shard, chunk, near_a, 2, source).start()
        block(shard, chunk, twin, 3, source).start()

    def from_own(chunk):
        @pl.when(z > 0)
        def _():
            block(shard, chunk, twin, 3).wait_recv()
            sends(chunk, None)

    def from_a(chunk):
        block(shard_a, chunk, twin, 3).wait_recv()
        block(shard_a, chunk, near_b, 1).start()
        block(shard_a, chunk, twin, 3).start()

    def from_b(chunk):
        for place in shards_b:
            block(place, chunk, twin, 3).wait_recv()
            block(place, chunk, twin, 3).start()

    def pass_on(piece):
        for kind, (goes, device) in enumerate(routes):
            pl.when(goes)(lambda kind=kind, device=device: copy(piece, device, kind).start())

    def positions(piece):
        @pl.when(me != root)
        def _():
            copy(piece, twin, 3).wait_recv()
            pass_on(piece)

    @pl.when(z == 0)
    def _():
        for chunk in range(CHUNKS):
            sends(chunk, block_ref)

    @pl.when(me == root)
    def _():
        mine.wait()
        gift.wait_recv()
        for piece in range(PIECES):
            part = slice(piece * rows, (piece + 1) * rows)
            out_ref[part, :] = stage[part, :].astype(BF)
            pass_on(piece)

    from_own(0)
    from_own(1)
    from_a(0)
    from_own(2)
    from_a(1)
    from_b(0)
    from_a(2)
    positions(0)
    from_b(1)
    positions(1)
    positions(2)
    positions(3)
    from_b(2)

    def from_twin(place, carry):
        for chunk in range(CHUNKS):
            block(place * 2 + 1 - core, chunk, twin, 3).wait_recv()
        return carry

    lax.fori_loop(0, 4, from_twin, 0)
    for piece in range(PIECES):
        for kind, (goes, device) in enumerate(routes):
            pl.when(goes)(
                lambda piece=piece, kind=kind, device=device: copy(
                    piece, device, kind
                ).wait_send()
            )
    for chunk in range(CHUNKS):

        @pl.when(z < PLANES - 1)
        def _(chunk=chunk):
            block(shard, chunk, me + 8, 0).wait_send()

        block(shard, chunk, near_b, 1).wait_send()
        block(shard, chunk, near_a, 2).wait_send()
        block(shard, chunk, twin, 3).wait_send()
        block(shard_a, chunk, near_b, 1).wait_send()
        block(shard_a, chunk, twin, 3).wait_send()
        for place in shards_b:
            block(place, chunk, twin, 3).wait_send()

    @pl.when(me == first_owner)
    def _():
        gift.wait_send()

    @pl.when(z == 0)
    def _():
        own.wait()


def place_split(devices, owned):
    first_owner = VOCAB // owned
    first_row = VOCAB - first_owner * owned
    return first_owner, first_row, owned - first_row


def broadcast(table, block, split, ident):
    return pl.pallas_call(
        functools.partial(broadcast_kernel, split),
        in_specs=[pl.BlockSpec(memory_space=pl.ANY)] * 2,
        out_specs=[
            pl.BlockSpec(memory_space=pltpu.VMEM),
            pl.BlockSpec(memory_space=pl.ANY),
        ],
        out_shape=[
            jax.ShapeDtypeStruct((LENGTH, D), BF),
            jax.ShapeDtypeStruct((8,) + block.shape, BF),
        ],
        scratch_shapes=[
            pltpu.VMEM((LENGTH, D), F32),
            pltpu.SemaphoreType.DMA,
            pltpu.SemaphoreType.DMA((3,)),
            pltpu.SemaphoreType.DMA((4, PIECES)),
            pltpu.SemaphoreType.DMA((PIECES,)),
            pltpu.SemaphoreType.DMA((4, 8, CHUNKS)),
            pltpu.SemaphoreType.DMA((8, CHUNKS)),
        ],
        compiler_params=pltpu.CompilerParams(collective_id=ident, has_side_effects=True),
        cost_estimate=pl.CostEstimate(flops=0, bytes_accessed=100_000_000, transcendentals=0),
        name="broadcast",
    )(table, block)


def homecoming_kernel(
    split,
    place_ref,
    first_ref,
    vec_ref,
    out_ref,
    mats_ref,
    vec_sum_ref,
    sums,
    from_twin,
    from_b,
    from_a,
    from_z,
    ready,
    own,
    own_twin,
    own_b,
    own_a,
    own_high,
    sems,
    z_sem,
    piece_sem,
    home_sem,
    load_sem,
    twin_sem,
    b_sem,
    a_sem,
    high_sem,
    vec_in,
    vec_sem,
):
    first_owner, first_row, count = split
    root = first_owner + 1
    me, core, z, a, b, step_a, step_b, near_a, near_b, twin = neighbours()
    rows = place_ref.shape[4]
    height = first_ref.shape[1] // CHUNKS
    out_ref[...] = jnp.zeros_like(out_ref)
    barrier = pltpu.get_barrier_semaphore()

    def each(step, carry):
        pl.semaphore_signal(
            barrier, inc=1, device_id=(lax.rem(me + step, 32),), device_id_type=MESH
        )
        return carry

    lax.fori_loop(1, 32, each, 0)
    pl.semaphore_wait(barrier, 31)

    def remote(source, target, send, receive, device):
        return pltpu.make_async_remote_copy(
            src_ref=source,
            dst_ref=target,
            send_sem=send,
            recv_sem=receive,
            device_id=(device,),
            device_id_type=MESH,
        )

    def add(total, extra):
        return (total.astype(F32) + extra.astype(F32)).astype(BF)

    x = jnp.where(core == 0, b, a)
    y = jnp.where(core == 0, a, b)
    gift = remote(place_ref.at[:, :, :, 1 - core], from_twin, sems.at[0, 0], sems.at[0, 1], twin)
    gift.start()
    loads, gifts = [], []
    for slot in range(4):
        other_b, other_a = slot < 2, slot % 2 == 0
        a_at, b_at = (1 - a if other_a else a), (1 - b if other_b else b)
        shard = a_at * step_a + b_at * step_b + core
        loads.append(pltpu.make_async_copy(first_ref.at[shard], own.at[slot], load_sem.at[slot]))
        a_at, b_at = (1 - b if other_a else b), (1 - a if other_b else a)
        shard = a_at * step_b + b_at * step_a + 1 - core
        gifts.append(
            remote(
                first_ref.at[shard],
                own_twin.at[slot],
                twin_sem.at[0, slot],
                twin_sem.at[1, slot],
                twin,
            )
        )
    for slot in range(4):
        gifts[slot].start()
        loads[slot].start()

    def vec_copy(source, target, device):
        return remote(
            vec_ref.at[source],
            vec_in.at[target],
            vec_sem.at[0, source],
            vec_sem.at[1, target],
            device,
        )

    def vec_start(step, carry):
        device = lax.rem(me + step, 32)
        vec_copy(device, me, device).start()
        return carry

    def vec_wait(step, carry):
        device = lax.rem(me + step, 32)
        vec_copy(device, device, device).wait_recv()
        vec_copy(device, device, device).wait_send()
        return carry

    lax.fori_loop(1, 32, vec_start, 0)
    vec_in[me] = vec_ref[me]
    gift.wait_recv()
    sums[...] = add(place_ref[:, :, :, core], from_twin[...])

    @pl.when(core == 0)
    def _():
        remote(sums.at[:, :, 1 - x], from_b, sems.at[1, 0], sems.at[1, 1], near_b).start()

    @pl.when(core == 1)
    def _():
        remote(sums.at[:, 1 - y], from_b, sems.at[1, 0], sems.at[1, 1], near_b).start()

    over_b = [
        remote(own.at[slot], own_b.at[slot], b_sem.at[0, slot], b_sem.at[1, slot], near_b)
        for slot in range(2)
    ]
    for slot in range(4):
        loads[slot].wait()
        gifts[slot].wait_recv()
        own[slot] = add(own[slot], own_twin[slot])
        if slot < 2:
            over_b[slot].start()

    small_b = remote(sums.at[:, 0], from_b, sems.at[1, 0], sems.at[1, 1], near_b)
    small_b.wait_recv()

    @pl.when(core == 0)
    def _():
        from_b[...] = add(sums[:, :, x], from_b[...])

    @pl.when(core == 1)
    def _():
        from_b[...] = add(sums[:, y], from_b[...])

    small_a = remote(from_b.at[:, 1 - a], from_a, sems.at[2, 0], sems.at[2, 1], near_a)
    small_a.start()
    over_a = remote(own.at[2], own_a, a_sem.at[0], a_sem.at[1], near_a)
    for slot in range(2):
        over_b[slot].wait_recv()
        own[2 + slot] = add(own[2 + slot], own_b[slot])
        if slot == 0:
            over_a.start()
    small_a.wait_recv()
    from_a[...] = add(from_b[:, a], from_a[...])

    def column(plane, action):
        @pl.when(plane != z)
        def _():
            action(
                remote(
                    from_a.at[plane],
                    from_z.at[z],
                    z_sem.at[0, plane],
                    z_sem.at[1, z],
                    me + 8 * (plane - z),
                )
            )

    for plane in range(PLANES):
        column(plane, lambda item: item.start())
    over_a.wait_recv()

    def down(chunk):
        part = pl.ds(chunk * height, height)
        return remote(
            own.at[3, part],
            own_high.at[part],
            high_sem.at[0, chunk],
            high_sem.at[1, chunk],
            me - 8,
        )

    for chunk in range(CHUNKS):
        part = pl.ds(chunk * height, height)
        own[3, part] = add(own[3, part], own_a[part])

        @pl.when(z < PLANES - 1)
        def _(chunk=chunk, part=part):
            down(chunk).wait_recv()
            own[3, part] = add(own[3, part], own_high[part])

        @pl.when(z > 0)
        def _(chunk=chunk):
            down(chunk).start()

    mats_ref[...] = own[3].astype(F32)
    ready[...] = from_a[z].astype(F32)
    for plane in range(PLANES):

        @pl.when(plane != z)
        def _(plane=plane):
            remote(
                from_a.at[plane], from_z.at[plane], z_sem.at[0, plane], z_sem.at[1, plane], twin
            ).wait_recv()
            ready[...] += from_z[plane].astype(F32)

    def home(device, half):
        place = device * rows + half * 8
        early = place < count
        owner = jnp.where(early, first_owner, root)
        spot = pl.multiple_of(jnp.where(early, first_row + place, place - count), 8)
        return owner, spot

    def piece(device, half):
        owner, spot = home(device, half)
        return remote(
            ready.at[pl.ds(half * 8, 8)],
            out_ref.at[pl.ds(spot, 8)],
            piece_sem.at[half],
            home_sem.at[device * 2 + half],
            owner,
        )

    for half in range(2):
        owner, spot = home(me, half)

        @pl.when(owner == me)
        def _(half=half, spot=spot):
            out_ref[pl.ds(spot, 8), :] = ready[half * 8 : half * 8 + 8, :]

        @pl.when(owner != me)
        def _(half=half):
            piece(me, half).start()

    def arrive(index, carry):
        device, half = index // 2, lax.rem(index, 2)
        owner, _ = home(device, half)

        @pl.when(jnp.logical_and(owner == me, device != me))
        def _():
            piece(device, half).wait_recv()

        return carry

    @pl.when(me >= first_owner)
    def _():
        lax.fori_loop(0, 64, arrive, 0)

    for half in range(2):
        owner, _ = home(me, half)

        @pl.when(owner != me)
        def _(half=half):
            piece(me, half).wait_send()

    lax.fori_loop(1, 32, vec_wait, 0)
    vec_sum_ref[...] = jnp.sum(vec_in[...], axis=0)
    for item in [gift, small_b, small_a, over_a] + gifts + over_b:
        item.wait_send()
    for plane in range(PLANES):
        column(plane, lambda item: item.wait_send())
    for chunk in range(CHUNKS):

        @pl.when(z > 0)
        def _(chunk=chunk):
            down(chunk).wait_send()


def homecoming(place_sums, first, vecs, owned, split, ident):
    rows = LENGTH // 32
    small = (rows, D)
    shape = first.shape[1:]
    return pl.pallas_call(
        functools.partial(homecoming_kernel, split),
        in_specs=[
            pl.BlockSpec(memory_space=pltpu.VMEM),
            pl.BlockSpec(memory_space=pl.ANY),
            pl.BlockSpec(memory_space=pltpu.VMEM),
        ],
        out_specs=[pl.BlockSpec(memory_space=pltpu.VMEM)] * 3,
        out_shape=[
            jax.ShapeDtypeStruct((owned, D), F32),
            jax.ShapeDtypeStruct(shape, F32),
            jax.ShapeDtypeStruct(vecs.shape[1:], F32),
        ],
        scratch_shapes=[
            pltpu.VMEM((4, 2, 2) + small, BF),
            pltpu.VMEM((4, 2, 2) + small, BF),
            pltpu.VMEM((4, 2) + small, BF),
            pltpu.VMEM((4,) + small, BF),
            pltpu.VMEM((4,) + small, BF),
            pltpu.VMEM(small, F32),
            pltpu.VMEM((4,) + shape, BF),
            pltpu.VMEM((4,) + shape, BF),
            pltpu.VMEM((2,) + shape, BF),
            pltpu.VMEM(shape, BF),
            pltpu.VMEM(shape, BF),
            pltpu.SemaphoreType.DMA((3, 2)),
            pltpu.SemaphoreType.DMA((2, 4)),
            pltpu.SemaphoreType.DMA((2,)),
            pltpu.SemaphoreType.DMA((64,)),
            pltpu.SemaphoreType.DMA((4,)),
            pltpu.SemaphoreType.DMA((2, 4)),
            pltpu.SemaphoreType.DMA((2, 2)),
            pltpu.SemaphoreType.DMA((2,)),
            pltpu.SemaphoreType.DMA((2, CHUNKS)),
            pltpu.VMEM(vecs.shape, F32),
            pltpu.SemaphoreType.DMA((2, 32)),
        ],
        compiler_params=pltpu.CompilerParams(
            collective_id=ident, has_side_effects=True, vmem_limit_bytes=40 * MB
        ),
        cost_estimate=pl.CostEstimate(
            flops=0, bytes_accessed=200_000_000, transcendentals=0
        ),
        name="homecoming",
    )(place_sums.reshape((4, 2, 2, 2) + small), first, vecs)


def forward_kernel(
    by_kernel,
    key_ref,
    found_ref,
    extra_ref,
    place_ref,
    w_ref,
    bias_ref,
    block_ref,
    x_ref,
    xb_ref,
    proj_ref,
    att_ref,
    lse_ref,
    *scratch,
):
    seq, head = pl.program_id(0), pl.program_id(1)
    pairs = HEADS // 2
    step = seq * (pairs + 1) + head
    if by_kernel:
        gather = RestSpread(block_ref, scratch[0], scratch[1:])
        for when, actions in gather.schedule().items():

            @pl.when(step == when)
            def _(actions=actions):
                for action in actions:
                    action()

    @pl.when(head == 0)
    def _():
        slots = lax.broadcasted_iota(jnp.int32, (LENGTH, found_ref.shape[0]), 1)
        picked = (key_ref[...] == slots).astype(BF)
        inputs = dot_nn(picked, found_ref[...]) + extra_ref[...].astype(F32)
        inputs = inputs + place_ref[...].astype(F32)
        x_ref[...] = inputs
        inputs_b = inputs.astype(BF)
        xb_ref[...] = inputs_b
        for start in range(0, QKV, D):
            cols = slice(start, start + D)
            part = dot_nt(inputs_b, w_ref[cols, :]) + bias_ref[:, cols]
            proj_ref[:, cols] = part.astype(BF)

    @pl.when(head > 0)
    def _():
        width = 2 * HEAD_DIM
        start = (head - 1) * width
        query = proj_ref[:, pl.ds(pl.multiple_of(start, width), width)]
        keys = proj_ref[:, pl.ds(pl.multiple_of(D + start, width), width)]
        values_t = proj_ref[:, pl.ds(pl.multiple_of(2 * D + start, width), width)].T
        lane = lax.broadcasted_iota(jnp.int32, query.shape, 1)
        outs = []
        for half in range(2):
            mine = (lane < HEAD_DIM) if half == 0 else (lane >= HEAD_DIM)
            picked = jnp.where(mine, query, jnp.zeros_like(query))
            scores = dot_nt(keys, picked)
            highest = jnp.max(scores, 0, keepdims=True)
            expo = jnp.exp2((scores - highest) * (SCORE * LOG2E))
            total = jnp.sum(expo, 0, keepdims=True)
            part = values_t[half * HEAD_DIM : (half + 1) * HEAD_DIM, :]
            outs.append(dot_nn(part, expo.astype(BF)) / total)
            lse_ref[0, half : half + 1, :] = highest * (SCORE * LOG2E) + jnp.log2(total)
        att_ref[...] = jnp.concatenate(outs, 0).T.astype(BF)


def forward(by_kernel, key, found, extra, places, w_qkv, bias, block, ident):
    rows = key.shape[0]
    seqs = rows // LENGTH
    pairs = HEADS // 2
    slots = found.shape[0]

    def row(width):
        return pl.BlockSpec((LENGTH, width), lambda s, h: (s, 0))

    def steady(shape):
        return pl.BlockSpec(
            shape, lambda s, h: (0, 0), pipeline_mode=pl.Buffered(buffer_count=1)
        )

    out_specs = [
        row(D),
        row(D),
        row(QKV),
        pl.BlockSpec((LENGTH, 2 * HEAD_DIM), lambda s, h: (s, jnp.maximum(h - 1, 0))),
        pl.BlockSpec(
            (1, 2, LENGTH), lambda s, h: (s * pairs + jnp.maximum(h - 1, 0), 0, 0)
        ),
    ]
    out_shape = [
        jax.ShapeDtypeStruct((rows, D), F32),
        jax.ShapeDtypeStruct((rows, D), BF),
        jax.ShapeDtypeStruct((rows, QKV), BF),
        jax.ShapeDtypeStruct((rows, D), BF),
        jax.ShapeDtypeStruct((seqs * pairs, 2, LENGTH), F32),
    ]
    params = {}
    scratch = []
    if by_kernel:
        out_specs.append(pl.BlockSpec(memory_space=pl.ANY))
        out_shape.append(jax.ShapeDtypeStruct((24,) + block.shape, BF))
        params = dict(collective_id=ident, has_side_effects=True)
        scratch = RestSpread.scratch()
    return pl.pallas_call(
        functools.partial(forward_kernel, by_kernel),
        grid=(seqs, pairs + 1),
        in_specs=[
            row(1),
            steady((slots, D)),
            row(D),
            steady((LENGTH, D)),
            steady((QKV, D)),
            steady((1, QKV)),
            pl.BlockSpec(memory_space=pl.ANY),
        ],
        out_specs=out_specs,
        out_shape=out_shape,
        scratch_shapes=scratch,
        compiler_params=pltpu.CompilerParams(vmem_limit_bytes=56 * MB, **params),
        cost_estimate=pl.CostEstimate(
            flops=40_000_000_000, bytes_accessed=60_000_000, transcendentals=0
        ),
        name="forward",
    )(key, found, extra, places, w_qkv, bias, block)


def backward_kernel(
    by_kernel,
    q_ref,
    k_ref,
    v_ref,
    att_ref,
    g_ref,
    lse_ref,
    first_ref,
    xb_ref,
    key_ref,
    w_ref,
    rest_ref,
    grad_ref,
    place_ref,
    weights_ref,
    sent_ref,
    bias_ref,
    mats_ref,
    proj,
    total,
    places,
    sent,
    *scratch,
):
    seq, head = pl.program_id(0), pl.program_id(1)
    pairs = HEADS // 2
    step = seq * (pairs + 1) + head

    @pl.when(step == 0)
    def _():
        total[...] = jnp.zeros_like(total)
        places[...] = jnp.zeros_like(places)
        sent[...] = jnp.zeros_like(sent)
        bias_ref[...] = jnp.zeros_like(bias_ref)
        mats_ref[...] = jnp.zeros_like(mats_ref)

    if by_kernel:
        sums = RestSums(rest_ref, mats_ref, scratch)
        for when, actions in sums.schedule().items():

            @pl.when(step == when)
            def _(actions=actions):
                for action in actions:
                    action()

    @pl.when(head < pairs)
    def _():
        cols = pl.ds(pl.multiple_of(head * 2 * HEAD_DIM, 2 * HEAD_DIM), 2 * HEAD_DIM)
        query = q_ref[...]
        keys = k_ref[...]
        values = v_ref[...]
        grad = g_ref[...]
        lane = lax.broadcasted_iota(jnp.int32, query.shape, 1)
        first = lane < HEAD_DIM
        product = (att_ref[...].astype(F32) * grad.astype(F32)).T
        zero = jnp.zeros_like(query)
        g_q, g_k, g_v = [], [], []
        for half in range(2):
            mine = first if half == 0 else jnp.logical_not(first)
            scores = dot_nt(keys, jnp.where(mine, query, zero))
            probs = jnp.exp2(scores * (SCORE * LOG2E) - lse_ref[0, half : half + 1, :])
            delta = jnp.sum(
                product[half * HEAD_DIM : (half + 1) * HEAD_DIM, :], 0, keepdims=True
            )
            g_probs = dot_nt(values, jnp.where(mine, grad, zero))
            g_v.append(dot_nn(probs.astype(BF), grad))
            g_scores = (probs * (g_probs - delta)).astype(BF)
            g_k.append(dot_nn(g_scores, query))
            g_q.append(dot_tn(g_scores, keys))
        grad_q = jnp.where(first, g_q[0], g_q[1]) * SCORE
        grad_k = jnp.where(first, g_k[0], g_k[1]) * SCORE
        grad_v = jnp.where(first, g_v[0], g_v[1])
        proj[0, :, cols] = grad_q.astype(BF)
        proj[1, :, cols] = grad_k.astype(BF)
        proj[2, :, cols] = grad_v.astype(BF)
        bias_ref[0:1, cols] += jnp.sum(grad_q, 0, keepdims=True)
        bias_ref[1:2, cols] += jnp.sum(grad_v, 0, keepdims=True)

    @pl.when(head == pairs)
    def _():
        g_in = first_ref[...]
        inputs_b = xb_ref[...]
        for part in range(3):
            cols = slice(part * D, (part + 1) * D)
            g_in = g_in + dot_nn(proj[part], w_ref[cols, :])
            total[cols, :] += dot_tn(proj[part], inputs_b)
        g_in_b = g_in.astype(BF)
        grad_ref[...] = g_in_b
        places[...] += g_in
        slots = lax.broadcasted_iota(jnp.int32, (LENGTH, sent.shape[0]), 1)
        sent[...] += dot_tn((key_ref[...] == slots).astype(BF), g_in_b)

    @pl.when(step == pl.num_programs(0) * (pairs + 1) - 1)
    def _():
        sent_ref[...] = sent[...].astype(BF)
        weights_ref[...] = total[...].astype(BF)
        place_ref[...] = places[...].astype(BF)


def backward(
    by_kernel, projected, attended, grad_att, lse, g_first, inputs_b, key, room, w_qkv, rest, ident
):
    rows = projected.shape[0]
    seqs = rows // LENGTH
    pairs = HEADS // 2
    block = (LENGTH, 2 * HEAD_DIM)
    shape = rest.shape[1:]

    def pair(offset):
        return pl.BlockSpec(block, lambda s, h: (s, offset + jnp.minimum(h, pairs - 1)))

    def row(width):
        return pl.BlockSpec((LENGTH, width), lambda s, h: (s, 0))

    def steady(shape):
        return pl.BlockSpec(
            shape, lambda s, h: (0, 0), pipeline_mode=pl.Buffered(buffer_count=1)
        )

    def kept(shape):
        return pl.BlockSpec(shape, lambda s, h: (0, 0))

    return pl.pallas_call(
        functools.partial(backward_kernel, by_kernel),
        grid=(seqs, pairs + 1),
        in_specs=[
            pair(0),
            pair(pairs),
            pair(2 * pairs),
            pair(0),
            pair(0),
            pl.BlockSpec(
                (1, 2, LENGTH), lambda s, h: (s * pairs + jnp.minimum(h, pairs - 1), 0, 0)
            ),
            row(D),
            row(D),
            row(1),
            steady((QKV, D)),
            pl.BlockSpec(memory_space=pl.ANY),
        ],
        out_specs=[
            row(D),
            kept((LENGTH, D)),
            kept((QKV, D)),
            kept((room, D)),
            kept((8, D)),
            kept(shape),
        ],
        out_shape=[
            jax.ShapeDtypeStruct((rows, D), BF),
            jax.ShapeDtypeStruct((LENGTH, D), BF),
            jax.ShapeDtypeStruct((QKV, D), BF),
            jax.ShapeDtypeStruct((room, D), BF),
            jax.ShapeDtypeStruct((8, D), F32),
            jax.ShapeDtypeStruct(shape, F32),
        ],
        scratch_shapes=[
            pltpu.VMEM((3, LENGTH, D), BF),
            pltpu.VMEM((QKV, D), F32),
            pltpu.VMEM((LENGTH, D), F32),
            pltpu.VMEM((room, D), F32),
        ]
        + (RestSums.scratch(shape) if by_kernel else []),
        compiler_params=pltpu.CompilerParams(
            vmem_limit_bytes=60 * MB,
            **(dict(collective_id=ident, has_side_effects=True) if by_kernel else {}),
        ),
        cost_estimate=pl.CostEstimate(
            flops=60_000_000_000, bytes_accessed=60_000_000, transcendentals=0
        ),
        name="backward",
    )(
        projected,
        projected,
        projected,
        attended,
        grad_att,
        lse,
        g_first,
        inputs_b,
        key,
        w_qkv,
        rest,
    )


def slots_of(ids, owned):
    count = ids.shape[0]
    order = jnp.arange(count, dtype=jnp.int32)
    repeated = jnp.any(
        (ids[:, None] == ids[None, :]) & (order[:, None] < order[None, :]), axis=0
    )
    first = jnp.logical_not(repeated)
    base = (ids // owned) * owned
    below = (
        first[:, None]
        & (ids[:, None] >= base[None, :])
        & (ids[:, None] < ids[None, :])
    )
    return jnp.sum(below.astype(jnp.int32), axis=0)


def requests_of(ids, owner, slot, owned, devices, start, room):
    key = jnp.where((slot >= start) & (slot < start + room), owner * room + slot - start, -1)
    spots = jnp.arange(devices * room, dtype=jnp.int32)
    asked = jnp.max(
        jnp.where(key[:, None] == spots[None, :], (ids - owner * owned)[:, None], -1), axis=0
    )
    return key, asked


def pick(index, amount):
    return (index[:, None] == jnp.arange(amount, dtype=jnp.int32)[None, :]).astype(BF)


def adam_direction(param, first, second, grad, corr_one, corr_two, decay):
    first_next = beta_one * first + (1.0 - beta_one) * grad
    second_next = beta_two * second + (1.0 - beta_two) * grad * grad
    update = first_next / corr_one / (jnp.sqrt(second_next / corr_two) + adam_eps)
    return (update + decay * param, first_next)


def body(
    devices,
    token_ids,
    masked,
    swap_kind,
    swap_ids,
    out_grad,
    embed_table,
    table_first,
    table_second,
    layer_mats,
    mats_first,
    mats_second,
    layer_vecs,
    vecs_first,
    vecs_second,
):
    axis = "fsdp"
    rows = token_ids.shape[0]
    owned = embed_table.shape[0]
    entries = layer_vecs.shape[0]
    columns = layer_mats.shape[1]
    me = lax.axis_index(axis)
    by_kernel = devices == 32
    split = place_split(devices, owned)
    replaced = jnp.where(swap_kind < 8, mask_token, jnp.where(swap_kind == 8, swap_ids, token_ids))
    chosen = jnp.where(masked == 1, replaced, token_ids)

    def swap(blocks):
        return lax.all_to_all(blocks, axis, 0, 0, tiled=True)

    block = layer_mats.astype(BF).T

    room = 16 * -(-1536 // (16 * devices))
    more = 16
    owner = chosen // owned
    slot = slots_of(chosen, owned)
    most = jnp.max(slot) + 1
    key, asked = requests_of(chosen, owner, slot, owned, devices, 0, room)
    _, asked_more = requests_of(chosen, owner, slot, owned, devices, room, more)
    table_b = embed_table.astype(BF)
    own_vecs = layer_vecs.astype(BF).astype(F32)
    notes = jnp.concatenate(
        [
            asked.reshape(devices, room).astype(F32),
            asked_more.reshape(devices, more).astype(F32),
            jnp.broadcast_to(own_vecs[None], (devices, entries)),
            jnp.broadcast_to(most.astype(F32), (devices, 1)),
        ],
        axis=1,
    )
    notes = swap(notes)
    wanted = notes[:, :room].astype(jnp.int32).reshape(-1)
    wanted_more = notes[:, room : room + more].astype(jnp.int32).reshape(-1)
    vecs = notes[:, room + more : room + more + entries].reshape(-1)
    longest = jnp.max(notes[:, room + more + entries]).astype(jnp.int32)
    found = dot_nn(pick(wanted, owned), table_b).astype(BF)
    found, table, block = lax.optimization_barrier((found, embed_table, block))
    found = swap(found.reshape(devices, room, D)).reshape(-1, D)
    if by_kernel:
        places, w_qkv = broadcast(table, block, split, 1)
        w_qkv = w_qkv.reshape(QKV, D)
    else:
        spots = VOCAB + jnp.arange(LENGTH, dtype=jnp.int32) - me * owned
        places = lax.psum(dot_nn(pick(spots, owned), table_b), axis).astype(BF)
        mats_t = lax.all_gather(block, axis, axis=0, tiled=True)
        w_qkv, rest = mats_t[:QKV], mats_t[QKV:]
    rounds = (longest - room + more - 1) // more

    def further(turn):
        key, asked = requests_of(chosen, owner, slot, owned, devices, room + turn * more, more)
        wanted = lax.cond(
            turn == 0,
            lambda: wanted_more,
            lambda: swap(asked.reshape(devices, more)).reshape(-1),
        )
        return key, wanted

    def fetch_more(state):
        turn, extra = state
        key, wanted = further(turn)
        found = dot_nn(pick(wanted, owned), table_b).astype(BF)
        found = swap(found.reshape(devices, more, D)).reshape(-1, D)
        return turn + 1, extra + dot_nn(pick(key, devices * more), found).astype(BF)

    _, extra = lax.while_loop(
        lambda state: state[0] < rounds,
        fetch_more,
        (jnp.int32(0), jnp.zeros((rows, D), BF)),
    )

    bias_qkv = jnp.concatenate([vecs[:D], jnp.zeros((D,), F32), vecs[D : 2 * D]])[None]
    bias_up = vecs[5 * D : 5 * D + FF][None]
    small = jnp.concatenate(
        [vecs[2 * D : 5 * D], vecs[5 * D + FF :], jnp.zeros((2 * D,), F32)]
    ).reshape(8, D)

    results = forward(by_kernel, key[:, None], found, extra, places, w_qkv, bias_qkv, block, 4)
    inputs, inputs_b, projected, attended, lse = results[:5]
    if by_kernel:
        rest = results[5].reshape(-1, D)
    (
        outputs,
        normed_b,
        hidden_b,
        g_mid_b,
        g_up_b,
        g_first,
        g_first_b,
        g_att_b,
        sums,
    ) = middle(attended, inputs, out_grad, masked[:, None], rest, small, bias_up)
    g_rest = rest_gradients(g_first_b, attended, g_up_b, normed_b, hidden_b, g_mid_b)
    input_grad, g_places, g_qkv, sent, bias_sums, rest_grad = backward(
        by_kernel,
        projected,
        attended,
        g_att_b,
        lse,
        g_first,
        inputs_b,
        key[:, None],
        devices * room,
        w_qkv,
        g_rest.reshape(-1, columns, D),
        2,
    )

    g_vecs = jnp.concatenate(
        [
            bias_sums[0],
            bias_sums[1],
            sums[1, :D],
            sums[2, :D],
            sums[3, :D],
            sums[0],
            sums[4, :D],
            sums[5, :D],
            sums[6, :D],
        ]
    )
    g_vecs = g_vecs.reshape(devices, entries)
    sent, g_places, g_qkv = lax.optimization_barrier((sent, g_places, g_qkv))
    sent = swap(sent.reshape(devices, room, D)).reshape(-1, D)
    if by_kernel:
        padded = jnp.pad(g_vecs, ((0, 0), (0, 1024 - entries))).reshape(devices, 8, 128)
        g_own_places, first_grad, vecs_grad = homecoming(
            g_places, g_qkv.reshape(-1, columns, D), padded, owned, split, 3
        )
        vecs_grad = vecs_grad.reshape(1024)[:entries]
        mats_grad = jnp.where(me < QKV // columns, first_grad, rest_grad).T
    else:
        vecs_grad = jnp.sum(swap(g_vecs), axis=0)
        total = lax.psum(g_places.astype(F32), axis)
        spots = me * owned + jnp.arange(owned, dtype=jnp.int32) - VOCAB
        inside = (spots >= 0) & (spots < LENGTH)
        g_own_places = jnp.where(
            inside[:, None], total[jnp.clip(spots, 0, LENGTH - 1)], 0.0
        )
        mats_grad = lax.psum_scatter(
            jnp.concatenate([g_qkv, g_rest], axis=0), axis, scatter_dimension=0, tiled=True
        )
        mats_grad = mats_grad.astype(F32).T
    table_grad = dot_tn(pick(wanted, owned), sent) + g_own_places

    def send_more(state):
        turn, total = state
        key, wanted = further(turn)
        sent = dot_tn(pick(key, devices * more), input_grad).astype(BF)
        sent = swap(sent.reshape(devices, more, D)).reshape(-1, D)
        return turn + 1, total + dot_tn(pick(wanted, owned), sent)

    _, table_grad = lax.while_loop(
        lambda state: state[0] < rounds, send_more, (jnp.int32(0), table_grad)
    )

    counter = jnp.float32(STEP)
    corr_one = 1.0 - jnp.power(jnp.float32(beta_one), counter)
    corr_two = 1.0 - jnp.power(jnp.float32(beta_two), counter)
    table_step, table_first_next = adam_direction(
        embed_table, table_first, table_second, table_grad, corr_one, corr_two, decay_rate
    )
    mats_step, mats_first_next = adam_direction(
        layer_mats, mats_first, mats_second, mats_grad, corr_one, corr_two, decay_rate
    )
    vecs_step, vecs_first_next = adam_direction(
        layer_vecs, vecs_first, vecs_second, vecs_grad, corr_one, corr_two, 0.0
    )
    return (
        outputs,
        input_grad,
        table_grad,
        mats_grad,
        vecs_grad,
        table_step,
        table_first_next,
        mats_step,
        mats_first_next,
        vecs_step,
        vecs_first_next,
    )


def solution(mesh):
    line = P("fsdp")
    by_rows = P("fsdp", None)
    by_cols = P(None, "fsdp")
    return jax.shard_map(
        functools.partial(body, mesh.shape["fsdp"]),
        mesh=mesh,
        in_specs=(
            line,
            line,
            line,
            line,
            by_rows,
            by_rows,
            by_rows,
            by_rows,
            by_cols,
            by_cols,
            by_cols,
            line,
            line,
            line,
        ),
        out_specs=(
            by_rows,
            by_rows,
            by_rows,
            by_cols,
            line,
            by_rows,
            by_rows,
            by_cols,
            by_cols,
            line,
            line,
        ),
        check_vma=False,
    )
```

```python
import functools

import jax
import jax.numpy as jnp
from jax import lax
from jax.experimental import pallas as pl
from jax.experimental.pallas import tpu as pltpu
from jax.sharding import PartitionSpec as P

D = 768
HEADS = 12
HEAD_DIM = 64
FF = 3072
VOCAB = 14592
LENGTH = 512
STEP = 10
QKV = 3 * D

norm_eps = 1e-12
mask_token = 103
beta_one = 0.9
beta_two = 0.999
adam_eps = 1e-06
decay_rate = 0.01

BF = jnp.bfloat16
F32 = jnp.float32
LOG2E = 1.4426950408889634
SCORE = HEAD_DIM ** (-0.5)
MB = 1024 * 1024

ROW_TILE = 256


def dot_nn(left, right):
    return lax.dot_general(
        left, right, (((1,), (0,)), ((), ())), preferred_element_type=F32
    )


def dot_nt(left, right):
    return lax.dot_general(
        left, right, (((1,), (1,)), ((), ())), preferred_element_type=F32
    )


def dot_tn(left, right):
    return lax.dot_general(
        left, right, (((0,), (0,)), ((), ())), preferred_element_type=F32
    )


def gelu_parts(values):
    size = jnp.abs(values)
    frac = 1.0 / (1.0 + (0.3275911 * 0.7071067811865476) * size)
    expo = jnp.exp2(values * values * (-0.5 * LOG2E))
    poly = 1.061405429 * 0.5
    for coef in (-1.453152027, 1.421413741, -0.284496736, 0.254829592):
        poly = poly * frac + 0.5 * coef
    tail = poly * frac * expo
    cdf = jnp.where(values >= 0, 1.0 - tail, tail)
    return values * cdf, cdf + values * expo * 0.3989422804014327


def norm_parts(total):
    centre = jnp.mean(total, -1, keepdims=True)
    centered = total - centre
    variance = jnp.mean(centered * centered, -1, keepdims=True)
    scale = lax.rsqrt(variance + norm_eps)
    return centered * scale, scale


def norm_back(scaled, unit, scale):
    return scale * (
        scaled
        - jnp.mean(scaled, -1, keepdims=True)
        - unit * jnp.mean(scaled * unit, -1, keepdims=True)
    )


def middle_kernel(
    att_ref,
    x_ref,
    go_ref,
    mask_ref,
    wout_ref,
    up_0,
    up_1,
    up_2,
    up_3,
    down_0,
    down_1,
    down_2,
    down_3,
    vec_ref,
    bup_ref,
    out_ref,
    normed_ref,
    hidden_ref,
    gmid_ref,
    gup_ref,
    gfirst_ref,
    gfirstb_ref,
    gatt_ref,
    sums_ref,
    slope_ref,
):
    @pl.when(pl.program_id(0) == 0)
    def _():
        sums_ref[...] = jnp.zeros_like(sums_ref)

    ups = (up_0, up_1, up_2, up_3)
    downs = (down_0, down_1, down_2, down_3)
    bias_out = vec_ref[0:1, :]
    gain_one = vec_ref[1:2, :]
    shift_one = vec_ref[2:3, :]
    bias_down = vec_ref[3:4, :]
    gain_two = vec_ref[4:5, :]
    shift_two = vec_ref[5:6, :]

    def note(row, values):
        sums_ref[row : row + 1, :] += jnp.sum(values, 0, keepdims=True)

    branch = dot_nt(att_ref[...], wout_ref[...]) + bias_out
    unit_one, scale_one = norm_parts(x_ref[...] + branch)
    normed = unit_one * gain_one + shift_one
    normed_b = normed.astype(BF)
    normed_ref[...] = normed_b
    downward = jnp.zeros(normed.shape, F32)
    for start in range(0, FF, D):
        cols = slice(start, start + D)
        upward = dot_nt(normed_b, ups[start // D][...]) + bup_ref[0:1, cols]
        hidden, slope = gelu_parts(upward)
        slope_ref[:, cols] = slope
        hidden_b = hidden.astype(BF)
        hidden_ref[:, cols] = hidden_b
        downward += dot_nn(hidden_b, downs[start // D][...])
    unit_two, scale_two = norm_parts(normed + downward + bias_down)
    out_ref[...] = (unit_two * gain_two + shift_two).astype(BF)
    g_out = go_ref[...].astype(F32) * mask_ref[...].astype(F32)
    note(10, g_out * unit_two)
    note(11, g_out)
    g_mid = norm_back(g_out * gain_two, unit_two, scale_two)
    note(9, g_mid)
    g_mid_b = g_mid.astype(BF)
    gmid_ref[...] = g_mid_b
    g_normed = g_mid
    for start in range(0, FF, D):
        cols = slice(start, start + D)
        g_up = dot_nt(g_mid_b, downs[start // D][...]) * slope_ref[:, cols]
        note(5 + start // D, g_up)
        g_up_b = g_up.astype(BF)
        gup_ref[:, cols] = g_up_b
        g_normed += dot_nn(g_up_b, ups[start // D][...])
    note(3, g_normed * unit_one)
    note(4, g_normed)
    g_first = norm_back(g_normed * gain_one, unit_one, scale_one)
    note(2, g_first)
    gfirst_ref[...] = g_first
    g_first_b = g_first.astype(BF)
    gfirstb_ref[...] = g_first_b
    gatt_ref[...] = dot_nn(g_first_b, wout_ref[...]).astype(BF)


def middle(attended, inputs, out_grad, masked, rest, vecs, bias_up):
    rows = attended.shape[0]
    tile = ROW_TILE

    def row(width):
        return pl.BlockSpec((tile, width), lambda i: (i, 0))

    def whole(shape, place=0):
        return pl.BlockSpec(
            shape, lambda i: (place, 0), pipeline_mode=pl.Buffered(buffer_count=1)
        )

    return pl.pallas_call(
        middle_kernel,
        grid=(rows // tile,),
        in_specs=[
            row(D),
            row(D),
            row(D),
            row(1),
            *[whole((D, D), place) for place in range(9)],
            whole((8, D)),
            whole((1, FF)),
        ],
        out_specs=[
            row(D),
            row(D),
            row(FF),
            row(D),
            row(FF),
            row(D),
            row(D),
            row(D),
            pl.BlockSpec((16, D), lambda i: (0, 0)),
        ],
        out_shape=[
            jax.ShapeDtypeStruct((rows, D), BF),
            jax.ShapeDtypeStruct((rows, D), BF),
            jax.ShapeDtypeStruct((rows, FF), BF),
            jax.ShapeDtypeStruct((rows, D), BF),
            jax.ShapeDtypeStruct((rows, FF), BF),
            jax.ShapeDtypeStruct((rows, D), F32),
            jax.ShapeDtypeStruct((rows, D), BF),
            jax.ShapeDtypeStruct((rows, D), BF),
            jax.ShapeDtypeStruct((16, D), F32),
        ],
        scratch_shapes=[pltpu.VMEM((tile, FF), F32)],
        compiler_params=pltpu.CompilerParams(vmem_limit_bytes=56 * MB),
        name="middle",
    )(attended, inputs, out_grad, masked, *[rest] * 9, vecs, bias_up)


def fixed(shape, place=0):
    return pl.BlockSpec(
        shape, lambda i: (place, 0), pipeline_mode=pl.Buffered(buffer_count=1)
    )


def rest_kernel(first_ref, att_ref, up_ref, normed_ref, hidden_ref, mid_ref, out_ref):
    step = pl.program_id(0)
    chunks = FF // D

    @pl.when(step == 0)
    def _():
        out_ref[...] = dot_tn(first_ref[...], att_ref[...]).astype(BF)

    @pl.when(jnp.logical_and(step > 0, step <= chunks))
    def _():
        out_ref[...] = dot_tn(up_ref[...], normed_ref[...]).astype(BF)

    @pl.when(step > chunks)
    def _():
        out_ref[...] = dot_tn(hidden_ref[...], mid_ref[...]).astype(BF)


def rest_gradients(g_first_b, attended, g_up_b, normed_b, hidden_b, g_mid_b):
    rows = attended.shape[0]
    chunks = FF // D
    full = fixed((rows, D))
    return pl.pallas_call(
        rest_kernel,
        grid=(1 + 2 * chunks,),
        in_specs=[
            full,
            full,
            pl.BlockSpec((rows, D), lambda i: (0, jnp.clip(i - 1, 0, chunks - 1))),
            full,
            pl.BlockSpec((rows, D), lambda i: (0, jnp.clip(i - 1 - chunks, 0, chunks - 1))),
            full,
        ],
        out_specs=pl.BlockSpec((D, D), lambda i: (i, 0)),
        out_shape=jax.ShapeDtypeStruct((D + 2 * FF, D), BF),
        compiler_params=pltpu.CompilerParams(vmem_limit_bytes=56 * MB),
        cost_estimate=pl.CostEstimate(
            flops=22_000_000_000, bytes_accessed=50_000_000, transcendentals=0
        ),
        name="rest_gradients",
    )(g_first_b, attended, g_up_b, normed_b, hidden_b, g_mid_b)


MESH = pl.DeviceIdType.MESH
PLANES = 4


def neighbours():
    me = lax.axis_index("fsdp")
    core = lax.rem(me, 2)
    x = lax.rem(me // 2, 2)
    y = lax.rem(me // 4, 2)
    z = me // 8
    step_a = 4 - 2 * core
    step_b = 2 + 2 * core
    a = jnp.where(core == 0, y, x)
    b = jnp.where(core == 0, x, y)
    near_a = me + step_a * (1 - 2 * a)
    near_b = me + step_b * (1 - 2 * b)
    twin = me + 1 - 2 * core
    return me, core, z, a, b, step_a, step_b, near_a, near_b, twin


def greet(me, z, near_a, near_b, twin):
    barrier = pltpu.get_barrier_semaphore()

    def hello(device):
        pl.semaphore_signal(barrier, inc=1, device_id=(device,), device_id_type=MESH)

    for device in (near_a, near_b, twin):
        hello(device)

    @pl.when(z > 0)
    def _():
        hello(me - 8)

    @pl.when(z < PLANES - 1)
    def _():
        hello(me + 8)

    inner = jnp.logical_and(z > 0, z < PLANES - 1)
    pl.semaphore_wait(barrier, jnp.where(inner, 5, 4))


class RestSpread:
    def __init__(self, in_ref, out_ref, scratch):
        self.in_ref, self.out_ref = in_ref, out_ref
        self.own_sem, self.send_sem, self.recv_sem = scratch
        self.place = neighbours()

    @staticmethod
    def scratch():
        return [
            pltpu.SemaphoreType.DMA,
            pltpu.SemaphoreType.DMA((5, 24)),
            pltpu.SemaphoreType.DMA((24,)),
        ]

    def copy(self, shard, device, kind, source=None):
        return pltpu.make_async_remote_copy(
            src_ref=self.out_ref.at[shard] if source is None else source,
            dst_ref=self.out_ref.at[shard],
            send_sem=self.send_sem.at[kind, shard],
            recv_sem=self.recv_sem.at[shard],
            device_id=(device,),
            device_id_type=MESH,
        )

    def shard(self, plane, other_a, other_b):
        me, core, z, a, b, step_a, step_b, near_a, near_b, twin = self.place
        a_at = 1 - a if other_a else a
        b_at = 1 - b if other_b else b
        return jnp.maximum(plane - 1, 0) * 8 + a_at * step_a + b_at * step_b + core

    def planes(self, far):
        z = self.place[2]
        for way in (1, -1) if far else (1,):
            plane = z - way * far
            yield way, plane, jnp.logical_and(plane >= 1, plane < PLANES)

    def routes(self, far):
        me, core, z, a, b, step_a, step_b, near_a, near_b, twin = self.place
        for way, plane, there in self.planes(far):
            shard = self.shard(plane, False, False)
            for onward in (way,) if far else (1, -1):
                goes = jnp.logical_and(z + onward >= 0, z + onward < PLANES)
                yield (
                    jnp.logical_and(there, goes),
                    shard,
                    me + 8 * onward,
                    0 if onward == 1 else 1,
                )
            yield there, shard, near_b, 3
            yield there, shard, near_a, 2
            yield there, shard, twin, 4

    def routes_a(self, far):
        near_b, twin = self.place[8:]
        for way, plane, there in self.planes(far):
            shard = self.shard(plane, True, False)
            yield there, shard, near_b, 3
            yield there, shard, twin, 4

    def routes_b(self, far):
        twin = self.place[9]
        for way, plane, there in self.planes(far):
            for other_a in (False, True):
                yield there, self.shard(plane, other_a, True), twin, 4

    def own(self):
        return pltpu.make_async_copy(
            self.in_ref, self.out_ref.at[self.shard(self.place[2], False, False)], self.own_sem
        )

    def start(self):
        me, core, z, a, b, step_a, step_b, near_a, near_b, twin = self.place
        greet(me, z, near_a, near_b, twin)

        @pl.when(z > 0)
        def _():
            self.own().start()

        for goes, shard, device, kind in self.routes(0):
            pl.when(goes)(
                lambda shard=shard, device=device, kind=kind: self.copy(
                    shard, device, kind, self.in_ref
                ).start()
            )

    def pass_on(self, routes):
        seen = []
        for goes, shard, device, kind in routes:
            if kind == 4:
                seen.append((goes, shard))
        for goes, shard in seen:
            pl.when(goes)(
                lambda shard=shard: self.copy(shard, self.place[9], 4).wait_recv()
            )
            for other, place, device, kind in routes:
                if place is shard:
                    pl.when(other)(
                        lambda shard=shard, device=device, kind=kind: self.copy(
                            shard, device, kind
                        ).start()
                    )

    def column(self, far):
        self.pass_on(list(self.routes(far)))

    def along_a(self, far):
        self.pass_on(list(self.routes_a(far)))

    def along_b(self, far):
        self.pass_on(list(self.routes_b(far)))

    def end(self):
        me, core, z, a, b, step_a, step_b, near_a, near_b, twin = self.place

        def from_twin(place, carry):
            self.copy(place * 2 + 1 - core, twin, 4).wait_recv()
            return carry

        lax.fori_loop(0, 12, from_twin, 0)
        for far in range(PLANES):
            for routes in (self.routes(far), self.routes_a(far), self.routes_b(far)):
                for goes, shard, device, kind in routes:
                    pl.when(goes)(
                        lambda shard=shard, device=device, kind=kind: self.copy(
                            shard, device, kind
                        ).wait_send()
                    )

        @pl.when(z > 0)
        def _():
            self.own().wait()

    def schedule(self):
        return {
            0: [self.start],
            6: [lambda: self.column(1)],
            11: [lambda: self.column(2), lambda: self.along_a(0)],
            13: [lambda: self.along_a(1)],
            16: [lambda: self.column(3)],
            21: [lambda: self.along_a(2), lambda: self.along_a(3)],
            23: [lambda: self.along_b(0)],
            24: [lambda: self.along_b(1)],
            25: [lambda: self.along_b(2)],
            26: [lambda: self.along_b(3)],
            27: [self.end],
        }


class RestSums:
    TURNS = PLANES - 1

    def __init__(self, in_ref, out_ref, scratch):
        self.in_ref, self.out_ref = in_ref, out_ref
        (
            self.own,
            self.from_twin,
            self.from_b,
            self.from_a,
            self.from_low,
            self.from_high,
            self.load_sem,
            self.twin_sem,
            self.b_sem,
            self.a_sem,
            self.low_sem,
            self.high_sem,
        ) = scratch
        self.place = neighbours()

    @staticmethod
    def scratch(shape):
        return [
            pltpu.VMEM((12,) + shape, BF),
            pltpu.VMEM((12,) + shape, BF),
            pltpu.VMEM((6,) + shape, BF),
            pltpu.VMEM((3,) + shape, BF),
            pltpu.VMEM((4,) + shape, BF),
            pltpu.VMEM((4,) + shape, BF),
            pltpu.SemaphoreType.DMA((12,)),
            pltpu.SemaphoreType.DMA((2, 12)),
            pltpu.SemaphoreType.DMA((2, 6)),
            pltpu.SemaphoreType.DMA((2, 3)),
            pltpu.SemaphoreType.DMA((2, 4)),
            pltpu.SemaphoreType.DMA((2, 4)),
        ]

    def remote(self, source, target, sems, slot, device):
        return pltpu.make_async_remote_copy(
            src_ref=source,
            dst_ref=target.at[slot],
            send_sem=sems.at[0, slot],
            recv_sem=sems.at[1, slot],
            device_id=(device,),
            device_id_type=MESH,
        )

    def plane_of(self, turn):
        z = self.place[2]
        last = PLANES - 1 - turn
        inner = (1, 3, 2)[turn]
        return jnp.where(z < 2, last, jnp.where(z == 2, inner, 1 + turn))

    def shards(self, slot):
        me, core, z, a, b, step_a, step_b, near_a, near_b, twin = self.place
        other_b, turn, other_a = slot < 6, slot % 6 // 2, slot % 2 == 0
        base = (self.plane_of(turn) - 1) * 8
        a_at = 1 - a if other_a else a
        b_at = 1 - b if other_b else b
        mine = base + a_at * step_a + b_at * step_b + core
        a_at = 1 - b if other_a else b
        b_at = 1 - a if other_b else a
        twins = base + a_at * step_b + b_at * step_a + 1 - core
        return mine, twins

    def load(self, slot):
        return pltpu.make_async_copy(
            self.in_ref.at[self.shards(slot)[0]], self.own.at[slot], self.load_sem.at[slot]
        )

    def gift(self, slot):
        return self.remote(
            self.in_ref.at[self.shards(slot)[1]],
            self.from_twin,
            self.twin_sem,
            slot,
            self.place[9],
        )

    def over_b(self, slot):
        return self.remote(self.own.at[slot], self.from_b, self.b_sem, slot, self.place[8])

    def over_a(self, turn):
        return self.remote(
            self.own.at[6 + 2 * turn], self.from_a, self.a_sem, turn, self.place[7]
        )

    def along(self, turn, up):
        plane = self.plane_of(turn)
        source = self.own.at[7 + 2 * turn]
        if up:
            return self.remote(source, self.from_low, self.low_sem, plane, self.place[0] + 8)
        return self.remote(source, self.from_high, self.high_sem, plane, self.place[0] - 8)

    def add(self, slot, arrived):
        self.own[slot] = self.own[slot] + arrived[...]

    def start(self):
        me, core, z, a, b, step_a, step_b, near_a, near_b, twin = self.place
        greet(me, z, near_a, near_b, twin)
        for slot in (0, 1, 2, 3, 6, 7, 4, 5, 8, 9, 10, 11):
            self.gift(slot).start()
            self.load(slot).start()

    def far(self, turn):
        for slot in (2 * turn, 2 * turn + 1):
            self.load(slot).wait()
            self.gift(slot).wait_recv()
            self.add(slot, self.from_twin.at[slot])
            self.over_b(slot).start()

    def near(self, turn):
        for slot in (6 + 2 * turn, 7 + 2 * turn):
            self.load(slot).wait()
            self.gift(slot).wait_recv()
            self.add(slot, self.from_twin.at[slot])

    def stage_b(self, turn):
        for slot in (2 * turn, 2 * turn + 1):
            self.over_b(slot).wait_recv()
            self.add(6 + slot, self.from_b.at[slot])
        self.over_a(turn).start()

    def stage_a(self, turn):
        z = self.place[2]
        slot = 7 + 2 * turn
        self.over_a(turn).wait_recv()
        self.add(slot, self.from_a.at[turn])

        @pl.when(z == 0)
        def _():
            self.along(turn, True).start()

        if turn < 2:

            @pl.when(z == PLANES - 1)
            def _():
                self.along(turn, False).start()

    def stage_z(self, turn):
        z = self.place[2]
        slot = 7 + 2 * turn
        plane = self.plane_of(turn)
        if turn < 2:
            inner = jnp.logical_and(z > 0, z < PLANES - 1)

            @pl.when(jnp.logical_and(inner, plane > z))
            def _():
                self.along(turn, True).wait_recv()
                self.add(slot, self.from_low.at[plane])
                self.along(turn, True).start()

            @pl.when(jnp.logical_and(inner, plane < z))
            def _():
                self.along(turn, False).wait_recv()
                self.add(slot, self.from_high.at[plane])
                self.along(turn, False).start()

            return

        @pl.when(z > 0)
        def _():
            self.along(turn, True).wait_recv()
            self.out_ref[...] = self.own[slot].astype(F32) + self.from_low[plane].astype(F32)

        @pl.when(jnp.logical_and(z > 0, z < PLANES - 1))
        def _():
            self.along(turn, False).wait_recv()
            self.out_ref[...] += self.from_high[plane].astype(F32)

    def end(self):
        z = self.place[2]
        for slot in range(12):
            self.gift(slot).wait_send()
        for slot in range(6):
            self.over_b(slot).wait_send()
        for turn in range(self.TURNS):
            self.over_a(turn).wait_send()
            plane = self.plane_of(turn)

            @pl.when(plane > z)
            def _(turn=turn):
                self.along(turn, True).wait_send()

            @pl.when(plane < z)
            def _(turn=turn):
                self.along(turn, False).wait_send()

    def schedule(self):
        return {
            0: [self.start],
            2: [lambda: self.far(0)],
            3: [lambda: self.near(0)],
            6: [lambda: self.far(1)],
            7: [lambda: self.near(1)],
            8: [lambda: self.stage_b(0)],
            9: [lambda: self.far(2)],
            10: [lambda: self.near(2)],
            14: [lambda: self.stage_b(1), lambda: self.stage_a(0)],
            18: [lambda: self.stage_b(2)],
            19: [lambda: self.stage_a(1)],
            20: [lambda: self.stage_z(0)],
            22: [lambda: self.stage_a(2)],
            24: [lambda: self.stage_z(1)],
            27: [lambda: self.stage_z(2), self.end],
        }


PIECES = 4
CHUNKS = 3


def broadcast_kernel(
    split,
    table_ref,
    block_ref,
    out_ref,
    w_ref,
    stage,
    own_sem,
    load_sem,
    send_sem,
    recv_sem,
    w_send,
    w_recv,
):
    first_owner, first_row, count = split
    me, core, z, a, b, step_a, step_b, near_a, near_b, twin = neighbours()
    greet(me, z, near_a, near_b, twin)
    rows = LENGTH // PIECES
    height = block_ref.shape[0] // CHUNKS
    root = first_owner + 1
    gift = pltpu.make_async_remote_copy(
        src_ref=table_ref.at[pl.ds(first_row, count)],
        dst_ref=stage.at[pl.ds(0, count)],
        send_sem=load_sem.at[0],
        recv_sem=load_sem.at[1],
        device_id=(root,),
        device_id_type=MESH,
    )
    mine = pltpu.make_async_copy(
        table_ref.at[pl.ds(0, LENGTH - count)],
        stage.at[pl.ds(count, LENGTH - count)],
        load_sem.at[2],
    )
    shard = lax.rem(me, 8)
    own = pltpu.make_async_copy(block_ref, w_ref.at[shard], own_sem)

    @pl.when(me == first_owner)
    def _():
        gift.start()

    @pl.when(me == root)
    def _():
        mine.start()

    @pl.when(z == 0)
    def _():
        own.start()

    def copy(piece, device, kind):
        part = pl.ds(piece * rows, rows)
        return pltpu.make_async_remote_copy(
            src_ref=out_ref.at[part],
            dst_ref=out_ref.at[part],
            send_sem=send_sem.at[kind, piece],
            recv_sem=recv_sem.at[piece],
            device_id=(device,),
            device_id_type=MESH,
        )

    def block(place, chunk, device, kind, source=None):
        part = pl.ds(chunk * height, height)
        return pltpu.make_async_remote_copy(
            src_ref=w_ref.at[place, part] if source is None else source.at[part],
            dst_ref=w_ref.at[place, part],
            send_sem=w_send.at[kind, place, chunk],
            recv_sem=w_recv.at[place, chunk],
            device_id=(device,),
            device_id_type=MESH,
        )

    trunk = jnp.logical_and(core == 1, jnp.logical_and(a == 1, b == 1))
    branch = jnp.logical_and(core == 1, jnp.logical_and(a == 0, b == 1))
    routes = (
        (jnp.logical_and(trunk, z > 0), me - 8),
        (trunk, near_a),
        (jnp.logical_or(trunk, branch), near_b),
        (core == 1, twin),
    )
    shard_a = (1 - a) * step_a + b * step_b + core
    shards_b = [
        a * step_a + (1 - b) * step_b + core,
        (1 - a) * step_a + (1 - b) * step_b + core,
    ]

    def sends(chunk, source):
        pl.when(z < PLANES - 1)(lambda: block(shard, chunk, me + 8, 0, source).start())
        block(shard, chunk, near_b, 1, source).start()
        block(shard, chunk, near_a, 2, source).start()
        block(shard, chunk, twin, 3, source).start()

    def from_own(chunk):
        @pl.when(z > 0)
        def _():
            block(shard, chunk, twin, 3).wait_recv()
            sends(chunk, None)

    def from_a(chunk):
        block(shard_a, chunk, twin, 3).wait_recv()
        block(shard_a, chunk, near_b, 1).start()
        block(shard_a, chunk, twin, 3).start()

    def from_b(chunk):
        for place in shards_b:
            block(place, chunk, twin, 3).wait_recv()
            block(place, chunk, twin, 3).start()

    def pass_on(piece):
        for kind, (goes, device) in enumerate(routes):
            pl.when(goes)(lambda kind=kind, device=device: copy(piece, device, kind).start())

    def positions(condition, piece):
        @pl.when(jnp.logical_and(condition, me != root))
        def _():
            copy(piece, twin, 3).wait_recv()
            pass_on(piece)

    @pl.when(z == 0)
    def _():
        for chunk in range(CHUNKS):
            sends(chunk, block_ref)

    @pl.when(me == root)
    def _():
        mine.wait()
        gift.wait_recv()
        for piece in range(PIECES):
            part = slice(piece * rows, (piece + 1) * rows)
            out_ref[part, :] = stage[part, :].astype(BF)
            pass_on(piece)

    from_own(0)
    positions(trunk, 0)
    from_own(1)
    positions(trunk, 1)
    from_own(2)
    positions(trunk, 2)
    positions(trunk, 3)
    others = jnp.logical_not(trunk)
    from_a(0)
    from_a(1)
    positions(others, 0)
    from_a(2)
    from_b(0)
    positions(others, 1)
    from_b(1)
    positions(others, 2)
    from_b(2)
    positions(others, 3)

    def from_twin(place, carry):
        for chunk in range(CHUNKS):
            block(place * 2 + 1 - core, chunk, twin, 3).wait_recv()
        return carry

    lax.fori_loop(0, 4, from_twin, 0)
    for piece in range(PIECES):
        for kind, (goes, device) in enumerate(routes):
            pl.when(goes)(
                lambda piece=piece, kind=kind, device=device: copy(
                    piece, device, kind
                ).wait_send()
            )
    for chunk in range(CHUNKS):

        @pl.when(z < PLANES - 1)
        def _(chunk=chunk):
            block(shard, chunk, me + 8, 0).wait_send()

        block(shard, chunk, near_b, 1).wait_send()
        block(shard, chunk, near_a, 2).wait_send()
        block(shard, chunk, twin, 3).wait_send()
        block(shard_a, chunk, near_b, 1).wait_send()
        block(shard_a, chunk, twin, 3).wait_send()
        for place in shards_b:
            block(place, chunk, twin, 3).wait_send()

    @pl.when(me == first_owner)
    def _():
        gift.wait_send()

    @pl.when(z == 0)
    def _():
        own.wait()


def place_split(devices, owned):
    first_owner = VOCAB // owned
    first_row = VOCAB - first_owner * owned
    return first_owner, first_row, owned - first_row


def broadcast(table, block, split, ident):
    return pl.pallas_call(
        functools.partial(broadcast_kernel, split),
        in_specs=[pl.BlockSpec(memory_space=pl.ANY)] * 2,
        out_specs=[
            pl.BlockSpec(memory_space=pltpu.VMEM),
            pl.BlockSpec(memory_space=pl.ANY),
        ],
        out_shape=[
            jax.ShapeDtypeStruct((LENGTH, D), BF),
            jax.ShapeDtypeStruct((8,) + block.shape, BF),
        ],
        scratch_shapes=[
            pltpu.VMEM((LENGTH, D), F32),
            pltpu.SemaphoreType.DMA,
            pltpu.SemaphoreType.DMA((3,)),
            pltpu.SemaphoreType.DMA((4, PIECES)),
            pltpu.SemaphoreType.DMA((PIECES,)),
            pltpu.SemaphoreType.DMA((4, 8, CHUNKS)),
            pltpu.SemaphoreType.DMA((8, CHUNKS)),
        ],
        compiler_params=pltpu.CompilerParams(collective_id=ident, has_side_effects=True),
        cost_estimate=pl.CostEstimate(flops=0, bytes_accessed=100_000_000, transcendentals=0),
        name="broadcast",
    )(table, block)


def homecoming_kernel(
    split,
    place_ref,
    first_ref,
    vec_ref,
    out_ref,
    mats_ref,
    vec_sum_ref,
    sums,
    from_twin,
    from_b,
    from_a,
    from_z,
    ready,
    own,
    own_twin,
    own_b,
    own_a,
    own_high,
    sems,
    z_sem,
    piece_sem,
    home_sem,
    load_sem,
    twin_sem,
    b_sem,
    a_sem,
    high_sem,
    vec_in,
    vec_sem,
):
    first_owner, first_row, count = split
    root = first_owner + 1
    me, core, z, a, b, step_a, step_b, near_a, near_b, twin = neighbours()
    rows = place_ref.shape[4]
    height = first_ref.shape[1] // CHUNKS
    out_ref[...] = jnp.zeros_like(out_ref)
    barrier = pltpu.get_barrier_semaphore()

    def each(step, carry):
        pl.semaphore_signal(
            barrier, inc=1, device_id=(lax.rem(me + step, 32),), device_id_type=MESH
        )
        return carry

    lax.fori_loop(1, 32, each, 0)
    pl.semaphore_wait(barrier, 31)

    def remote(source, target, send, receive, device):
        return pltpu.make_async_remote_copy(
            src_ref=source,
            dst_ref=target,
            send_sem=send,
            recv_sem=receive,
            device_id=(device,),
            device_id_type=MESH,
        )

    def add(total, extra):
        return (total.astype(F32) + extra.astype(F32)).astype(BF)

    x = jnp.where(core == 0, b, a)
    y = jnp.where(core == 0, a, b)
    gift = remote(place_ref.at[:, :, :, 1 - core], from_twin, sems.at[0, 0], sems.at[0, 1], twin)
    gift.start()
    loads, gifts = [], []
    for slot in range(4):
        other_b, other_a = slot < 2, slot % 2 == 0
        a_at, b_at = (1 - a if other_a else a), (1 - b if other_b else b)
        shard = a_at * step_a + b_at * step_b + core
        loads.append(pltpu.make_async_copy(first_ref.at[shard], own.at[slot], load_sem.at[slot]))
        a_at, b_at = (1 - b if other_a else b), (1 - a if other_b else a)
        shard = a_at * step_b + b_at * step_a + 1 - core
        gifts.append(
            remote(
                first_ref.at[shard],
                own_twin.at[slot],
                twin_sem.at[0, slot],
                twin_sem.at[1, slot],
                twin,
            )
        )
    for slot in range(4):
        gifts[slot].start()
        loads[slot].start()

    def vec_copy(source, target, device):
        return remote(
            vec_ref.at[source],
            vec_in.at[target],
            vec_sem.at[0, source],
            vec_sem.at[1, target],
            device,
        )

    def vec_start(step, carry):
        device = lax.rem(me + step, 32)
        vec_copy(device, me, device).start()
        return carry

    def vec_wait(step, carry):
        device = lax.rem(me + step, 32)
        vec_copy(device, device, device).wait_recv()
        vec_copy(device, device, device).wait_send()
        return carry

    lax.fori_loop(1, 32, vec_start, 0)
    vec_in[me] = vec_ref[me]
    gift.wait_recv()
    sums[...] = add(place_ref[:, :, :, core], from_twin[...])

    @pl.when(core == 0)
    def _():
        remote(sums.at[:, :, 1 - x], from_b, sems.at[1, 0], sems.at[1, 1], near_b).start()

    @pl.when(core == 1)
    def _():
        remote(sums.at[:, 1 - y], from_b, sems.at[1, 0], sems.at[1, 1], near_b).start()

    over_b = [
        remote(own.at[slot], own_b.at[slot], b_sem.at[0, slot], b_sem.at[1, slot], near_b)
        for slot in range(2)
    ]
    for slot in range(4):
        loads[slot].wait()
        gifts[slot].wait_recv()
        own[slot] = add(own[slot], own_twin[slot])
        if slot < 2:
            over_b[slot].start()

    small_b = remote(sums.at[:, 0], from_b, sems.at[1, 0], sems.at[1, 1], near_b)
    small_b.wait_recv()

    @pl.when(core == 0)
    def _():
        from_b[...] = add(sums[:, :, x], from_b[...])

    @pl.when(core == 1)
    def _():
        from_b[...] = add(sums[:, y], from_b[...])

    small_a = remote(from_b.at[:, 1 - a], from_a, sems.at[2, 0], sems.at[2, 1], near_a)
    small_a.start()
    over_a = remote(own.at[2], own_a, a_sem.at[0], a_sem.at[1], near_a)
    for slot in range(2):
        over_b[slot].wait_recv()
        own[2 + slot] = add(own[2 + slot], own_b[slot])
        if slot == 0:
            over_a.start()
    small_a.wait_recv()
    from_a[...] = add(from_b[:, a], from_a[...])

    def column(plane, action):
        @pl.when(plane != z)
        def _():
            action(
                remote(
                    from_a.at[plane],
                    from_z.at[z],
                    z_sem.at[0, plane],
                    z_sem.at[1, z],
                    me + 8 * (plane - z),
                )
            )

    for plane in range(PLANES):
        column(plane, lambda item: item.start())
    over_a.wait_recv()

    def down(chunk):
        part = pl.ds(chunk * height, height)
        return remote(
            own.at[3, part],
            own_high.at[part],
            high_sem.at[0, chunk],
            high_sem.at[1, chunk],
            me - 8,
        )

    for chunk in range(CHUNKS):
        part = pl.ds(chunk * height, height)
        own[3, part] = add(own[3, part], own_a[part])

        @pl.when(z < PLANES - 1)
        def _(chunk=chunk, part=part):
            down(chunk).wait_recv()
            own[3, part] = add(own[3, part], own_high[part])

        @pl.when(z > 0)
        def _(chunk=chunk):
            down(chunk).start()

    mats_ref[...] = own[3].astype(F32)
    ready[...] = from_a[z].astype(F32)
    for plane in range(PLANES):

        @pl.when(plane != z)
        def _(plane=plane):
            remote(
                from_a.at[plane], from_z.at[plane], z_sem.at[0, plane], z_sem.at[1, plane], twin
            ).wait_recv()
            ready[...] += from_z[plane].astype(F32)

    def home(device, half):
        place = device * rows + half * 8
        early = place < count
        owner = jnp.where(early, first_owner, root)
        spot = pl.multiple_of(jnp.where(early, first_row + place, place - count), 8)
        return owner, spot

    def piece(device, half):
        owner, spot = home(device, half)
        return remote(
            ready.at[pl.ds(half * 8, 8)],
            out_ref.at[pl.ds(spot, 8)],
            piece_sem.at[half],
            home_sem.at[device * 2 + half],
            owner,
        )

    for half in range(2):
        owner, spot = home(me, half)

        @pl.when(owner == me)
        def _(half=half, spot=spot):
            out_ref[pl.ds(spot, 8), :] = ready[half * 8 : half * 8 + 8, :]

        @pl.when(owner != me)
        def _(half=half):
            piece(me, half).start()

    def arrive(index, carry):
        device, half = index // 2, lax.rem(index, 2)
        owner, _ = home(device, half)

        @pl.when(jnp.logical_and(owner == me, device != me))
        def _():
            piece(device, half).wait_recv()

        return carry

    @pl.when(me >= first_owner)
    def _():
        lax.fori_loop(0, 64, arrive, 0)

    for half in range(2):
        owner, _ = home(me, half)

        @pl.when(owner != me)
        def _(half=half):
            piece(me, half).wait_send()

    lax.fori_loop(1, 32, vec_wait, 0)
    vec_sum_ref[...] = jnp.sum(vec_in[...], axis=0)
    for item in [gift, small_b, small_a, over_a] + gifts + over_b:
        item.wait_send()
    for plane in range(PLANES):
        column(plane, lambda item: item.wait_send())
    for chunk in range(CHUNKS):

        @pl.when(z > 0)
        def _(chunk=chunk):
            down(chunk).wait_send()


def homecoming(place_sums, first, vecs, owned, split, ident):
    rows = LENGTH // 32
    small = (rows, D)
    shape = first.shape[1:]
    return pl.pallas_call(
        functools.partial(homecoming_kernel, split),
        in_specs=[
            pl.BlockSpec(memory_space=pltpu.VMEM),
            pl.BlockSpec(memory_space=pl.ANY),
            pl.BlockSpec(memory_space=pltpu.VMEM),
        ],
        out_specs=[pl.BlockSpec(memory_space=pltpu.VMEM)] * 3,
        out_shape=[
            jax.ShapeDtypeStruct((owned, D), F32),
            jax.ShapeDtypeStruct(shape, F32),
            jax.ShapeDtypeStruct(vecs.shape[1:], F32),
        ],
        scratch_shapes=[
            pltpu.VMEM((4, 2, 2) + small, BF),
            pltpu.VMEM((4, 2, 2) + small, BF),
            pltpu.VMEM((4, 2) + small, BF),
            pltpu.VMEM((4,) + small, BF),
            pltpu.VMEM((4,) + small, BF),
            pltpu.VMEM(small, F32),
            pltpu.VMEM((4,) + shape, BF),
            pltpu.VMEM((4,) + shape, BF),
            pltpu.VMEM((2,) + shape, BF),
            pltpu.VMEM(shape, BF),
            pltpu.VMEM(shape, BF),
            pltpu.SemaphoreType.DMA((3, 2)),
            pltpu.SemaphoreType.DMA((2, 4)),
            pltpu.SemaphoreType.DMA((2,)),
            pltpu.SemaphoreType.DMA((64,)),
            pltpu.SemaphoreType.DMA((4,)),
            pltpu.SemaphoreType.DMA((2, 4)),
            pltpu.SemaphoreType.DMA((2, 2)),
            pltpu.SemaphoreType.DMA((2,)),
            pltpu.SemaphoreType.DMA((2, CHUNKS)),
            pltpu.VMEM(vecs.shape, F32),
            pltpu.SemaphoreType.DMA((2, 32)),
        ],
        compiler_params=pltpu.CompilerParams(
            collective_id=ident, has_side_effects=True, vmem_limit_bytes=40 * MB
        ),
        cost_estimate=pl.CostEstimate(
            flops=0, bytes_accessed=200_000_000, transcendentals=0
        ),
        name="homecoming",
    )(place_sums.reshape((4, 2, 2, 2) + small), first, vecs)


def forward_kernel(
    by_kernel,
    key_ref,
    found_ref,
    extra_ref,
    place_ref,
    w_ref,
    bias_ref,
    block_ref,
    x_ref,
    xb_ref,
    proj_ref,
    att_ref,
    lse_ref,
    *scratch,
):
    seq, head = pl.program_id(0), pl.program_id(1)
    pairs = HEADS // 2
    step = seq * (pairs + 1) + head
    if by_kernel:
        gather = RestSpread(block_ref, scratch[0], scratch[1:])
        for when, actions in gather.schedule().items():

            @pl.when(step == when)
            def _(actions=actions):
                for action in actions:
                    action()

    @pl.when(head == 0)
    def _():
        slots = lax.broadcasted_iota(jnp.int32, (LENGTH, found_ref.shape[0]), 1)
        picked = (key_ref[...] == slots).astype(BF)
        inputs = dot_nn(picked, found_ref[...]) + extra_ref[...].astype(F32)
        inputs = inputs + place_ref[...].astype(F32)
        x_ref[...] = inputs
        inputs_b = inputs.astype(BF)
        xb_ref[...] = inputs_b
        for start in range(0, QKV, D):
            cols = slice(start, start + D)
            part = dot_nt(inputs_b, w_ref[cols, :]) + bias_ref[:, cols]
            proj_ref[:, cols] = part.astype(BF)

    @pl.when(head > 0)
    def _():
        width = 2 * HEAD_DIM
        start = (head - 1) * width
        query = proj_ref[:, pl.ds(pl.multiple_of(start, width), width)]
        keys = proj_ref[:, pl.ds(pl.multiple_of(D + start, width), width)]
        values_t = proj_ref[:, pl.ds(pl.multiple_of(2 * D + start, width), width)].T
        lane = lax.broadcasted_iota(jnp.int32, query.shape, 1)
        outs = []
        for half in range(2):
            mine = (lane < HEAD_DIM) if half == 0 else (lane >= HEAD_DIM)
            picked = jnp.where(mine, query, jnp.zeros_like(query))
            scores = dot_nt(keys, picked)
            highest = jnp.max(scores, 0, keepdims=True)
            expo = jnp.exp2((scores - highest) * (SCORE * LOG2E))
            total = jnp.sum(expo, 0, keepdims=True)
            part = values_t[half * HEAD_DIM : (half + 1) * HEAD_DIM, :]
            outs.append(dot_nn(part, expo.astype(BF)) / total)
            lse_ref[0, half : half + 1, :] = highest * (SCORE * LOG2E) + jnp.log2(total)
        att_ref[...] = jnp.concatenate(outs, 0).T.astype(BF)


def forward(by_kernel, key, found, extra, places, w_qkv, bias, block, ident):
    rows = key.shape[0]
    seqs = rows // LENGTH
    pairs = HEADS // 2
    slots = found.shape[0]

    def row(width):
        return pl.BlockSpec((LENGTH, width), lambda s, h: (s, 0))

    def steady(shape):
        return pl.BlockSpec(
            shape, lambda s, h: (0, 0), pipeline_mode=pl.Buffered(buffer_count=1)
        )

    out_specs = [
        row(D),
        row(D),
        row(QKV),
        pl.BlockSpec((LENGTH, 2 * HEAD_DIM), lambda s, h: (s, jnp.maximum(h - 1, 0))),
        pl.BlockSpec(
            (1, 2, LENGTH), lambda s, h: (s * pairs + jnp.maximum(h - 1, 0), 0, 0)
        ),
    ]
    out_shape = [
        jax.ShapeDtypeStruct((rows, D), F32),
        jax.ShapeDtypeStruct((rows, D), BF),
        jax.ShapeDtypeStruct((rows, QKV), BF),
        jax.ShapeDtypeStruct((rows, D), BF),
        jax.ShapeDtypeStruct((seqs * pairs, 2, LENGTH), F32),
    ]
    params = {}
    scratch = []
    if by_kernel:
        out_specs.append(pl.BlockSpec(memory_space=pl.ANY))
        out_shape.append(jax.ShapeDtypeStruct((24,) + block.shape, BF))
        params = dict(collective_id=ident, has_side_effects=True)
        scratch = RestSpread.scratch()
    return pl.pallas_call(
        functools.partial(forward_kernel, by_kernel),
        grid=(seqs, pairs + 1),
        in_specs=[
            row(1),
            steady((slots, D)),
            row(D),
            steady((LENGTH, D)),
            steady((QKV, D)),
            steady((1, QKV)),
            pl.BlockSpec(memory_space=pl.ANY),
        ],
        out_specs=out_specs,
        out_shape=out_shape,
        scratch_shapes=scratch,
        compiler_params=pltpu.CompilerParams(vmem_limit_bytes=56 * MB, **params),
        cost_estimate=pl.CostEstimate(
            flops=40_000_000_000, bytes_accessed=60_000_000, transcendentals=0
        ),
        name="forward",
    )(key, found, extra, places, w_qkv, bias, block)


def backward_kernel(
    by_kernel,
    q_ref,
    k_ref,
    v_ref,
    att_ref,
    g_ref,
    lse_ref,
    first_ref,
    xb_ref,
    key_ref,
    sums_ref,
    w_ref,
    rest_ref,
    grad_ref,
    place_ref,
    weights_ref,
    sent_ref,
    bias_ref,
    mats_ref,
    proj,
    total,
    places,
    sent,
    *scratch,
):
    seq, head = pl.program_id(0), pl.program_id(1)
    pairs = HEADS // 2
    step = seq * (pairs + 1) + head

    @pl.when(step == 0)
    def _():
        total[...] = jnp.zeros_like(total)
        places[...] = jnp.zeros_like(places)
        sent[...] = jnp.zeros_like(sent)
        bias_ref[...] = sums_ref[...]
        mats_ref[...] = jnp.zeros_like(mats_ref)

    if by_kernel:
        sums = RestSums(rest_ref, mats_ref, scratch)
        for when, actions in sums.schedule().items():

            @pl.when(step == when)
            def _(actions=actions):
                for action in actions:
                    action()

    @pl.when(head < pairs)
    def _():
        cols = pl.ds(pl.multiple_of(head * 2 * HEAD_DIM, 2 * HEAD_DIM), 2 * HEAD_DIM)
        query = q_ref[...]
        keys = k_ref[...]
        values = v_ref[...]
        grad = g_ref[...]
        lane = lax.broadcasted_iota(jnp.int32, query.shape, 1)
        first = lane < HEAD_DIM
        product = (att_ref[...].astype(F32) * grad.astype(F32)).T
        zero = jnp.zeros_like(query)
        g_q, g_k, g_v = [], [], []
        for half in range(2):
            mine = first if half == 0 else jnp.logical_not(first)
            scores = dot_nt(keys, jnp.where(mine, query, zero))
            probs = jnp.exp2(scores * (SCORE * LOG2E) - lse_ref[0, half : half + 1, :])
            delta = jnp.sum(
                product[half * HEAD_DIM : (half + 1) * HEAD_DIM, :], 0, keepdims=True
            )
            g_probs = dot_nt(values, jnp.where(mine, grad, zero))
            g_v.append(dot_nn(probs.astype(BF), grad))
            g_scores = (probs * (g_probs - delta)).astype(BF)
            g_k.append(dot_nn(g_scores, query))
            g_q.append(dot_tn(g_scores, keys))
        grad_q = jnp.where(first, g_q[0], g_q[1]) * SCORE
        grad_k = jnp.where(first, g_k[0], g_k[1]) * SCORE
        grad_v = jnp.where(first, g_v[0], g_v[1])
        proj[0, :, cols] = grad_q.astype(BF)
        proj[1, :, cols] = grad_k.astype(BF)
        proj[2, :, cols] = grad_v.astype(BF)
        bias_ref[0:1, cols] += jnp.sum(grad_q, 0, keepdims=True)
        bias_ref[1:2, cols] += jnp.sum(grad_v, 0, keepdims=True)

    @pl.when(head == pairs)
    def _():
        g_in = first_ref[...]
        inputs_b = xb_ref[...]
        for part in range(3):
            cols = slice(part * D, (part + 1) * D)
            g_in = g_in + dot_nn(proj[part], w_ref[cols, :])
            total[cols, :] += dot_tn(proj[part], inputs_b)
        g_in_b = g_in.astype(BF)
        grad_ref[...] = g_in_b
        places[...] += g_in
        slots = lax.broadcasted_iota(jnp.int32, (LENGTH, sent.shape[0]), 1)
        sent[...] += dot_tn((key_ref[...] == slots).astype(BF), g_in_b)

    @pl.when(step == pl.num_programs(0) * (pairs + 1) - 1)
    def _():
        sent_ref[...] = sent[...].astype(BF)
        weights_ref[...] = total[...].astype(BF)
        place_ref[...] = places[...].astype(BF)


def backward(
    by_kernel, projected, attended, grad_att, lse, g_first, inputs_b, key, sums, room, w_qkv, rest, ident
):
    rows = projected.shape[0]
    seqs = rows // LENGTH
    pairs = HEADS // 2
    block = (LENGTH, 2 * HEAD_DIM)
    shape = rest.shape[1:]

    def pair(offset):
        return pl.BlockSpec(block, lambda s, h: (s, offset + jnp.minimum(h, pairs - 1)))

    def row(width):
        return pl.BlockSpec((LENGTH, width), lambda s, h: (s, 0))

    def steady(shape):
        return pl.BlockSpec(
            shape, lambda s, h: (0, 0), pipeline_mode=pl.Buffered(buffer_count=1)
        )

    def kept(shape):
        return pl.BlockSpec(shape, lambda s, h: (0, 0))

    return pl.pallas_call(
        functools.partial(backward_kernel, by_kernel),
        grid=(seqs, pairs + 1),
        in_specs=[
            pair(0),
            pair(pairs),
            pair(2 * pairs),
            pair(0),
            pair(0),
            pl.BlockSpec(
                (1, 2, LENGTH), lambda s, h: (s * pairs + jnp.minimum(h, pairs - 1), 0, 0)
            ),
            row(D),
            row(D),
            row(1),
            steady((16, D)),
            steady((QKV, D)),
            pl.BlockSpec(memory_space=pl.ANY),
        ],
        out_specs=[
            row(D),
            kept((LENGTH, D)),
            kept((QKV, D)),
            kept((room, D)),
            kept((16, D)),
            kept(shape),
        ],
        out_shape=[
            jax.ShapeDtypeStruct((rows, D), BF),
            jax.ShapeDtypeStruct((LENGTH, D), BF),
            jax.ShapeDtypeStruct((QKV, D), BF),
            jax.ShapeDtypeStruct((room, D), BF),
            jax.ShapeDtypeStruct((16, D), F32),
            jax.ShapeDtypeStruct(shape, F32),
        ],
        scratch_shapes=[
            pltpu.VMEM((3, LENGTH, D), BF),
            pltpu.VMEM((QKV, D), F32),
            pltpu.VMEM((LENGTH, D), F32),
            pltpu.VMEM((room, D), F32),
        ]
        + (RestSums.scratch(shape) if by_kernel else []),
        compiler_params=pltpu.CompilerParams(
            vmem_limit_bytes=60 * MB,
            **(dict(collective_id=ident, has_side_effects=True) if by_kernel else {}),
        ),
        cost_estimate=pl.CostEstimate(
            flops=60_000_000_000, bytes_accessed=60_000_000, transcendentals=0
        ),
        name="backward",
    )(
        projected,
        projected,
        projected,
        attended,
        grad_att,
        lse,
        g_first,
        inputs_b,
        key,
        sums,
        w_qkv,
        rest,
    )


def slots_of(ids, owned):
    count = ids.shape[0]
    order = jnp.arange(count, dtype=jnp.int32)
    repeated = jnp.any(
        (ids[:, None] == ids[None, :]) & (order[:, None] < order[None, :]), axis=0
    )
    first = jnp.logical_not(repeated)
    base = (ids // owned) * owned
    below = (
        first[:, None]
        & (ids[:, None] >= base[None, :])
        & (ids[:, None] < ids[None, :])
    )
    return jnp.sum(below.astype(jnp.int32), axis=0)


def requests_of(ids, owner, slot, owned, devices, start, room):
    key = jnp.where((slot >= start) & (slot < start + room), owner * room + slot - start, -1)
    spots = jnp.arange(devices * room, dtype=jnp.int32)
    asked = jnp.max(
        jnp.where(key[:, None] == spots[None, :], (ids - owner * owned)[:, None], -1), axis=0
    )
    return key, asked


def pick(index, amount):
    return (index[:, None] == jnp.arange(amount, dtype=jnp.int32)[None, :]).astype(BF)


def adam_direction(param, first, second, grad, corr_one, corr_two, decay):
    first_next = beta_one * first + (1.0 - beta_one) * grad
    second_next = beta_two * second + (1.0 - beta_two) * grad * grad
    update = first_next / corr_one / (jnp.sqrt(second_next / corr_two) + adam_eps)
    return (update + decay * param, first_next)


def body(
    devices,
    token_ids,
    masked,
    swap_kind,
    swap_ids,
    out_grad,
    embed_table,
    table_first,
    table_second,
    layer_mats,
    mats_first,
    mats_second,
    layer_vecs,
    vecs_first,
    vecs_second,
):
    axis = "fsdp"
    rows = token_ids.shape[0]
    owned = embed_table.shape[0]
    entries = layer_vecs.shape[0]
    columns = layer_mats.shape[1]
    me = lax.axis_index(axis)
    by_kernel = devices == 32
    split = place_split(devices, owned)
    replaced = jnp.where(swap_kind < 8, mask_token, jnp.where(swap_kind == 8, swap_ids, token_ids))
    chosen = jnp.where(masked == 1, replaced, token_ids)

    def swap(blocks):
        return lax.all_to_all(blocks, axis, 0, 0, tiled=True)

    block = layer_mats.astype(BF).T

    room = 16 * -(-1536 // (16 * devices))
    more = 16
    owner = chosen // owned
    slot = slots_of(chosen, owned)
    most = jnp.max(slot) + 1
    key, asked = requests_of(chosen, owner, slot, owned, devices, 0, room)
    _, asked_more = requests_of(chosen, owner, slot, owned, devices, room, more)
    table_b = embed_table.astype(BF)
    own_vecs = layer_vecs.astype(BF).astype(F32)
    notes = jnp.concatenate(
        [
            asked.reshape(devices, room).astype(F32),
            asked_more.reshape(devices, more).astype(F32),
            jnp.broadcast_to(own_vecs[None], (devices, entries)),
            jnp.broadcast_to(most.astype(F32), (devices, 1)),
        ],
        axis=1,
    )
    notes = swap(notes)
    wanted = notes[:, :room].astype(jnp.int32).reshape(-1)
    wanted_more = notes[:, room : room + more].astype(jnp.int32).reshape(-1)
    vecs = notes[:, room + more : room + more + entries].reshape(-1)
    longest = jnp.max(notes[:, room + more + entries]).astype(jnp.int32)
    found = dot_nn(pick(wanted, owned), table_b).astype(BF)
    found, table, block = lax.optimization_barrier((found, embed_table, block))
    found = swap(found.reshape(devices, room, D)).reshape(-1, D)
    if by_kernel:
        places, w_qkv = broadcast(table, block, split, 1)
        w_qkv = w_qkv.reshape(QKV, D)
    else:
        spots = VOCAB + jnp.arange(LENGTH, dtype=jnp.int32) - me * owned
        places = lax.psum(dot_nn(pick(spots, owned), table_b), axis).astype(BF)
        mats_t = lax.all_gather(block, axis, axis=0, tiled=True)
        w_qkv, rest = mats_t[:QKV], mats_t[QKV:]
    rounds = (longest - room + more - 1) // more

    def further(turn):
        key, asked = requests_of(chosen, owner, slot, owned, devices, room + turn * more, more)
        wanted = lax.cond(
            turn == 0,
            lambda: wanted_more,
            lambda: swap(asked.reshape(devices, more)).reshape(-1),
        )
        return key, wanted

    def fetch_more(state):
        turn, extra = state
        key, wanted = further(turn)
        found = dot_nn(pick(wanted, owned), table_b).astype(BF)
        found = swap(found.reshape(devices, more, D)).reshape(-1, D)
        return turn + 1, extra + dot_nn(pick(key, devices * more), found).astype(BF)

    _, extra = lax.while_loop(
        lambda state: state[0] < rounds,
        fetch_more,
        (jnp.int32(0), jnp.zeros((rows, D), BF)),
    )

    bias_qkv = jnp.concatenate([vecs[:D], jnp.zeros((D,), F32), vecs[D : 2 * D]])[None]
    bias_up = vecs[5 * D : 5 * D + FF][None]
    small = jnp.concatenate(
        [vecs[2 * D : 5 * D], vecs[5 * D + FF :], jnp.zeros((2 * D,), F32)]
    ).reshape(8, D)

    results = forward(by_kernel, key[:, None], found, extra, places, w_qkv, bias_qkv, block, 4)
    inputs, inputs_b, projected, attended, lse = results[:5]
    if by_kernel:
        rest = results[5].reshape(-1, D)
    (
        outputs,
        normed_b,
        hidden_b,
        g_mid_b,
        g_up_b,
        g_first,
        g_first_b,
        g_att_b,
        sums,
    ) = middle(attended, inputs, out_grad, masked[:, None], rest, small, bias_up)
    g_rest = rest_gradients(g_first_b, attended, g_up_b, normed_b, hidden_b, g_mid_b)
    input_grad, g_places, g_qkv, sent, sums, rest_grad = backward(
        by_kernel,
        projected,
        attended,
        g_att_b,
        lse,
        g_first,
        inputs_b,
        key[:, None],
        sums,
        devices * room,
        w_qkv,
        g_rest.reshape(-1, columns, D),
        2,
    )

    g_vecs = sums[:12].reshape(devices, entries)
    sent, g_places, g_qkv = lax.optimization_barrier((sent, g_places, g_qkv))
    sent = swap(sent.reshape(devices, room, D)).reshape(-1, D)
    if by_kernel:
        padded = jnp.pad(g_vecs, ((0, 0), (0, 1024 - entries))).reshape(devices, 8, 128)
        g_own_places, first_grad, vecs_grad = homecoming(
            g_places, g_qkv.reshape(-1, columns, D), padded, owned, split, 3
        )
        vecs_grad = vecs_grad.reshape(1024)[:entries]
        mats_grad = jnp.where(me < QKV // columns, first_grad, rest_grad).T
    else:
        vecs_grad = jnp.sum(swap(g_vecs), axis=0)
        total = lax.psum(g_places.astype(F32), axis)
        spots = me * owned + jnp.arange(owned, dtype=jnp.int32) - VOCAB
        inside = (spots >= 0) & (spots < LENGTH)
        g_own_places = jnp.where(
            inside[:, None], total[jnp.clip(spots, 0, LENGTH - 1)], 0.0
        )
        mats_grad = lax.psum_scatter(
            jnp.concatenate([g_qkv, g_rest], axis=0), axis, scatter_dimension=0, tiled=True
        )
        mats_grad = mats_grad.astype(F32).T
    table_grad = dot_tn(pick(wanted, owned), sent) + g_own_places

    def send_more(state):
        turn, total = state
        key, wanted = further(turn)
        sent = dot_tn(pick(key, devices * more), input_grad).astype(BF)
        sent = swap(sent.reshape(devices, more, D)).reshape(-1, D)
        return turn + 1, total + dot_tn(pick(wanted, owned), sent)

    _, table_grad = lax.while_loop(
        lambda state: state[0] < rounds, send_more, (jnp.int32(0), table_grad)
    )

    counter = jnp.float32(STEP)
    corr_one = 1.0 - jnp.power(jnp.float32(beta_one), counter)
    corr_two = 1.0 - jnp.power(jnp.float32(beta_two), counter)
    table_step, table_first_next = adam_direction(
        embed_table, table_first, table_second, table_grad, corr_one, corr_two, decay_rate
    )
    mats_step, mats_first_next = adam_direction(
        layer_mats, mats_first, mats_second, mats_grad, corr_one, corr_two, decay_rate
    )
    vecs_step, vecs_first_next = adam_direction(
        layer_vecs, vecs_first, vecs_second, vecs_grad, corr_one, corr_two, 0.0
    )
    return (
        outputs,
        input_grad,
        table_grad,
        mats_grad,
        vecs_grad,
        table_step,
        table_first_next,
        mats_step,
        mats_first_next,
        vecs_step,
        vecs_first_next,
    )


def solution(mesh):
    line = P("fsdp")
    by_rows = P("fsdp", None)
    by_cols = P(None, "fsdp")
    return jax.shard_map(
        functools.partial(body, mesh.shape["fsdp"]),
        mesh=mesh,
        in_specs=(
            line,
            line,
            line,
            line,
            by_rows,
            by_rows,
            by_rows,
            by_rows,
            by_cols,
            by_cols,
            by_cols,
            line,
            line,
            line,
        ),
        out_specs=(
            by_rows,
            by_rows,
            by_rows,
            by_cols,
            line,
            by_rows,
            by_rows,
            by_cols,
            by_cols,
            line,
            line,
        ),
        check_vma=False,
    )
```

```python
import functools

import jax
import jax.numpy as jnp
from jax import lax
from jax.experimental import pallas as pl
from jax.experimental.pallas import tpu as pltpu
from jax.sharding import PartitionSpec as P

D = 768
HEADS = 12
HEAD_DIM = 64
FF = 3072
VOCAB = 14592
LENGTH = 512
STEP = 10
QKV = 3 * D

norm_eps = 1e-12
mask_token = 103
beta_one = 0.9
beta_two = 0.999
adam_eps = 1e-06
decay_rate = 0.01

BF = jnp.bfloat16
F32 = jnp.float32
LOG2E = 1.4426950408889634
SCORE = HEAD_DIM ** (-0.5)
MB = 1024 * 1024

ROW_TILE = 256


def dot_nn(left, right):
    return lax.dot_general(
        left, right, (((1,), (0,)), ((), ())), preferred_element_type=F32
    )


def dot_nt(left, right):
    return lax.dot_general(
        left, right, (((1,), (1,)), ((), ())), preferred_element_type=F32
    )


def dot_tn(left, right):
    return lax.dot_general(
        left, right, (((0,), (0,)), ((), ())), preferred_element_type=F32
    )


def gelu_parts(values):
    size = jnp.abs(values)
    frac = 1.0 / (1.0 + (0.3275911 * 0.7071067811865476) * size)
    expo = jnp.exp2(values * values * (-0.5 * LOG2E))
    poly = 1.061405429 * 0.5
    for coef in (-1.453152027, 1.421413741, -0.284496736, 0.254829592):
        poly = poly * frac + 0.5 * coef
    tail = poly * frac * expo
    cdf = jnp.where(values >= 0, 1.0 - tail, tail)
    return values * cdf, cdf + values * expo * 0.3989422804014327


def norm_parts(total):
    centre = jnp.mean(total, -1, keepdims=True)
    centered = total - centre
    variance = jnp.mean(centered * centered, -1, keepdims=True)
    scale = lax.rsqrt(variance + norm_eps)
    return centered * scale, scale


def norm_back(scaled, unit, scale):
    return scale * (
        scaled
        - jnp.mean(scaled, -1, keepdims=True)
        - unit * jnp.mean(scaled * unit, -1, keepdims=True)
    )


def middle_kernel(
    att_ref,
    x_ref,
    go_ref,
    mask_ref,
    wout_ref,
    up_0,
    up_1,
    up_2,
    up_3,
    down_0,
    down_1,
    down_2,
    down_3,
    vec_ref,
    bup_ref,
    out_ref,
    normed_ref,
    hidden_ref,
    gmid_ref,
    gup_ref,
    gfirst_ref,
    gfirstb_ref,
    gatt_ref,
    sums_ref,
    slope_ref,
):
    @pl.when(pl.program_id(0) == 0)
    def _():
        sums_ref[...] = jnp.zeros_like(sums_ref)

    ups = (up_0, up_1, up_2, up_3)
    downs = (down_0, down_1, down_2, down_3)
    bias_out = vec_ref[0:1, :]
    gain_one = vec_ref[1:2, :]
    shift_one = vec_ref[2:3, :]
    bias_down = vec_ref[3:4, :]
    gain_two = vec_ref[4:5, :]
    shift_two = vec_ref[5:6, :]

    def note(row, values):
        sums_ref[row : row + 1, :] += jnp.sum(values, 0, keepdims=True)

    branch = dot_nt(att_ref[...], wout_ref[...]) + bias_out
    unit_one, scale_one = norm_parts(x_ref[...] + branch)
    normed = unit_one * gain_one + shift_one
    normed_b = normed.astype(BF)
    normed_ref[...] = normed_b
    downward = jnp.zeros(normed.shape, F32)
    for start in range(0, FF, D):
        cols = slice(start, start + D)
        upward = dot_nt(normed_b, ups[start // D][...]) + bup_ref[0:1, cols]
        hidden, slope = gelu_parts(upward)
        slope_ref[:, cols] = slope
        hidden_b = hidden.astype(BF)
        hidden_ref[:, cols] = hidden_b
        downward += dot_nn(hidden_b, downs[start // D][...])
    unit_two, scale_two = norm_parts(normed + downward + bias_down)
    out_ref[...] = (unit_two * gain_two + shift_two).astype(BF)
    g_out = go_ref[...].astype(F32) * mask_ref[...].astype(F32)
    note(10, g_out * unit_two)
    note(11, g_out)
    g_mid = norm_back(g_out * gain_two, unit_two, scale_two)
    note(9, g_mid)
    g_mid_b = g_mid.astype(BF)
    gmid_ref[...] = g_mid_b
    g_normed = g_mid
    for start in range(0, FF, D):
        cols = slice(start, start + D)
        g_up = dot_nt(g_mid_b, downs[start // D][...]) * slope_ref[:, cols]
        note(5 + start // D, g_up)
        g_up_b = g_up.astype(BF)
        gup_ref[:, cols] = g_up_b
        g_normed += dot_nn(g_up_b, ups[start // D][...])
    note(3, g_normed * unit_one)
    note(4, g_normed)
    g_first = norm_back(g_normed * gain_one, unit_one, scale_one)
    note(2, g_first)
    gfirst_ref[...] = g_first
    g_first_b = g_first.astype(BF)
    gfirstb_ref[...] = g_first_b
    gatt_ref[...] = dot_nn(g_first_b, wout_ref[...]).astype(BF)


def middle(attended, inputs, out_grad, masked, rest, vecs, bias_up):
    rows = attended.shape[0]
    tile = ROW_TILE

    def row(width):
        return pl.BlockSpec((tile, width), lambda i: (i, 0))

    def whole(shape, place=0):
        return pl.BlockSpec(
            shape, lambda i: (place, 0), pipeline_mode=pl.Buffered(buffer_count=1)
        )

    return pl.pallas_call(
        middle_kernel,
        grid=(rows // tile,),
        in_specs=[
            row(D),
            row(D),
            row(D),
            row(1),
            *[whole((D, D), place) for place in range(9)],
            whole((8, D)),
            whole((1, FF)),
        ],
        out_specs=[
            row(D),
            row(D),
            row(FF),
            row(D),
            row(FF),
            row(D),
            row(D),
            row(D),
            pl.BlockSpec((16, D), lambda i: (0, 0)),
        ],
        out_shape=[
            jax.ShapeDtypeStruct((rows, D), BF),
            jax.ShapeDtypeStruct((rows, D), BF),
            jax.ShapeDtypeStruct((rows, FF), BF),
            jax.ShapeDtypeStruct((rows, D), BF),
            jax.ShapeDtypeStruct((rows, FF), BF),
            jax.ShapeDtypeStruct((rows, D), F32),
            jax.ShapeDtypeStruct((rows, D), BF),
            jax.ShapeDtypeStruct((rows, D), BF),
            jax.ShapeDtypeStruct((16, D), F32),
        ],
        scratch_shapes=[pltpu.VMEM((tile, FF), F32)],
        compiler_params=pltpu.CompilerParams(vmem_limit_bytes=56 * MB),
        name="middle",
    )(attended, inputs, out_grad, masked, *[rest] * 9, vecs, bias_up)


def fixed(shape, place=0):
    return pl.BlockSpec(
        shape, lambda i: (place, 0), pipeline_mode=pl.Buffered(buffer_count=1)
    )


def rest_kernel(first_ref, att_ref, up_ref, normed_ref, hidden_ref, mid_ref, out_ref):
    step = pl.program_id(0)
    chunks = FF // D

    @pl.when(step == 0)
    def _():
        out_ref[...] = dot_tn(first_ref[...], att_ref[...]).astype(BF)

    @pl.when(jnp.logical_and(step > 0, step <= chunks))
    def _():
        out_ref[...] = dot_tn(up_ref[...], normed_ref[...]).astype(BF)

    @pl.when(step > chunks)
    def _():
        out_ref[...] = dot_tn(hidden_ref[...], mid_ref[...]).astype(BF)


def rest_gradients(g_first_b, attended, g_up_b, normed_b, hidden_b, g_mid_b):
    rows = attended.shape[0]
    chunks = FF // D
    full = fixed((rows, D))
    return pl.pallas_call(
        rest_kernel,
        grid=(1 + 2 * chunks,),
        in_specs=[
            full,
            full,
            pl.BlockSpec((rows, D), lambda i: (0, jnp.clip(i - 1, 0, chunks - 1))),
            full,
            pl.BlockSpec((rows, D), lambda i: (0, jnp.clip(i - 1 - chunks, 0, chunks - 1))),
            full,
        ],
        out_specs=pl.BlockSpec((D, D), lambda i: (i, 0)),
        out_shape=jax.ShapeDtypeStruct((D + 2 * FF, D), BF),
        compiler_params=pltpu.CompilerParams(vmem_limit_bytes=56 * MB),
        cost_estimate=pl.CostEstimate(
            flops=22_000_000_000, bytes_accessed=50_000_000, transcendentals=0
        ),
        name="rest_gradients",
    )(g_first_b, attended, g_up_b, normed_b, hidden_b, g_mid_b)


MESH = pl.DeviceIdType.MESH
PLANES = 4


def neighbours():
    me = lax.axis_index("fsdp")
    core = lax.rem(me, 2)
    x = lax.rem(me // 2, 2)
    y = lax.rem(me // 4, 2)
    z = me // 8
    step_a = 4 - 2 * core
    step_b = 2 + 2 * core
    a = jnp.where(core == 0, y, x)
    b = jnp.where(core == 0, x, y)
    near_a = me + step_a * (1 - 2 * a)
    near_b = me + step_b * (1 - 2 * b)
    twin = me + 1 - 2 * core
    return me, core, z, a, b, step_a, step_b, near_a, near_b, twin


def greet(me, z, near_a, near_b, twin):
    barrier = pltpu.get_barrier_semaphore()

    def hello(device):
        pl.semaphore_signal(barrier, inc=1, device_id=(device,), device_id_type=MESH)

    for device in (near_a, near_b, twin):
        hello(device)

    @pl.when(z > 0)
    def _():
        hello(me - 8)

    @pl.when(z < PLANES - 1)
    def _():
        hello(me + 8)

    inner = jnp.logical_and(z > 0, z < PLANES - 1)
    pl.semaphore_wait(barrier, jnp.where(inner, 5, 4))


class RestSpread:
    def __init__(self, in_ref, out_ref, scratch):
        self.in_ref, self.out_ref = in_ref, out_ref
        self.own_sem, self.send_sem, self.recv_sem = scratch
        self.place = neighbours()

    @staticmethod
    def scratch():
        return [
            pltpu.SemaphoreType.DMA,
            pltpu.SemaphoreType.DMA((5, 24)),
            pltpu.SemaphoreType.DMA((24,)),
        ]

    def copy(self, shard, device, kind, source=None):
        return pltpu.make_async_remote_copy(
            src_ref=self.out_ref.at[shard] if source is None else source,
            dst_ref=self.out_ref.at[shard],
            send_sem=self.send_sem.at[kind, shard],
            recv_sem=self.recv_sem.at[shard],
            device_id=(device,),
            device_id_type=MESH,
        )

    def shard(self, plane, other_a, other_b):
        me, core, z, a, b, step_a, step_b, near_a, near_b, twin = self.place
        a_at = 1 - a if other_a else a
        b_at = 1 - b if other_b else b
        return jnp.maximum(plane - 1, 0) * 8 + a_at * step_a + b_at * step_b + core

    def planes(self, far):
        z = self.place[2]
        for way in (1, -1) if far else (1,):
            plane = z - way * far
            yield way, plane, jnp.logical_and(plane >= 1, plane < PLANES)

    def routes(self, far):
        me, core, z, a, b, step_a, step_b, near_a, near_b, twin = self.place
        for way, plane, there in self.planes(far):
            shard = self.shard(plane, False, False)
            for onward in (way,) if far else (1, -1):
                goes = jnp.logical_and(z + onward >= 0, z + onward < PLANES)
                yield (
                    jnp.logical_and(there, goes),
                    shard,
                    me + 8 * onward,
                    0 if onward == 1 else 1,
                )
            yield there, shard, near_a, 2
            yield there, shard, near_b, 3
            yield there, shard, twin, 4

    def routes_a(self, far):
        near_b, twin = self.place[8:]
        for way, plane, there in self.planes(far):
            shard = self.shard(plane, True, False)
            yield there, shard, near_b, 3
            yield there, shard, twin, 4

    def routes_b(self, far):
        twin = self.place[9]
        for way, plane, there in self.planes(far):
            for other_a in (False, True):
                yield there, self.shard(plane, other_a, True), twin, 4

    def own(self):
        return pltpu.make_async_copy(
            self.in_ref, self.out_ref.at[self.shard(self.place[2], False, False)], self.own_sem
        )

    def start(self):
        me, core, z, a, b, step_a, step_b, near_a, near_b, twin = self.place
        greet(me, z, near_a, near_b, twin)

        @pl.when(z > 0)
        def _():
            self.own().start()

        for goes, shard, device, kind in self.routes(0):
            pl.when(goes)(
                lambda shard=shard, device=device, kind=kind: self.copy(
                    shard, device, kind, self.in_ref
                ).start()
            )

    def pass_on(self, routes):
        seen = []
        for goes, shard, device, kind in routes:
            if kind == 4:
                seen.append((goes, shard))
        for goes, shard in seen:
            pl.when(goes)(
                lambda shard=shard: self.copy(shard, self.place[9], 4).wait_recv()
            )
            for other, place, device, kind in routes:
                if place is shard:
                    pl.when(other)(
                        lambda shard=shard, device=device, kind=kind: self.copy(
                            shard, device, kind
                        ).start()
                    )

    def column(self, far):
        self.pass_on(list(self.routes(far)))

    def along_a(self, far):
        self.pass_on(list(self.routes_a(far)))

    def along_b(self, far):
        self.pass_on(list(self.routes_b(far)))

    def end(self):
        me, core, z, a, b, step_a, step_b, near_a, near_b, twin = self.place

        def from_twin(place, carry):
            self.copy(place * 2 + 1 - core, twin, 4).wait_recv()
            return carry

        lax.fori_loop(0, 12, from_twin, 0)
        for far in range(PLANES):
            for routes in (self.routes(far), self.routes_a(far), self.routes_b(far)):
                for goes, shard, device, kind in routes:
                    pl.when(goes)(
                        lambda shard=shard, device=device, kind=kind: self.copy(
                            shard, device, kind
                        ).wait_send()
                    )

        @pl.when(z > 0)
        def _():
            self.own().wait()

    def schedule(self):
        return {
            0: [self.start],
            6: [lambda: self.column(1)],
            11: [lambda: self.column(2), lambda: self.along_a(0)],
            13: [lambda: self.along_a(1)],
            16: [lambda: self.column(3)],
            21: [lambda: self.along_a(2), lambda: self.along_a(3)],
            23: [lambda: self.along_b(0)],
            24: [lambda: self.along_b(1)],
            25: [lambda: self.along_b(2)],
            26: [lambda: self.along_b(3)],
            27: [self.end],
        }


class RestSums:
    TURNS = PLANES - 1

    def __init__(self, in_ref, out_ref, scratch):
        self.in_ref, self.out_ref = in_ref, out_ref
        (
            self.own,
            self.from_twin,
            self.from_b,
            self.from_a,
            self.from_low,
            self.from_high,
            self.load_sem,
            self.twin_sem,
            self.b_sem,
            self.a_sem,
            self.low_sem,
            self.high_sem,
        ) = scratch
        self.place = neighbours()

    @staticmethod
    def scratch(shape):
        return [
            pltpu.VMEM((12,) + shape, BF),
            pltpu.VMEM((12,) + shape, BF),
            pltpu.VMEM((6,) + shape, BF),
            pltpu.VMEM((3,) + shape, BF),
            pltpu.VMEM((4,) + shape, BF),
            pltpu.VMEM((4,) + shape, BF),
            pltpu.SemaphoreType.DMA((12,)),
            pltpu.SemaphoreType.DMA((2, 12)),
            pltpu.SemaphoreType.DMA((2, 6)),
            pltpu.SemaphoreType.DMA((2, 3)),
            pltpu.SemaphoreType.DMA((2, 4)),
            pltpu.SemaphoreType.DMA((2, 4)),
        ]

    def remote(self, source, target, sems, slot, device):
        return pltpu.make_async_remote_copy(
            src_ref=source,
            dst_ref=target.at[slot],
            send_sem=sems.at[0, slot],
            recv_sem=sems.at[1, slot],
            device_id=(device,),
            device_id_type=MESH,
        )

    def plane_of(self, turn):
        z = self.place[2]
        last = PLANES - 1 - turn
        inner = (1, 3, 2)[turn]
        return jnp.where(z < 2, last, jnp.where(z == 2, inner, 1 + turn))

    def shards(self, slot):
        me, core, z, a, b, step_a, step_b, near_a, near_b, twin = self.place
        other_b, turn, other_a = slot < 6, slot % 6 // 2, slot % 2 == 0
        base = (self.plane_of(turn) - 1) * 8
        a_at = 1 - a if other_a else a
        b_at = 1 - b if other_b else b
        mine = base + a_at * step_a + b_at * step_b + core
        a_at = 1 - b if other_a else b
        b_at = 1 - a if other_b else a
        twins = base + a_at * step_b + b_at * step_a + 1 - core
        return mine, twins

    def load(self, slot):
        return pltpu.make_async_copy(
            self.in_ref.at[self.shards(slot)[0]], self.own.at[slot], self.load_sem.at[slot]
        )

    def gift(self, slot):
        return self.remote(
            self.in_ref.at[self.shards(slot)[1]],
            self.from_twin,
            self.twin_sem,
            slot,
            self.place[9],
        )

    def over_b(self, slot):
        return self.remote(self.own.at[slot], self.from_b, self.b_sem, slot, self.place[8])

    def over_a(self, turn):
        return self.remote(
            self.own.at[6 + 2 * turn], self.from_a, self.a_sem, turn, self.place[7]
        )

    def along(self, turn, up):
        plane = self.plane_of(turn)
        source = self.own.at[7 + 2 * turn]
        if up:
            return self.remote(source, self.from_low, self.low_sem, plane, self.place[0] + 8)
        return self.remote(source, self.from_high, self.high_sem, plane, self.place[0] - 8)

    def add(self, slot, arrived):
        self.own[slot] = self.own[slot] + arrived[...]

    def start(self):
        me, core, z, a, b, step_a, step_b, near_a, near_b, twin = self.place
        greet(me, z, near_a, near_b, twin)
        for slot in (0, 1, 2, 3, 6, 7, 4, 5, 8, 9, 10, 11):
            self.gift(slot).start()
            self.load(slot).start()

    def far(self, turn):
        for slot in (2 * turn, 2 * turn + 1):
            self.load(slot).wait()
            self.gift(slot).wait_recv()
            self.add(slot, self.from_twin.at[slot])
            self.over_b(slot).start()

    def near(self, turn):
        for slot in (6 + 2 * turn, 7 + 2 * turn):
            self.load(slot).wait()
            self.gift(slot).wait_recv()
            self.add(slot, self.from_twin.at[slot])

    def stage_b(self, turn):
        for slot in (2 * turn, 2 * turn + 1):
            self.over_b(slot).wait_recv()
            self.add(6 + slot, self.from_b.at[slot])
        self.over_a(turn).start()

    def stage_a(self, turn):
        z = self.place[2]
        slot = 7 + 2 * turn
        self.over_a(turn).wait_recv()
        self.add(slot, self.from_a.at[turn])

        @pl.when(z == 0)
        def _():
            self.along(turn, True).start()

        if turn < 2:

            @pl.when(z == PLANES - 1)
            def _():
                self.along(turn, False).start()

    def stage_z(self, turn):
        z = self.place[2]
        slot = 7 + 2 * turn
        plane = self.plane_of(turn)
        if turn < 2:
            inner = jnp.logical_and(z > 0, z < PLANES - 1)

            @pl.when(jnp.logical_and(inner, plane > z))
            def _():
                self.along(turn, True).wait_recv()
                self.add(slot, self.from_low.at[plane])
                self.along(turn, True).start()

            @pl.when(jnp.logical_and(inner, plane < z))
            def _():
                self.along(turn, False).wait_recv()
                self.add(slot, self.from_high.at[plane])
                self.along(turn, False).start()

            return

        @pl.when(z > 0)
        def _():
            self.along(turn, True).wait_recv()
            self.out_ref[...] = self.own[slot].astype(F32) + self.from_low[plane].astype(F32)

        @pl.when(jnp.logical_and(z > 0, z < PLANES - 1))
        def _():
            self.along(turn, False).wait_recv()
            self.out_ref[...] += self.from_high[plane].astype(F32)

    def end(self):
        z = self.place[2]
        for slot in range(12):
            self.gift(slot).wait_send()
        for slot in range(6):
            self.over_b(slot).wait_send()
        for turn in range(self.TURNS):
            self.over_a(turn).wait_send()
            plane = self.plane_of(turn)

            @pl.when(plane > z)
            def _(turn=turn):
                self.along(turn, True).wait_send()

            @pl.when(plane < z)
            def _(turn=turn):
                self.along(turn, False).wait_send()

    def schedule(self):
        return {
            0: [self.start],
            2: [lambda: self.far(0)],
            3: [lambda: self.near(0)],
            6: [lambda: self.far(1)],
            7: [lambda: self.near(1)],
            8: [lambda: self.stage_b(0)],
            9: [lambda: self.far(2)],
            10: [lambda: self.near(2)],
            14: [lambda: self.stage_b(1), lambda: self.stage_a(0)],
            18: [lambda: self.stage_b(2)],
            19: [lambda: self.stage_a(1)],
            20: [lambda: self.stage_z(0)],
            22: [lambda: self.stage_a(2)],
            24: [lambda: self.stage_z(1)],
            27: [lambda: self.stage_z(2), self.end],
        }


PIECES = 4
CHUNKS = 3


def broadcast_kernel(
    split,
    table_ref,
    block_ref,
    out_ref,
    w_ref,
    stage,
    own_sem,
    load_sem,
    send_sem,
    recv_sem,
    w_send,
    w_recv,
):
    first_owner, first_row, count = split
    me, core, z, a, b, step_a, step_b, near_a, near_b, twin = neighbours()
    greet(me, z, near_a, near_b, twin)
    rows = LENGTH // PIECES
    height = block_ref.shape[0] // CHUNKS
    root = first_owner + 1
    gift = pltpu.make_async_remote_copy(
        src_ref=table_ref.at[pl.ds(first_row, count)],
        dst_ref=stage.at[pl.ds(0, count)],
        send_sem=load_sem.at[0],
        recv_sem=load_sem.at[1],
        device_id=(root,),
        device_id_type=MESH,
    )
    mine = pltpu.make_async_copy(
        table_ref.at[pl.ds(0, LENGTH - count)],
        stage.at[pl.ds(count, LENGTH - count)],
        load_sem.at[2],
    )
    shard = lax.rem(me, 8)
    own = pltpu.make_async_copy(block_ref, w_ref.at[shard], own_sem)

    @pl.when(me == first_owner)
    def _():
        gift.start()

    @pl.when(me == root)
    def _():
        mine.start()

    @pl.when(z == 0)
    def _():
        own.start()

    def copy(piece, device, kind):
        part = pl.ds(piece * rows, rows)
        return pltpu.make_async_remote_copy(
            src_ref=out_ref.at[part],
            dst_ref=out_ref.at[part],
            send_sem=send_sem.at[kind, piece],
            recv_sem=recv_sem.at[piece],
            device_id=(device,),
            device_id_type=MESH,
        )

    def block(place, chunk, device, kind, source=None):
        part = pl.ds(chunk * height, height)
        return pltpu.make_async_remote_copy(
            src_ref=w_ref.at[place, part] if source is None else source.at[part],
            dst_ref=w_ref.at[place, part],
            send_sem=w_send.at[kind, place, chunk],
            recv_sem=w_recv.at[place, chunk],
            device_id=(device,),
            device_id_type=MESH,
        )

    trunk = jnp.logical_and(core == 1, jnp.logical_and(a == 1, b == 1))
    branch = jnp.logical_and(core == 1, jnp.logical_and(a == 0, b == 1))
    routes = (
        (jnp.logical_and(trunk, z > 0), me - 8),
        (trunk, near_a),
        (jnp.logical_or(trunk, branch), near_b),
        (core == 1, twin),
    )
    shard_a = (1 - a) * step_a + b * step_b + core
    shards_b = [
        a * step_a + (1 - b) * step_b + core,
        (1 - a) * step_a + (1 - b) * step_b + core,
    ]

    def sends(chunk, source):
        pl.when(z < PLANES - 1)(lambda: block(shard, chunk, me + 8, 0, source).start())
        block(shard, chunk, near_a, 2, source).start()
        block(shard, chunk, near_b, 1, source).start()
        block(shard, chunk, twin, 3, source).start()

    def from_own(chunk):
        @pl.when(z > 0)
        def _():
            block(shard, chunk, twin, 3).wait_recv()
            sends(chunk, None)

    def from_a(chunk):
        block(shard_a, chunk, twin, 3).wait_recv()
        block(shard_a, chunk, near_b, 1).start()
        block(shard_a, chunk, twin, 3).start()

    def from_b(chunk):
        for place in shards_b:
            block(place, chunk, twin, 3).wait_recv()
            block(place, chunk, twin, 3).start()

    def pass_on(piece):
        for kind, (goes, device) in enumerate(routes):
            pl.when(goes)(lambda kind=kind, device=device: copy(piece, device, kind).start())

    def positions(condition, piece):
        @pl.when(jnp.logical_and(condition, me != root))
        def _():
            copy(piece, twin, 3).wait_recv()
            pass_on(piece)

    @pl.when(z == 0)
    def _():
        for chunk in range(CHUNKS):
            sends(chunk, block_ref)

    @pl.when(me == root)
    def _():
        mine.wait()
        gift.wait_recv()
        for piece in range(PIECES):
            part = slice(piece * rows, (piece + 1) * rows)
            out_ref[part, :] = stage[part, :].astype(BF)
            pass_on(piece)

    from_own(0)
    positions(trunk, 0)
    from_own(1)
    positions(trunk, 1)
    from_own(2)
    positions(trunk, 2)
    positions(trunk, 3)
    others = jnp.logical_not(trunk)
    from_a(0)
    from_a(1)
    positions(others, 0)
    from_a(2)
    from_b(0)
    positions(others, 1)
    from_b(1)
    positions(others, 2)
    from_b(2)
    positions(others, 3)

    def from_twin(place, carry):
        for chunk in range(CHUNKS):
            block(place * 2 + 1 - core, chunk, twin, 3).wait_recv()
        return carry

    lax.fori_loop(0, 4, from_twin, 0)
    for piece in range(PIECES):
        for kind, (goes, device) in enumerate(routes):
            pl.when(goes)(
                lambda piece=piece, kind=kind, device=device: copy(
                    piece, device, kind
                ).wait_send()
            )
    for chunk in range(CHUNKS):

        @pl.when(z < PLANES - 1)
        def _(chunk=chunk):
            block(shard, chunk, me + 8, 0).wait_send()

        block(shard, chunk, near_b, 1).wait_send()
        block(shard, chunk, near_a, 2).wait_send()
        block(shard, chunk, twin, 3).wait_send()
        block(shard_a, chunk, near_b, 1).wait_send()
        block(shard_a, chunk, twin, 3).wait_send()
        for place in shards_b:
            block(place, chunk, twin, 3).wait_send()

    @pl.when(me == first_owner)
    def _():
        gift.wait_send()

    @pl.when(z == 0)
    def _():
        own.wait()


def place_split(devices, owned):
    first_owner = VOCAB // owned
    first_row = VOCAB - first_owner * owned
    return first_owner, first_row, owned - first_row


def broadcast(table, block, split, ident):
    return pl.pallas_call(
        functools.partial(broadcast_kernel, split),
        in_specs=[pl.BlockSpec(memory_space=pl.ANY)] * 2,
        out_specs=[
            pl.BlockSpec(memory_space=pltpu.VMEM),
            pl.BlockSpec(memory_space=pl.ANY),
        ],
        out_shape=[
            jax.ShapeDtypeStruct((LENGTH, D), BF),
            jax.ShapeDtypeStruct((8,) + block.shape, BF),
        ],
        scratch_shapes=[
            pltpu.VMEM((LENGTH, D), F32),
            pltpu.SemaphoreType.DMA,
            pltpu.SemaphoreType.DMA((3,)),
            pltpu.SemaphoreType.DMA((4, PIECES)),
            pltpu.SemaphoreType.DMA((PIECES,)),
            pltpu.SemaphoreType.DMA((4, 8, CHUNKS)),
            pltpu.SemaphoreType.DMA((8, CHUNKS)),
        ],
        compiler_params=pltpu.CompilerParams(collective_id=ident, has_side_effects=True),
        cost_estimate=pl.CostEstimate(flops=0, bytes_accessed=100_000_000, transcendentals=0),
        name="broadcast",
    )(table, block)


def homecoming_kernel(
    split,
    place_ref,
    first_ref,
    vec_ref,
    out_ref,
    mats_ref,
    vec_sum_ref,
    sums,
    from_twin,
    from_b,
    from_a,
    from_z,
    ready,
    own,
    own_twin,
    own_b,
    own_a,
    own_high,
    sems,
    z_sem,
    piece_sem,
    home_sem,
    load_sem,
    twin_sem,
    b_sem,
    a_sem,
    high_sem,
    vec_in,
    vec_sem,
):
    first_owner, first_row, count = split
    root = first_owner + 1
    me, core, z, a, b, step_a, step_b, near_a, near_b, twin = neighbours()
    rows = place_ref.shape[4]
    height = first_ref.shape[1] // CHUNKS
    out_ref[...] = jnp.zeros_like(out_ref)
    barrier = pltpu.get_barrier_semaphore()

    def each(step, carry):
        pl.semaphore_signal(
            barrier, inc=1, device_id=(lax.rem(me + step, 32),), device_id_type=MESH
        )
        return carry

    lax.fori_loop(1, 32, each, 0)
    pl.semaphore_wait(barrier, 31)

    def remote(source, target, send, receive, device):
        return pltpu.make_async_remote_copy(
            src_ref=source,
            dst_ref=target,
            send_sem=send,
            recv_sem=receive,
            device_id=(device,),
            device_id_type=MESH,
        )

    def add(total, extra):
        return (total.astype(F32) + extra.astype(F32)).astype(BF)

    x = jnp.where(core == 0, b, a)
    y = jnp.where(core == 0, a, b)
    gift = remote(place_ref.at[:, :, :, 1 - core], from_twin, sems.at[0, 0], sems.at[0, 1], twin)
    gift.start()
    loads, gifts = [], []
    for slot in range(4):
        other_b, other_a = slot < 2, slot % 2 == 0
        a_at, b_at = (1 - a if other_a else a), (1 - b if other_b else b)
        shard = a_at * step_a + b_at * step_b + core
        loads.append(pltpu.make_async_copy(first_ref.at[shard], own.at[slot], load_sem.at[slot]))
        a_at, b_at = (1 - b if other_a else b), (1 - a if other_b else a)
        shard = a_at * step_b + b_at * step_a + 1 - core
        gifts.append(
            remote(
                first_ref.at[shard],
                own_twin.at[slot],
                twin_sem.at[0, slot],
                twin_sem.at[1, slot],
                twin,
            )
        )
    for slot in range(4):
        gifts[slot].start()
        loads[slot].start()

    def vec_copy(source, target, device):
        return remote(
            vec_ref.at[source],
            vec_in.at[target],
            vec_sem.at[0, source],
            vec_sem.at[1, target],
            device,
        )

    def vec_start(step, carry):
        device = lax.rem(me + step, 32)
        vec_copy(device, me, device).start()
        return carry

    def vec_wait(step, carry):
        device = lax.rem(me + step, 32)
        vec_copy(device, device, device).wait_recv()
        vec_copy(device, device, device).wait_send()
        return carry

    lax.fori_loop(1, 32, vec_start, 0)
    vec_in[me] = vec_ref[me]
    gift.wait_recv()
    sums[...] = add(place_ref[:, :, :, core], from_twin[...])

    @pl.when(core == 0)
    def _():
        remote(sums.at[:, :, 1 - x], from_b, sems.at[1, 0], sems.at[1, 1], near_b).start()

    @pl.when(core == 1)
    def _():
        remote(sums.at[:, 1 - y], from_b, sems.at[1, 0], sems.at[1, 1], near_b).start()

    over_b = [
        remote(own.at[slot], own_b.at[slot], b_sem.at[0, slot], b_sem.at[1, slot], near_b)
        for slot in range(2)
    ]
    for slot in range(4):
        loads[slot].wait()
        gifts[slot].wait_recv()
        own[slot] = add(own[slot], own_twin[slot])
        if slot < 2:
            over_b[slot].start()

    small_b = remote(sums.at[:, 0], from_b, sems.at[1, 0], sems.at[1, 1], near_b)
    small_b.wait_recv()

    @pl.when(core == 0)
    def _():
        from_b[...] = add(sums[:, :, x], from_b[...])

    @pl.when(core == 1)
    def _():
        from_b[...] = add(sums[:, y], from_b[...])

    small_a = remote(from_b.at[:, 1 - a], from_a, sems.at[2, 0], sems.at[2, 1], near_a)
    small_a.start()
    over_a = remote(own.at[2], own_a, a_sem.at[0], a_sem.at[1], near_a)
    for slot in range(2):
        over_b[slot].wait_recv()
        own[2 + slot] = add(own[2 + slot], own_b[slot])
        if slot == 0:
            over_a.start()
    small_a.wait_recv()
    from_a[...] = add(from_b[:, a], from_a[...])

    def column(plane, action):
        @pl.when(plane != z)
        def _():
            action(
                remote(
                    from_a.at[plane],
                    from_z.at[z],
                    z_sem.at[0, plane],
                    z_sem.at[1, z],
                    me + 8 * (plane - z),
                )
            )

    for plane in range(PLANES):
        column(plane, lambda item: item.start())
    over_a.wait_recv()

    def down(chunk):
        part = pl.ds(chunk * height, height)
        return remote(
            own.at[3, part],
            own_high.at[part],
            high_sem.at[0, chunk],
            high_sem.at[1, chunk],
            me - 8,
        )

    for chunk in range(CHUNKS):
        part = pl.ds(chunk * height, height)
        own[3, part] = add(own[3, part], own_a[part])

        @pl.when(z < PLANES - 1)
        def _(chunk=chunk, part=part):
            down(chunk).wait_recv()
            own[3, part] = add(own[3, part], own_high[part])

        @pl.when(z > 0)
        def _(chunk=chunk):
            down(chunk).start()

    mats_ref[...] = own[3].astype(F32)
    ready[...] = from_a[z].astype(F32)
    for plane in range(PLANES):

        @pl.when(plane != z)
        def _(plane=plane):
            remote(
                from_a.at[plane], from_z.at[plane], z_sem.at[0, plane], z_sem.at[1, plane], twin
            ).wait_recv()
            ready[...] += from_z[plane].astype(F32)

    def home(device, half):
        place = device * rows + half * 8
        early = place < count
        owner = jnp.where(early, first_owner, root)
        spot = pl.multiple_of(jnp.where(early, first_row + place, place - count), 8)
        return owner, spot

    def piece(device, half):
        owner, spot = home(device, half)
        return remote(
            ready.at[pl.ds(half * 8, 8)],
            out_ref.at[pl.ds(spot, 8)],
            piece_sem.at[half],
            home_sem.at[device * 2 + half],
            owner,
        )

    for half in range(2):
        owner, spot = home(me, half)

        @pl.when(owner == me)
        def _(half=half, spot=spot):
            out_ref[pl.ds(spot, 8), :] = ready[half * 8 : half * 8 + 8, :]

        @pl.when(owner != me)
        def _(half=half):
            piece(me, half).start()

    def arrive(index, carry):
        device, half = index // 2, lax.rem(index, 2)
        owner, _ = home(device, half)

        @pl.when(jnp.logical_and(owner == me, device != me))
        def _():
            piece(device, half).wait_recv()

        return carry

    @pl.when(me >= first_owner)
    def _():
        lax.fori_loop(0, 64, arrive, 0)

    for half in range(2):
        owner, _ = home(me, half)

        @pl.when(owner != me)
        def _(half=half):
            piece(me, half).wait_send()

    lax.fori_loop(1, 32, vec_wait, 0)
    vec_sum_ref[...] = jnp.sum(vec_in[...], axis=0)
    for item in [gift, small_b, small_a, over_a] + gifts + over_b:
        item.wait_send()
    for plane in range(PLANES):
        column(plane, lambda item: item.wait_send())
    for chunk in range(CHUNKS):

        @pl.when(z > 0)
        def _(chunk=chunk):
            down(chunk).wait_send()


def homecoming(place_sums, first, vecs, owned, split, ident):
    rows = LENGTH // 32
    small = (rows, D)
    shape = first.shape[1:]
    return pl.pallas_call(
        functools.partial(homecoming_kernel, split),
        in_specs=[
            pl.BlockSpec(memory_space=pltpu.VMEM),
            pl.BlockSpec(memory_space=pl.ANY),
            pl.BlockSpec(memory_space=pltpu.VMEM),
        ],
        out_specs=[pl.BlockSpec(memory_space=pltpu.VMEM)] * 3,
        out_shape=[
            jax.ShapeDtypeStruct((owned, D), F32),
            jax.ShapeDtypeStruct(shape, F32),
            jax.ShapeDtypeStruct(vecs.shape[1:], F32),
        ],
        scratch_shapes=[
            pltpu.VMEM((4, 2, 2) + small, BF),
            pltpu.VMEM((4, 2, 2) + small, BF),
            pltpu.VMEM((4, 2) + small, BF),
            pltpu.VMEM((4,) + small, BF),
            pltpu.VMEM((4,) + small, BF),
            pltpu.VMEM(small, F32),
            pltpu.VMEM((4,) + shape, BF),
            pltpu.VMEM((4,) + shape, BF),
            pltpu.VMEM((2,) + shape, BF),
            pltpu.VMEM(shape, BF),
            pltpu.VMEM(shape, BF),
            pltpu.SemaphoreType.DMA((3, 2)),
            pltpu.SemaphoreType.DMA((2, 4)),
            pltpu.SemaphoreType.DMA((2,)),
            pltpu.SemaphoreType.DMA((64,)),
            pltpu.SemaphoreType.DMA((4,)),
            pltpu.SemaphoreType.DMA((2, 4)),
            pltpu.SemaphoreType.DMA((2, 2)),
            pltpu.SemaphoreType.DMA((2,)),
            pltpu.SemaphoreType.DMA((2, CHUNKS)),
            pltpu.VMEM(vecs.shape, F32),
            pltpu.SemaphoreType.DMA((2, 32)),
        ],
        compiler_params=pltpu.CompilerParams(
            collective_id=ident, has_side_effects=True, vmem_limit_bytes=40 * MB
        ),
        cost_estimate=pl.CostEstimate(
            flops=0, bytes_accessed=200_000_000, transcendentals=0
        ),
        name="homecoming",
    )(place_sums.reshape((4, 2, 2, 2) + small), first, vecs)


def forward_kernel(
    by_kernel,
    key_ref,
    found_ref,
    extra_ref,
    place_ref,
    w_ref,
    bias_ref,
    block_ref,
    x_ref,
    xb_ref,
    proj_ref,
    att_ref,
    lse_ref,
    *scratch,
):
    seq, head = pl.program_id(0), pl.program_id(1)
    pairs = HEADS // 2
    step = seq * (pairs + 1) + head
    if by_kernel:
        gather = RestSpread(block_ref, scratch[0], scratch[1:])
        for when, actions in gather.schedule().items():

            @pl.when(step == when)
            def _(actions=actions):
                for action in actions:
                    action()

    @pl.when(head == 0)
    def _():
        slots = lax.broadcasted_iota(jnp.int32, (LENGTH, found_ref.shape[0]), 1)
        picked = (key_ref[...] == slots).astype(BF)
        inputs = dot_nn(picked, found_ref[...]) + extra_ref[...].astype(F32)
        inputs = inputs + place_ref[...].astype(F32)
        x_ref[...] = inputs
        inputs_b = inputs.astype(BF)
        xb_ref[...] = inputs_b
        for start in range(0, QKV, D):
            cols = slice(start, start + D)
            part = dot_nt(inputs_b, w_ref[cols, :]) + bias_ref[:, cols]
            proj_ref[:, cols] = part.astype(BF)

    @pl.when(head > 0)
    def _():
        width = 2 * HEAD_DIM
        start = (head - 1) * width
        query = proj_ref[:, pl.ds(pl.multiple_of(start, width), width)]
        keys = proj_ref[:, pl.ds(pl.multiple_of(D + start, width), width)]
        values_t = proj_ref[:, pl.ds(pl.multiple_of(2 * D + start, width), width)].T
        lane = lax.broadcasted_iota(jnp.int32, query.shape, 1)
        outs = []
        for half in range(2):
            mine = (lane < HEAD_DIM) if half == 0 else (lane >= HEAD_DIM)
            picked = jnp.where(mine, query, jnp.zeros_like(query))
            scores = dot_nt(keys, picked)
            highest = jnp.max(scores, 0, keepdims=True)
            expo = jnp.exp2((scores - highest) * (SCORE * LOG2E))
            total = jnp.sum(expo, 0, keepdims=True)
            part = values_t[half * HEAD_DIM : (half + 1) * HEAD_DIM, :]
            outs.append(dot_nn(part, expo.astype(BF)) / total)
            lse_ref[0, half : half + 1, :] = highest * (SCORE * LOG2E) + jnp.log2(total)
        att_ref[...] = jnp.concatenate(outs, 0).T.astype(BF)


def forward(by_kernel, key, found, extra, places, w_qkv, bias, block, ident):
    rows = key.shape[0]
    seqs = rows // LENGTH
    pairs = HEADS // 2
    slots = found.shape[0]

    def row(width):
        return pl.BlockSpec((LENGTH, width), lambda s, h: (s, 0))

    def steady(shape):
        return pl.BlockSpec(
            shape, lambda s, h: (0, 0), pipeline_mode=pl.Buffered(buffer_count=1)
        )

    out_specs = [
        row(D),
        row(D),
        row(QKV),
        pl.BlockSpec((LENGTH, 2 * HEAD_DIM), lambda s, h: (s, jnp.maximum(h - 1, 0))),
        pl.BlockSpec(
            (1, 2, LENGTH), lambda s, h: (s * pairs + jnp.maximum(h - 1, 0), 0, 0)
        ),
    ]
    out_shape = [
        jax.ShapeDtypeStruct((rows, D), F32),
        jax.ShapeDtypeStruct((rows, D), BF),
        jax.ShapeDtypeStruct((rows, QKV), BF),
        jax.ShapeDtypeStruct((rows, D), BF),
        jax.ShapeDtypeStruct((seqs * pairs, 2, LENGTH), F32),
    ]
    params = {}
    scratch = []
    if by_kernel:
        out_specs.append(pl.BlockSpec(memory_space=pl.ANY))
        out_shape.append(jax.ShapeDtypeStruct((24,) + block.shape, BF))
        params = dict(collective_id=ident, has_side_effects=True)
        scratch = RestSpread.scratch()
    return pl.pallas_call(
        functools.partial(forward_kernel, by_kernel),
        grid=(seqs, pairs + 1),
        in_specs=[
            row(1),
            steady((slots, D)),
            row(D),
            steady((LENGTH, D)),
            steady((QKV, D)),
            steady((1, QKV)),
            pl.BlockSpec(memory_space=pl.ANY),
        ],
        out_specs=out_specs,
        out_shape=out_shape,
        scratch_shapes=scratch,
        compiler_params=pltpu.CompilerParams(vmem_limit_bytes=56 * MB, **params),
        cost_estimate=pl.CostEstimate(
            flops=40_000_000_000, bytes_accessed=60_000_000, transcendentals=0
        ),
        name="forward",
    )(key, found, extra, places, w_qkv, bias, block)


def backward_kernel(
    by_kernel,
    q_ref,
    k_ref,
    v_ref,
    att_ref,
    g_ref,
    lse_ref,
    first_ref,
    xb_ref,
    key_ref,
    sums_ref,
    w_ref,
    rest_ref,
    grad_ref,
    place_ref,
    weights_ref,
    sent_ref,
    bias_ref,
    mats_ref,
    proj,
    total,
    places,
    sent,
    *scratch,
):
    seq, head = pl.program_id(0), pl.program_id(1)
    pairs = HEADS // 2
    step = seq * (pairs + 1) + head

    @pl.when(step == 0)
    def _():
        total[...] = jnp.zeros_like(total)
        places[...] = jnp.zeros_like(places)
        sent[...] = jnp.zeros_like(sent)
        bias_ref[...] = sums_ref[...]
        mats_ref[...] = jnp.zeros_like(mats_ref)

    if by_kernel:
        sums = RestSums(rest_ref, mats_ref, scratch)
        for when, actions in sums.schedule().items():

            @pl.when(step == when)
            def _(actions=actions):
                for action in actions:
                    action()

    @pl.when(head < pairs)
    def _():
        cols = pl.ds(pl.multiple_of(head * 2 * HEAD_DIM, 2 * HEAD_DIM), 2 * HEAD_DIM)
        query = q_ref[...]
        keys = k_ref[...]
        values = v_ref[...]
        grad = g_ref[...]
        lane = lax.broadcasted_iota(jnp.int32, query.shape, 1)
        first = lane < HEAD_DIM
        product = (att_ref[...].astype(F32) * grad.astype(F32)).T
        zero = jnp.zeros_like(query)
        g_q, g_k, g_v = [], [], []
        for half in range(2):
            mine = first if half == 0 else jnp.logical_not(first)
            scores = dot_nt(keys, jnp.where(mine, query, zero))
            probs = jnp.exp2(scores * (SCORE * LOG2E) - lse_ref[0, half : half + 1, :])
            delta = jnp.sum(
                product[half * HEAD_DIM : (half + 1) * HEAD_DIM, :], 0, keepdims=True
            )
            g_probs = dot_nt(values, jnp.where(mine, grad, zero))
            g_v.append(dot_nn(probs.astype(BF), grad))
            g_scores = (probs * (g_probs - delta)).astype(BF)
            g_k.append(dot_nn(g_scores, query))
            g_q.append(dot_tn(g_scores, keys))
        grad_q = jnp.where(first, g_q[0], g_q[1]) * SCORE
        grad_k = jnp.where(first, g_k[0], g_k[1]) * SCORE
        grad_v = jnp.where(first, g_v[0], g_v[1])
        proj[0, :, cols] = grad_q.astype(BF)
        proj[1, :, cols] = grad_k.astype(BF)
        proj[2, :, cols] = grad_v.astype(BF)
        bias_ref[0:1, cols] += jnp.sum(grad_q, 0, keepdims=True)
        bias_ref[1:2, cols] += jnp.sum(grad_v, 0, keepdims=True)

    @pl.when(head == pairs)
    def _():
        g_in = first_ref[...]
        inputs_b = xb_ref[...]
        for part in range(3):
            cols = slice(part * D, (part + 1) * D)
            g_in = g_in + dot_nn(proj[part], w_ref[cols, :])
            total[cols, :] += dot_tn(proj[part], inputs_b)
        g_in_b = g_in.astype(BF)
        grad_ref[...] = g_in_b
        places[...] += g_in
        slots = lax.broadcasted_iota(jnp.int32, (LENGTH, sent.shape[0]), 1)
        sent[...] += dot_tn((key_ref[...] == slots).astype(BF), g_in_b)

    @pl.when(step == pl.num_programs(0) * (pairs + 1) - 1)
    def _():
        sent_ref[...] = sent[...].astype(BF)
        weights_ref[...] = total[...].astype(BF)
        place_ref[...] = places[...].astype(BF)


def backward(
    by_kernel, projected, attended, grad_att, lse, g_first, inputs_b, key, sums, room, w_qkv, rest, ident
):
    rows = projected.shape[0]
    seqs = rows // LENGTH
    pairs = HEADS // 2
    block = (LENGTH, 2 * HEAD_DIM)
    shape = rest.shape[1:]

    def pair(offset):
        return pl.BlockSpec(block, lambda s, h: (s, offset + jnp.minimum(h, pairs - 1)))

    def row(width):
        return pl.BlockSpec((LENGTH, width), lambda s, h: (s, 0))

    def steady(shape):
        return pl.BlockSpec(
            shape, lambda s, h: (0, 0), pipeline_mode=pl.Buffered(buffer_count=1)
        )

    def kept(shape):
        return pl.BlockSpec(shape, lambda s, h: (0, 0))

    return pl.pallas_call(
        functools.partial(backward_kernel, by_kernel),
        grid=(seqs, pairs + 1),
        in_specs=[
            pair(0),
            pair(pairs),
            pair(2 * pairs),
            pair(0),
            pair(0),
            pl.BlockSpec(
                (1, 2, LENGTH), lambda s, h: (s * pairs + jnp.minimum(h, pairs - 1), 0, 0)
            ),
            row(D),
            row(D),
            row(1),
            steady((16, D)),
            steady((QKV, D)),
            pl.BlockSpec(memory_space=pl.ANY),
        ],
        out_specs=[
            row(D),
            kept((LENGTH, D)),
            kept((QKV, D)),
            kept((room, D)),
            kept((16, D)),
            kept(shape),
        ],
        out_shape=[
            jax.ShapeDtypeStruct((rows, D), BF),
            jax.ShapeDtypeStruct((LENGTH, D), BF),
            jax.ShapeDtypeStruct((QKV, D), BF),
            jax.ShapeDtypeStruct((room, D), BF),
            jax.ShapeDtypeStruct((16, D), F32),
            jax.ShapeDtypeStruct(shape, F32),
        ],
        scratch_shapes=[
            pltpu.VMEM((3, LENGTH, D), BF),
            pltpu.VMEM((QKV, D), F32),
            pltpu.VMEM((LENGTH, D), F32),
            pltpu.VMEM((room, D), F32),
        ]
        + (RestSums.scratch(shape) if by_kernel else []),
        compiler_params=pltpu.CompilerParams(
            vmem_limit_bytes=60 * MB,
            **(dict(collective_id=ident, has_side_effects=True) if by_kernel else {}),
        ),
        cost_estimate=pl.CostEstimate(
            flops=60_000_000_000, bytes_accessed=60_000_000, transcendentals=0
        ),
        name="backward",
    )(
        projected,
        projected,
        projected,
        attended,
        grad_att,
        lse,
        g_first,
        inputs_b,
        key,
        sums,
        w_qkv,
        rest,
    )


def slots_of(ids, owned):
    count = ids.shape[0]
    order = jnp.arange(count, dtype=jnp.int32)
    repeated = jnp.any(
        (ids[:, None] == ids[None, :]) & (order[:, None] < order[None, :]), axis=0
    )
    first = jnp.logical_not(repeated)
    base = (ids // owned) * owned
    below = (
        first[:, None]
        & (ids[:, None] >= base[None, :])
        & (ids[:, None] < ids[None, :])
    )
    return jnp.sum(below.astype(jnp.int32), axis=0)


def requests_of(ids, owner, slot, owned, devices, start, room):
    key = jnp.where((slot >= start) & (slot < start + room), owner * room + slot - start, -1)
    spots = jnp.arange(devices * room, dtype=jnp.int32)
    asked = jnp.max(
        jnp.where(key[:, None] == spots[None, :], (ids - owner * owned)[:, None], -1), axis=0
    )
    return key, asked


def pick(index, amount):
    return (index[:, None] == jnp.arange(amount, dtype=jnp.int32)[None, :]).astype(BF)


def adam_direction(param, first, second, grad, corr_one, corr_two, decay):
    first_next = beta_one * first + (1.0 - beta_one) * grad
    second_next = beta_two * second + (1.0 - beta_two) * grad * grad
    update = first_next / corr_one / (jnp.sqrt(second_next / corr_two) + adam_eps)
    return (update + decay * param, first_next)


def body(
    devices,
    token_ids,
    masked,
    swap_kind,
    swap_ids,
    out_grad,
    embed_table,
    table_first,
    table_second,
    layer_mats,
    mats_first,
    mats_second,
    layer_vecs,
    vecs_first,
    vecs_second,
):
    axis = "fsdp"
    rows = token_ids.shape[0]
    owned = embed_table.shape[0]
    entries = layer_vecs.shape[0]
    columns = layer_mats.shape[1]
    me = lax.axis_index(axis)
    by_kernel = devices == 32
    split = place_split(devices, owned)
    replaced = jnp.where(swap_kind < 8, mask_token, jnp.where(swap_kind == 8, swap_ids, token_ids))
    chosen = jnp.where(masked == 1, replaced, token_ids)

    def swap(blocks):
        return lax.all_to_all(blocks, axis, 0, 0, tiled=True)

    block = layer_mats.astype(BF).T

    room = 16 * -(-1536 // (16 * devices))
    more = 16
    owner = chosen // owned
    slot = slots_of(chosen, owned)
    most = jnp.max(slot) + 1
    key, asked = requests_of(chosen, owner, slot, owned, devices, 0, room)
    _, asked_more = requests_of(chosen, owner, slot, owned, devices, room, more)
    table_b = embed_table.astype(BF)
    own_vecs = layer_vecs.astype(BF).astype(F32)
    notes = jnp.concatenate(
        [
            asked.reshape(devices, room).astype(F32),
            asked_more.reshape(devices, more).astype(F32),
            jnp.broadcast_to(own_vecs[None], (devices, entries)),
            jnp.broadcast_to(most.astype(F32), (devices, 1)),
        ],
        axis=1,
    )
    notes = swap(notes)
    wanted = notes[:, :room].astype(jnp.int32).reshape(-1)
    wanted_more = notes[:, room : room + more].astype(jnp.int32).reshape(-1)
    vecs = notes[:, room + more : room + more + entries].reshape(-1)
    longest = jnp.max(notes[:, room + more + entries]).astype(jnp.int32)
    found = dot_nn(pick(wanted, owned), table_b).astype(BF)
    found, table, block = lax.optimization_barrier((found, embed_table, block))
    found = swap(found.reshape(devices, room, D)).reshape(-1, D)
    if by_kernel:
        places, w_qkv = broadcast(table, block, split, 1)
        w_qkv = w_qkv.reshape(QKV, D)
    else:
        spots = VOCAB + jnp.arange(LENGTH, dtype=jnp.int32) - me * owned
        places = lax.psum(dot_nn(pick(spots, owned), table_b), axis).astype(BF)
        mats_t = lax.all_gather(block, axis, axis=0, tiled=True)
        w_qkv, rest = mats_t[:QKV], mats_t[QKV:]
    rounds = (longest - room + more - 1) // more

    def further(turn):
        key, asked = requests_of(chosen, owner, slot, owned, devices, room + turn * more, more)
        wanted = lax.cond(
            turn == 0,
            lambda: wanted_more,
            lambda: swap(asked.reshape(devices, more)).reshape(-1),
        )
        return key, wanted

    def fetch_more(state):
        turn, extra = state
        key, wanted = further(turn)
        found = dot_nn(pick(wanted, owned), table_b).astype(BF)
        found = swap(found.reshape(devices, more, D)).reshape(-1, D)
        return turn + 1, extra + dot_nn(pick(key, devices * more), found).astype(BF)

    _, extra = lax.while_loop(
        lambda state: state[0] < rounds,
        fetch_more,
        (jnp.int32(0), jnp.zeros((rows, D), BF)),
    )

    bias_qkv = jnp.concatenate([vecs[:D], jnp.zeros((D,), F32), vecs[D : 2 * D]])[None]
    bias_up = vecs[5 * D : 5 * D + FF][None]
    small = jnp.concatenate(
        [vecs[2 * D : 5 * D], vecs[5 * D + FF :], jnp.zeros((2 * D,), F32)]
    ).reshape(8, D)

    results = forward(by_kernel, key[:, None], found, extra, places, w_qkv, bias_qkv, block, 4)
    inputs, inputs_b, projected, attended, lse = results[:5]
    if by_kernel:
        rest = results[5].reshape(-1, D)
    (
        outputs,
        normed_b,
        hidden_b,
        g_mid_b,
        g_up_b,
        g_first,
        g_first_b,
        g_att_b,
        sums,
    ) = middle(attended, inputs, out_grad, masked[:, None], rest, small, bias_up)
    g_rest = rest_gradients(g_first_b, attended, g_up_b, normed_b, hidden_b, g_mid_b)
    input_grad, g_places, g_qkv, sent, sums, rest_grad = backward(
        by_kernel,
        projected,
        attended,
        g_att_b,
        lse,
        g_first,
        inputs_b,
        key[:, None],
        sums,
        devices * room,
        w_qkv,
        g_rest.reshape(-1, columns, D),
        2,
    )

    g_vecs = sums[:12].reshape(devices, entries)
    sent, g_places, g_qkv = lax.optimization_barrier((sent, g_places, g_qkv))
    sent = swap(sent.reshape(devices, room, D)).reshape(-1, D)
    if by_kernel:
        padded = jnp.pad(g_vecs, ((0, 0), (0, 1024 - entries))).reshape(devices, 8, 128)
        g_own_places, first_grad, vecs_grad = homecoming(
            g_places, g_qkv.reshape(-1, columns, D), padded, owned, split, 3
        )
        vecs_grad = vecs_grad.reshape(1024)[:entries]
        mats_grad = jnp.where(me < QKV // columns, first_grad, rest_grad).T
    else:
        vecs_grad = jnp.sum(swap(g_vecs), axis=0)
        total = lax.psum(g_places.astype(F32), axis)
        spots = me * owned + jnp.arange(owned, dtype=jnp.int32) - VOCAB
        inside = (spots >= 0) & (spots < LENGTH)
        g_own_places = jnp.where(
            inside[:, None], total[jnp.clip(spots, 0, LENGTH - 1)], 0.0
        )
        mats_grad = lax.psum_scatter(
            jnp.concatenate([g_qkv, g_rest], axis=0), axis, scatter_dimension=0, tiled=True
        )
        mats_grad = mats_grad.astype(F32).T
    table_grad = dot_tn(pick(wanted, owned), sent) + g_own_places

    def send_more(state):
        turn, total = state
        key, wanted = further(turn)
        sent = dot_tn(pick(key, devices * more), input_grad).astype(BF)
        sent = swap(sent.reshape(devices, more, D)).reshape(-1, D)
        return turn + 1, total + dot_tn(pick(wanted, owned), sent)

    _, table_grad = lax.while_loop(
        lambda state: state[0] < rounds, send_more, (jnp.int32(0), table_grad)
    )

    counter = jnp.float32(STEP)
    corr_one = 1.0 - jnp.power(jnp.float32(beta_one), counter)
    corr_two = 1.0 - jnp.power(jnp.float32(beta_two), counter)
    table_step, table_first_next = adam_direction(
        embed_table, table_first, table_second, table_grad, corr_one, corr_two, decay_rate
    )
    mats_step, mats_first_next = adam_direction(
        layer_mats, mats_first, mats_second, mats_grad, corr_one, corr_two, decay_rate
    )
    vecs_step, vecs_first_next = adam_direction(
        layer_vecs, vecs_first, vecs_second, vecs_grad, corr_one, corr_two, 0.0
    )
    return (
        outputs,
        input_grad,
        table_grad,
        mats_grad,
        vecs_grad,
        table_step,
        table_first_next,
        mats_step,
        mats_first_next,
        vecs_step,
        vecs_first_next,
    )


def solution(mesh):
    line = P("fsdp")
    by_rows = P("fsdp", None)
    by_cols = P(None, "fsdp")
    return jax.shard_map(
        functools.partial(body, mesh.shape["fsdp"]),
        mesh=mesh,
        in_specs=(
            line,
            line,
            line,
            line,
            by_rows,
            by_rows,
            by_rows,
            by_rows,
            by_cols,
            by_cols,
            by_cols,
            line,
            line,
            line,
        ),
        out_specs=(
            by_rows,
            by_rows,
            by_rows,
            by_cols,
            line,
            by_rows,
            by_rows,
            by_cols,
            by_cols,
            line,
            line,
        ),
        check_vma=False,
    )
```
